32 devices in a mesh: seq: 8 (over z, y), tp: 4 (over x, core).
Axes of the slice: x: 2, y: 2, z: 4, core: 2. Of those that a mesh axis runs over, the one named last changes fastest.
Arguments:
- stream_in: bfloat16 [8192, 2048], P('seq'), may hold values from -6 to 6
- doc_lengths: int32 [4], replicated, may hold values from 64 to 7808, as said below
- first_gain: bfloat16 [2048], P('seq'), may hold values from 0.5 to 1.5
- w_query: bfloat16 [2048, 256], P('seq', 'tp'), may hold values from -0.125 to 0.125
- w_key: bfloat16 [2048, 256], P('seq', 'tp'), may hold values from -0.125 to 0.125
- w_value: bfloat16 [2048, 2048], P('seq', 'tp'), may hold values from -0.125 to 0.125
- w_out: bfloat16 [2048, 2048], P('tp', 'seq'), may hold values from -2 to 2
- second_gain: bfloat16 [2048], P('seq'), may hold values from 0.5 to 1.5
- w_gate: bfloat16 [2048, 5504], P('seq', 'tp'), may hold values from -0.125 to 0.125
- w_up: bfloat16 [2048, 5504], P('seq', 'tp'), may hold values from -0.125 to 0.125
- w_down: bfloat16 [5504, 2048], P('tp', 'seq'), may hold values from -0.078125 to 0.078125
- cotangent: bfloat16 [8192, 2048], P('seq'), may hold values from -6 to 6
Outputs:
- activations: bfloat16 [8192, 2048], P('seq')
- input_grad: float32 [8192, 2048], P('seq')
- grad_first: float32 [2048], P('seq')
- grad_query: float32 [2048, 256], P('seq', 'tp')
- grad_key: float32 [2048, 256], P('seq', 'tp')
- grad_value: float32 [2048, 2048], P('seq', 'tp')
- grad_out: float32 [2048, 2048], P('tp', 'seq')
- grad_second: float32 [2048], P('seq')
- grad_gate: float32 [2048, 5504], P('seq', 'tp')
- grad_up: float32 [2048, 5504], P('seq', 'tp')
- grad_down: float32 [5504, 2048], P('tp', 'seq')
The draws below stay inside these ranges and needn't reach their ends.
Inputs may be any that keep to these rules, and one draw needn't show every extreme that they name: `doc_lengths`: 4 row lengths in order, laid end to end over all 8192 tokens: one long row of 7808 tokens, placed anywhere among them, that starts within the first 1024 tokens and ends within the last 1024, and 3 short rows in any order, one of 64 tokens and two whose lengths, each of 64 to 256, sum to 320.
All inputs are finite; a program needn't handle non-finite values.
Results may differ from the reference program's by a relative error of at most 0.024.
Values may be sent and summed in bfloat16 or wider, within the bound.
A program may use at most 256 MiB of HBM per device.

```python
import math
import jax
import jax.numpy as jnp
from jax import lax

D = 2048
FF = 5504
H = 16
FEAT = 16
PHI = 273
NSHORT = 3
SHORT = 256
NDOCS = 4
TOKENS = 8192


def draw_doc_lengths(key, part):
    key = jax.random.fold_in(key, 7)
    key_order, key_spot, key_size = jax.random.split(key, 3)
    least = SHORT // 4
    free_len = jax.random.randint(key_size, (), least, SHORT + 1).astype(jnp.int32)
    other_len = (5 * SHORT // 4 - free_len).astype(jnp.int32)
    base_rows = jnp.stack([jnp.array(least, jnp.int32), free_len, other_len]).astype(jnp.int32)
    order = jax.random.permutation(key_order, NSHORT).astype(jnp.int32)
    short_rows = base_rows[order].astype(jnp.int32)
    long_place = jax.random.randint(key_spot, (), 0, NSHORT + 1).astype(jnp.int32)
    longest = (TOKENS - jnp.sum(short_rows)).astype(jnp.int32)
    slot_index = jnp.arange(NDOCS, dtype=jnp.int32)
    early_part = short_rows[jnp.clip(slot_index, 0, NSHORT - 1)]
    later_part = short_rows[jnp.clip(slot_index - 1, 0, NSHORT - 1)]
    return jnp.where(slot_index < long_place, early_part, jnp.where(slot_index == long_place, longest, later_part)).astype(jnp.int32)


def raised(entries, own_key, source, target, blocks, factor):
    def block_of(position):
        return (jnp.arange(entries.shape[position]) // (entries.shape[position] // blocks)).reshape((-1,) + (1,) * (entries.ndim - 1 - position))

    one_side = jax.random.permutation(own_key, blocks)[block_of(target)]
    far = (block_of(target) + blocks // 2) % blocks
    return jnp.where((block_of(source) == one_side) | (block_of(source) == far), factor * entries, entries)


def levels(stream_key, extent, cuts, smallest, largest):
    def one(dim, parts):
        heights = jax.random.uniform(jax.random.fold_in(jax.random.fold_in(stream_key, 6), dim), (parts,), jnp.float32, smallest / len(cuts), largest / len(cuts))
        return jnp.repeat(jnp.exp(heights), extent[dim] // parts).reshape((-1,) + (1,) * (len(extent) - dim - 1))

    loudness = one(*cuts[0])
    for cut in cuts[1:]:
        loudness = loudness * one(*cut)
    return loudness


def gaussian(own_key, dims, deviation, bound, cuts=(), kind=jnp.bfloat16):
    values = deviation * jax.random.normal(own_key, dims, jnp.float32)
    if cuts:
        values = values * levels(own_key, dims, cuts, -0.22, 0.18)
    return jnp.clip(values, -bound, bound).astype(kind)


def heavy_noise(key, extent, scale, limit, cuts, heavy, held_as=jnp.bfloat16):
    entries = scale * jax.random.normal(key, extent, jnp.float32)
    if cuts:
        entries = entries * levels(key, extent, cuts, -0.22, 0.18)
    return jnp.clip(raised(entries, jax.random.fold_in(key, 3), *heavy), -limit, limit).astype(held_as)


def setup_inputs(seed: int = 0) -> dict:
    key_of = jax.random.split(jax.random.key(seed), 13)
    stream_in = heavy_noise(key_of[0], (TOKENS, D), 1.0, 6.0, ((0, 8),), (0, 1, 8, 2.0))
    doc_lengths = draw_doc_lengths(jax.random.fold_in(key_of[12], 71), 0)
    first_gain = jnp.clip(1.0 + 0.1 * jax.random.normal(key_of[2], (D,), jnp.float32), 0.5, 1.5).astype(jnp.bfloat16)
    w_query = gaussian(key_of[3], (D, H * FEAT), D ** -0.5, 0.125, ((0, 8), (1, 4)))
    w_key = gaussian(key_of[4], (D, H * FEAT), D ** -0.5, 0.125, ((0, 8), (1, 4)))
    w_value = gaussian(key_of[5], (D, D), D ** -0.5, 0.125, ((0, 8), (1, 4)))
    w_out = gaussian(key_of[6], (D, D), 8 ** -0.5, 2.0, ((0, 4), (1, 8)))
    second_gain = jnp.clip(1.0 + 0.1 * jax.random.normal(key_of[7], (D,), jnp.float32), 0.5, 1.5).astype(jnp.bfloat16)
    w_gate = gaussian(key_of[8], (D, FF), D ** -0.5, 0.125, ((0, 8), (1, 4)))
    w_up = gaussian(key_of[9], (D, FF), D ** -0.5, 0.125, ((0, 8), (1, 4)))
    w_down = gaussian(key_of[10], (FF, D), FF ** -0.5, 0.078125, ((0, 4), (1, 8)))
    cotangent = heavy_noise(key_of[11], (TOKENS, D), 1.0, 6.0, ((0, 8),), (0, 1, 8, 2.0))
    return dict(stream_in=stream_in, doc_lengths=doc_lengths, first_gain=first_gain, w_query=w_query, w_key=w_key, w_value=w_value, w_out=w_out, second_gain=second_gain, w_gate=w_gate, w_up=w_up, w_down=w_down, cotangent=cotangent)


HIGH = lax.Precision.HIGHEST
EPSILON = 1e-06

@jax.custom_vjp
def low(v):
    return lax.optimization_barrier(v.astype(jnp.bfloat16)).astype(jnp.float32)

@jax.custom_vjp
def low_back(v):
    return v

def low_keep(v):
    return (low(v), None)

def low_pass(kept, grad):
    return (grad,)

def back_keep(v):
    return (v, None)

def back_low(kept, grad):
    return (low(grad),)
low.defvjp(low_keep, low_pass)
low_back.defvjp(back_keep, back_low)

def rms_scale(values, gain):
    inverse = lax.rsqrt(lax.optimization_barrier(jnp.mean(values * values, axis=-1, keepdims=True)) + EPSILON)
    return values * inverse * gain

def features(vectors):
    halved = vectors * 0.5
    products = (halved[..., :, None] * halved[..., None, :]).reshape(halved.shape[:-1] + (halved.shape[-1] * halved.shape[-1],))
    unit_col = jnp.ones(halved.shape[:-1] + (1,), jnp.float32)
    return jnp.concatenate([unit_col, halved, products * (1.0 / math.sqrt(2.0))], axis=-1)

def attend(queries, key_rows, value_rows, state_in, norm_in, allowed, carried):
    scores = jnp.einsum('ihf,jhf->hij', queries, key_rows, precision=HIGH) * 0.25
    weights = (1.0 + scores + 0.5 * scores * scores) * allowed[None]
    numerator = jnp.einsum('hij,jhd->ihd', weights, value_rows, precision=HIGH)
    denominator = jnp.transpose(lax.optimization_barrier(jnp.sum(weights, axis=2)))
    query_feat = features(queries) * carried[:, None, None]
    numerator = numerator + jnp.einsum('ihf,hfd->ihd', query_feat, state_in, precision=HIGH)
    denominator = denominator + jnp.einsum('ihf,hf->ih', query_feat, norm_in, precision=HIGH)
    return numerator / denominator[:, :, None]

def local_state(key_rows, value_rows, keep):
    key_feat = features(key_rows) * keep[:, None, None]
    return (jnp.einsum('jhf,jhd->hfd', key_feat, value_rows, precision=HIGH), lax.optimization_barrier(jnp.sum(key_feat, axis=0)))

def doc_starts(lengths, positions):
    ends = jnp.cumsum(lengths).astype(jnp.int32)
    starts = (ends - lengths).astype(jnp.int32)
    chosen = jnp.where(starts[None, :] <= positions[:, None], starts[None, :], jnp.zeros_like(starts)[None, :])
    return lax.optimization_barrier(jnp.max(chosen, axis=1)).astype(jnp.int32)

def block_attend(carry, block):
    state, norm_tot = carry
    queries, key_rows, value_rows, starts, first = block
    size = queries.shape[0]
    counter = jnp.arange(size, dtype=jnp.int32)
    allowed = ((counter[None, :] <= counter[:, None]) & (starts[None, :] == starts[:, None])).astype(jnp.float32)
    carried = (starts < first).astype(jnp.float32)
    keep = (starts == starts[size - 1]).astype(jnp.float32)
    closes = (starts[size - 1] >= first).astype(jnp.float32)
    output = attend(queries, key_rows, value_rows, state, norm_tot, allowed, carried)
    state_loc, norm_loc = local_state(key_rows, value_rows, keep)
    return ((state_loc + (1.0 - closes) * state, norm_loc + (1.0 - closes) * norm_tot), output)

def forward(stream, lengths, first_gain, w_query, w_key, w_value, w_out, second_gain, w_gate, w_up, w_down):
    tokens_all = stream.shape[0]
    block = math.gcd(tokens_all, 512)
    count = tokens_all // block
    heads = w_query.shape[1] // FEAT
    width = w_value.shape[1] // heads
    h_one = low(rms_scale(stream, first_gain))
    queries = low_back(low(jnp.dot(h_one, w_query, precision=HIGH)))
    key_rows = low_back(low(jnp.dot(h_one, w_key, precision=HIGH)))
    value_rows = low_back(low(jnp.dot(h_one, w_value, precision=HIGH)))
    positions = jnp.arange(tokens_all, dtype=jnp.int32)
    starts = doc_starts(lengths, positions)
    firsts = (jnp.arange(count, dtype=jnp.int32) * block).astype(jnp.int32)
    blocks = (queries.reshape(count, block, heads, FEAT), key_rows.reshape(count, block, heads, FEAT), value_rows.reshape(count, block, heads, width), starts.reshape(count, block), firsts)
    initial = (jnp.zeros((heads, PHI, width), jnp.float32), jnp.zeros((heads, PHI), jnp.float32))
    _, outputs = lax.scan(jax.checkpoint(block_attend), initial, blocks)
    mixed = low(outputs.reshape(tokens_all, heads * width))
    middle = stream + low_back(jnp.dot(mixed, w_out, precision=HIGH))
    h_two = low(rms_scale(middle, second_gain))
    gate = low_back(jnp.dot(h_two, w_gate, precision=HIGH))
    up_proj = low_back(jnp.dot(h_two, w_up, precision=HIGH))
    hidden = low(jax.nn.silu(gate) * up_proj)
    return middle + low_back(jnp.dot(hidden, w_down, precision=HIGH))

def reference(stream_in, doc_lengths, first_gain, w_query, w_key, w_value, w_out, second_gain, w_gate, w_up, w_down, cotangent):
    floats = tuple((item.astype(jnp.float32) for item in (stream_in, first_gain, w_query, w_key, w_value, w_out, second_gain, w_gate, w_up, w_down)))

    def wrapped(stream, gain_one, query_w, key_w, value_w, out_w, gain_two, gate_w, up_w, down_w):
        return forward(stream, doc_lengths, gain_one, query_w, key_w, value_w, out_w, gain_two, gate_w, up_w, down_w)
    result, pullback = jax.vjp(wrapped, *floats)
    grads = pullback(cotangent.astype(jnp.float32))
    return (result.astype(jnp.bfloat16), grads[0], grads[1], grads[2], grads[3], grads[4], grads[5], grads[6], grads[7], grads[8], grads[9])
```

```python
import functools
import math

import jax
import jax.numpy as jnp
from jax import lax
from jax.experimental import pallas as pl
from jax.experimental.pallas import tpu as pltpu
from jax.sharding import PartitionSpec as P

FEAT = 16
MESH = pl.DeviceIdType.MESH
MIB = 2**20


HIGH = lax.Precision.HIGHEST
EPSILON = 1e-06


def remote(src, dst, send, recv, device):
    return pltpu.make_async_remote_copy(
        src_ref=src,
        dst_ref=dst,
        send_sem=send,
        recv_sem=recv,
        device_id=device,
        device_id_type=MESH,
    )


class Place:
    def __init__(self, n):
        self.n, self.m = n, n // 2
        self.s, self.t = lax.axis_index("seq"), lax.axis_index("tp")
        self.o, self.i = self.s // 2, lax.rem(self.s, 2)
        self.right, self.left = (self.s + 2, self.t), (self.s - 2, self.t)
        self.pair = (self.o * 2 + 1 - self.i, self.t)
        self.has_right, self.has_left = self.o < self.m - 1, self.o > 0
        self.balanced = self.m >= 4
        m, o = self.m, self.o
        self.end = (o == 0) | (o == m - 1)
        self.next = (o == 1) | (o == m - 2)
        self.partner = jnp.where(
            o == 0, 1, jnp.where(o == m - 1, m - 2, jnp.where(o == 1, 0, m - 1))
        )

    def greet(self, others=()):
        barrier = pltpu.get_barrier_semaphore()

        def signal(device):
            pl.semaphore_signal(barrier, inc=1, device_id=device, device_id_type=MESH)

        pl.when(self.has_right)(lambda: signal(self.right))
        pl.when(self.has_left)(lambda: signal(self.left))
        signal(self.pair)
        for other in others:
            signal(other)
        beside = self.has_right.astype(jnp.int32) + self.has_left.astype(jnp.int32)
        pl.semaphore_wait(barrier, beside + (1 + len(others)))


class Gather:
    def __init__(self, at, own, held, sems):
        self.at, self.own_ref, self.held = at, own, held
        self.send, self.recv, self.half_recv, self.local = sems

    @staticmethod
    def scratch(n):
        return [
            pltpu.SemaphoreType.DMA((3, n)),
            pltpu.SemaphoreType.DMA((n,)),
            pltpu.SemaphoreType.DMA((1,)),
            pltpu.SemaphoreType.DMA((1,)),
        ]

    def copy(self, slot, way, own=False):
        at = self.at
        return remote(
            self.own_ref if own else self.held.at[slot],
            self.held.at[slot],
            self.send.at[way, slot],
            self.recv.at[slot],
            (at.right, at.left, at.pair)[way],
        )

    def half(self, slot, way, which):
        at, rows = self.at, self.held.shape[1] // 2
        part = pl.ds(which * rows, rows)
        return remote(
            self.held.at[slot, part],
            self.held.at[slot, part],
            self.send.at[way, slot],
            self.recv.at[slot] if which == 0 else self.half_recv.at[0],
            (at.right, at.left, at.pair)[way],
        )

    def local_copy(self):
        return pltpu.make_async_copy(self.own_ref, self.held.at[self.at.s], self.local.at[0])

    def own(self):
        at = self.at
        self.local_copy().start()
        pl.when(at.has_right)(lambda: self.copy(at.s, 0, True).start())
        pl.when(at.has_left)(lambda: self.copy(at.s, 1, True).start())
        self.copy(at.s, 2, True).start()

    def to_pair(self, slot, act):
        at = self.at
        if not at.balanced:
            act(self.copy(slot, 2))
            return
        partner = slot // 2 == at.partner
        pl.when(jnp.logical_not(partner & (at.end | at.next)))(lambda: act(self.copy(slot, 2)))
        pl.when(partner & at.end)(lambda: act(self.half(slot, 2, 0)))

    def step(self, k):
        at = self.at
        for way in (0, 1):
            slot = at.s - 2 * k if way == 0 else at.s + 2 * k
            there = at.o - k >= 0 if way == 0 else at.o + k < at.m
            on = at.has_right if way == 0 else at.has_left

            @pl.when(there)
            def _(slot=slot, on=on, way=way):
                self.copy(slot, 2).wait_recv()
                pl.when(on)(lambda: self.copy(slot, way).start())
                self.to_pair(slot, lambda c: c.start())

    def extra_copies(self, act):
        at = self.at
        slot = at.o * 2 + 1 - at.i
        pl.when(at.o == 0)(lambda: act(self.copy(slot, 0)))
        pl.when(at.o == at.m - 1)(lambda: act(self.copy(slot, 1)))
        pl.when(at.o == 1)(lambda: act(self.half(slot, 1, 1)))
        pl.when(at.o == at.m - 2)(lambda: act(self.half(slot, 0, 1)))

    def extra(self):
        at = self.at
        if at.balanced:
            slot = at.o * 2 + 1 - at.i
            pl.when(at.end | at.next)(lambda: self.copy(slot, 2).wait_recv())
            self.extra_copies(lambda c: c.start())

    def arrive(self):
        at = self.at
        self.local_copy().wait()
        for layer in range(at.m):
            slot = layer * 2 + 1 - at.i
            if not at.balanced:
                self.copy(slot, 2).wait_recv()
                continue
            met = (at.o == layer) & (at.end | at.next)
            halved = at.end & (at.partner == layer)
            pl.when(jnp.logical_not(met | halved))(lambda: self.copy(slot, 2).wait_recv())

            @pl.when(halved)
            def _():
                self.half(slot, 2, 0).wait_recv()
                self.half(slot, 2, 1).wait_recv()

    def drain(self):
        at = self.at
        pl.when(at.has_right)(lambda: self.copy(at.s, 0, True).wait_send())
        pl.when(at.has_left)(lambda: self.copy(at.s, 1, True).wait_send())
        self.copy(at.s, 2, True).wait_send()
        for k in range(1, at.m):
            for way in (0, 1):
                slot = at.s - 2 * k if way == 0 else at.s + 2 * k
                there = at.o - k >= 0 if way == 0 else at.o + k < at.m
                on = at.has_right if way == 0 else at.has_left

                @pl.when(there)
                def _(slot=slot, on=on, way=way):
                    pl.when(on)(lambda: self.copy(slot, way).wait_send())
                    self.to_pair(slot, lambda c: c.wait_send())

        if at.balanced:
            self.extra_copies(lambda c: c.wait_send())


def gather_events(groups):
    m = groups[0].at.m
    events = [groups[0].own]
    for g, group in enumerate(groups):
        for k in range(1, m):
            if k == max(1, m - 1) and g + 1 < len(groups):
                events.append(groups[g + 1].own)
            events.append(functools.partial(group.step, k))
            if k == 1 and g:
                events.append(groups[g - 1].extra)
    events.append(groups[-1].extra)
    return events


def gather_all(n, shards):
    count = len(shards)

    def kernel(*refs):
        ins, outs, sems = refs[:count], refs[count : 2 * count], refs[2 * count :]
        at = Place(n)
        at.greet()
        groups = [Gather(at, ins[g], outs[g], sems[4 * g : 4 * g + 4]) for g in range(count)]
        for event in gather_events(groups):
            event()
        for group in groups:
            group.arrive()
            group.drain()

    return pl.pallas_call(
        kernel,
        out_shape=[jax.ShapeDtypeStruct((n,) + a.shape, a.dtype) for a in shards],
        in_specs=[pl.BlockSpec(memory_space=pl.ANY)] * count,
        out_specs=[pl.BlockSpec(memory_space=pl.ANY)] * count,
        scratch_shapes=Gather.scratch(n) * count,
        compiler_params=pltpu.CompilerParams(collective_id=0, has_side_effects=True),
    )(*shards)


def add_rows(total, part, start, rows):
    step = next(size for size in (64, 32, 16, 8) if rows % size == 0)

    @pl.loop(0, rows // step)
    def _(j):
        at = pl.ds(pl.multiple_of(start + j * step, 8), step)
        both = total[at, :].astype(jnp.float32) + part[at, :].astype(jnp.float32)
        total[at, :] = both.astype(total.dtype)


class Scatter:
    def __init__(self, at, parts, out, bufs, sems):
        self.at, self.parts, self.out = at, parts, out
        self.mine, self.from_pair, self.from_line, self.extra_ref = bufs
        (
            self.pair_send,
            self.pair_recv,
            self.line_send,
            self.line_recv,
            self.extra_send,
            self.extra_recv,
            self.local,
        ) = sems
        self.rows = self.mine.shape[1]

    @staticmethod
    def scratch(n, shape, dtype):
        m = n // 2
        return [pltpu.VMEM((size,) + shape, dtype) for size in (m, m, m + 1, 2)] + [
            pltpu.SemaphoreType.DMA((m,)),
            pltpu.SemaphoreType.DMA((m,)),
            pltpu.SemaphoreType.DMA((m,)),
            pltpu.SemaphoreType.DMA((m + 1,)),
            pltpu.SemaphoreType.DMA((2,)),
            pltpu.SemaphoreType.DMA((2,)),
            pltpu.SemaphoreType.DMA((m + 2,)),
        ]

    def load(self, layer):
        return pltpu.make_async_copy(
            self.parts.at[layer * 2 + self.at.i], self.mine.at[layer], self.local.at[layer]
        )

    def load_extra(self):
        at = self.at
        return pltpu.make_async_copy(
            self.parts.at[at.o * 2 + 1 - at.i], self.extra_ref.at[1], self.local.at[at.m]
        )

    def store(self):
        at = self.at
        return pltpu.make_async_copy(self.mine.at[at.o], self.out, self.local.at[at.m + 1])

    def to_pair(self, layer):
        return remote(
            self.parts.at[layer * 2 + 1 - self.at.i],
            self.from_pair.at[layer],
            self.pair_send.at[layer],
            self.pair_recv.at[layer],
            self.at.pair,
        )

    def half_to_pair(self, layer, which, src):
        half = self.rows // 2
        part = pl.ds(which * half, half)
        return remote(
            src.at[part],
            self.from_pair.at[layer, part],
            self.pair_send.at[layer] if which == 0 else self.extra_send.at[1],
            self.pair_recv.at[layer] if which == 0 else self.extra_recv.at[1],
            self.at.pair,
        )

    def sum_to_pair(self):
        return remote(
            self.extra_ref.at[1],
            self.from_pair.at[self.at.o],
            self.pair_send.at[self.at.o],
            self.pair_recv.at[self.at.o],
            self.at.pair,
        )

    def along(self, layer, way):
        at = self.at
        there = layer if way == 0 else jnp.where(layer == at.o - 1, at.m, layer)
        return remote(
            self.mine.at[layer],
            self.from_line.at[there],
            self.line_send.at[layer],
            self.line_recv.at[there],
            (at.right, at.left)[way],
        )

    def wait_line(self, place):
        remote(
            self.mine.at[0],
            self.from_line.at[place],
            self.line_send.at[0],
            self.line_recv.at[place],
            self.at.right,
        ).wait_recv()

    def shifted(self, way, which=None):
        at, half = self.at, self.rows // 2
        src, dst = self.parts.at[at.partner * 2 + 1 - at.i], self.extra_ref.at[0]
        if which is not None:
            src, dst = src.at[pl.ds(half, half)], dst.at[pl.ds(half, half)]
        return remote(
            src, dst, self.extra_send.at[0], self.extra_recv.at[0], (at.right, at.left)[way]
        )

    def far_first(self):
        at = self.at
        for d in range(at.m - 1, 0, -1):
            yield at.o + d, at.o + d < at.m
            yield at.o - d, at.o - d >= 0

    def pair_copies(self, act):
        at = self.at
        for layer, there in self.far_first():
            if not at.balanced:
                pl.when(there)(lambda: act(self.to_pair(layer)))
                continue
            partner = layer == at.partner
            pl.when(there & jnp.logical_not(partner & (at.end | at.next)))(
                lambda: act(self.to_pair(layer))
            )
            pl.when(there & partner & at.end)(
                lambda: act(self.half_to_pair(layer, 0, self.parts.at[layer * 2 + 1 - at.i]))
            )
        if not at.balanced:
            act(self.to_pair(at.o))
            return
        pl.when(jnp.logical_not(at.end | at.next))(lambda: act(self.to_pair(at.o)))
        pl.when(at.next)(
            lambda: act(self.half_to_pair(at.o, 0, self.parts.at[at.o * 2 + 1 - at.i]))
        )

    def shift_copies(self, act):
        at = self.at
        if at.balanced:
            pl.when(at.o == 0)(lambda: act(self.shifted(0, 1)))
            pl.when(at.o == at.m - 1)(lambda: act(self.shifted(1, 1)))
            pl.when(at.o == 1)(lambda: act(self.shifted(1)))
            pl.when(at.o == at.m - 2)(lambda: act(self.shifted(0)))

    def start(self):
        at = self.at
        self.shift_copies(lambda c: c.start())
        self.pair_copies(lambda c: c.start())
        for layer in range(at.m):
            self.load(layer).start()
        if at.balanced:
            self.load_extra().start()

    def extra(self):
        at = self.at
        if not at.balanced:
            return
        self.load_extra().wait()
        half = self.rows // 2

        @pl.when(at.end)
        def _():
            self.shifted(0).wait_recv()
            add_rows(self.extra_ref.at[1], self.extra_ref.at[0], 0, self.rows)
            self.sum_to_pair().start()

        @pl.when(at.next)
        def _():
            self.shifted(0, 1).wait_recv()
            add_rows(self.extra_ref.at[1], self.extra_ref.at[0], half, half)
            self.half_to_pair(at.o, 1, self.extra_ref.at[1]).start()

    def wait_pair(self, layer):
        at = self.at
        if not at.balanced:
            self.to_pair(layer).wait_recv()
            return
        partner, own = layer == at.partner, layer == at.o
        parted = (partner & at.end) | (own & at.next)
        pl.when(jnp.logical_not((partner & (at.end | at.next)) | (own & at.next)))(
            lambda: self.to_pair(layer).wait_recv()
        )
        pl.when(parted)(lambda: self.half_to_pair(layer, 0, self.extra_ref.at[1]).wait_recv())
        pl.when(own & at.next)(
            lambda: self.half_to_pair(layer, 1, self.extra_ref.at[1]).wait_recv()
        )

    def step(self, d):
        at = self.at
        for way in (0, 1):
            layer = at.o + d if way == 0 else at.o - d
            there = layer < at.m if way == 0 else layer >= 0
            behind = at.has_left if way == 0 else at.has_right

            @pl.when(there)
            def _(layer=layer, behind=behind, way=way):
                mine = self.mine.at[layer]
                self.load(layer).wait()
                self.wait_pair(layer)
                if at.balanced:
                    partner = layer == at.partner
                    pl.when(jnp.logical_not(partner & (at.end | at.next)))(
                        lambda: add_rows(mine, self.from_pair.at[layer], 0, self.rows)
                    )
                    pl.when(partner & at.end)(
                        lambda: add_rows(mine, self.from_pair.at[layer], 0, self.rows // 2)
                    )
                else:
                    add_rows(mine, self.from_pair.at[layer], 0, self.rows)

                @pl.when(behind)
                def _():
                    self.wait_line(layer)
                    add_rows(mine, self.from_line.at[layer], 0, self.rows)

                self.along(layer, way).start()

    def final(self):
        at = self.at
        mine = self.mine.at[at.o]
        self.load(at.o).wait()
        self.wait_pair(at.o)
        add_rows(mine, self.from_pair.at[at.o], 0, self.rows)

        @pl.when(at.has_left)
        def _():
            self.wait_line(at.o)
            add_rows(mine, self.from_line.at[at.o], 0, self.rows)

        @pl.when(at.has_right)
        def _():
            self.wait_line(at.m)
            add_rows(mine, self.from_line.at[at.m], 0, self.rows)

        self.store().start()

    def drain(self):
        at = self.at
        self.pair_copies(lambda c: c.wait_send())
        if at.balanced:
            pl.when(at.end)(lambda: self.sum_to_pair().wait_send())
            pl.when(at.next)(
                lambda: self.half_to_pair(at.o, 1, self.extra_ref.at[1]).wait_send()
            )
        self.shift_copies(lambda c: c.wait_send())
        for d in range(1, at.m):
            pl.when(at.o + d < at.m)(lambda: self.along(at.o + d, 0).wait_send())
            pl.when(at.o - d >= 0)(lambda: self.along(at.o - d, 1).wait_send())
        self.store().wait()


def scatter_all(n, parts):
    count = len(parts)
    shapes = [(a.shape[1:], a.dtype) for a in parts]

    def kernel(*refs):
        ins, outs, rest = refs[:count], refs[count : 2 * count], refs[2 * count :]
        at = Place(n)
        at.greet()
        groups = [
            Scatter(at, ins[g], outs[g], rest[11 * g : 11 * g + 4], rest[11 * g + 4 : 11 * g + 11])
            for g in range(count)
        ]
        groups[0].start()
        groups[1].start()
        for g, group in enumerate(groups):
            for d in range(at.m - 1, 0, -1):
                group.step(d)
                if d == at.m - 1 and g + 2 < count:
                    groups[g + 2].start()
            group.extra()
            if g:
                groups[g - 1].final()
        groups[-1].final()
        for group in groups:
            group.drain()

    return pl.pallas_call(
        kernel,
        out_shape=[jax.ShapeDtypeStruct(*kind) for kind in shapes],
        in_specs=[pl.BlockSpec(memory_space=pl.ANY)] * count,
        out_specs=[pl.BlockSpec(memory_space=pl.ANY)] * count,
        scratch_shapes=sum((Scatter.scratch(n, *kind) for kind in shapes), []),
        compiler_params=pltpu.CompilerParams(
            collective_id=1, has_side_effects=True, vmem_limit_bytes=60 * MIB
        ),
    )(*parts)


def entering(value, axis, join, neutral):
    place = lax.axis_index(axis)
    gathered = jax.tree.map(
        lambda a, kind: lax.all_gather(a.astype(kind), axis),
        value,
        (jnp.bfloat16, jnp.bfloat16, jnp.bfloat16),
    )
    state = jax.tree.map(lambda a, e: jnp.zeros_like(a) + jnp.asarray(e, a.dtype), value, neutral)

    def one(step, state):
        return join(
            state,
            jax.tree.map(
                lambda a, own: lax.dynamic_index_in_dim(a, step, 0, False).astype(own.dtype),
                gathered,
                value,
            ),
        )

    return lax.fori_loop(0, place, one, state)


def entering_2(value, axis, combine, identity):
    devices, index = (lax.axis_size(axis), lax.axis_index(axis))
    everything = jax.tree.map(
        lambda part, kind: lax.all_gather(part.astype(kind), axis),
        value,
        jax.tree.map(lambda a: jnp.bfloat16 if a.dtype == jnp.float32 else a.dtype, value),
    )
    start = jax.tree.map(
        lambda part, zero: jnp.broadcast_to(jnp.asarray(zero, part.dtype), part.shape),
        value,
        identity,
    )

    def step(k, before):
        at = devices - 1 - k
        reached = at > index
        new = combine(
            before, jax.tree.map(lambda part, own: part[at].astype(own.dtype), everything, value)
        )
        return jax.tree.map(lambda a, b: jnp.where(reached, a, b), new, before)

    return lax.fori_loop(0, devices, step, start)


def rms_scale(values, gain):
    inverse = lax.rsqrt(jnp.mean(values * values, axis=-1, keepdims=True) + EPSILON)
    return values * inverse * gain


def features(vectors):
    halved = vectors * 0.5
    products = (halved[..., :, None] * halved[..., None, :]).reshape(
        halved.shape[:-1] + (halved.shape[-1] * halved.shape[-1],)
    )
    unit_col = jnp.ones(halved.shape[:-1] + (1,), jnp.float32)
    return jnp.concatenate([unit_col, halved, products * (1.0 / math.sqrt(2.0))], axis=-1)


def attend(queries, key_rows, value_rows, state_in, norm_in, allowed, carried):
    scores = jnp.einsum("ihf,jhf->hij", queries, key_rows, precision=HIGH) * 0.25
    weights = (1.0 + scores + 0.5 * scores * scores) * allowed[None]
    numerator = jnp.einsum("hij,jhd->ihd", weights, value_rows, precision=HIGH)
    denominator = jnp.transpose(jnp.sum(weights, axis=2))
    query_feat = features(queries) * carried[:, None, None]
    numerator = numerator + jnp.einsum("ihf,hfd->ihd", query_feat, state_in, precision=HIGH)
    denominator = denominator + jnp.einsum("ihf,hf->ih", query_feat, norm_in, precision=HIGH)
    return numerator / denominator[:, :, None]


def local_state(key_rows, value_rows, keep):
    key_feat = features(key_rows) * keep[:, None, None]
    return (
        jnp.einsum("jhf,jhd->hfd", key_feat, value_rows, precision=HIGH),
        jnp.sum(key_feat, axis=0),
    )


def chain(earlier, later):
    state_a, norm_a, closes_a = earlier
    state_b, norm_b, closes_b = later
    carry_on = 1.0 - closes_b
    return (
        state_b + carry_on * state_a,
        norm_b + carry_on * norm_a,
        jnp.maximum(closes_a, closes_b),
    )


def doc_starts(lengths, positions):
    ends = jnp.cumsum(lengths)
    starts = ends - lengths
    chosen = jnp.where(
        starts[None, :] <= positions[:, None], starts[None, :], jnp.zeros_like(starts)[None, :]
    )
    return jnp.max(chosen, axis=1)


def contract_rows(left, right):
    return lax.dot_general(
        left, right, (((0,), (0,)), ((), ())), preferred_element_type=jnp.float32
    )


def contract_cols(left, right):
    return lax.dot_general(
        left, right, (((1,), (1,)), ((), ())), preferred_element_type=jnp.float32
    )


def on_device(
    stream_in,
    doc_lengths,
    first_gain,
    w_query,
    w_key,
    w_value,
    w_out,
    second_gain,
    w_gate,
    w_up,
    w_down,
    cotangent,
):
    n = lax.axis_size("seq")
    qkv_own = jnp.concatenate([w_query, w_key, w_value], axis=1)
    gains_own = jnp.concatenate([first_gain, second_gain]).astype(jnp.float32)
    gains_own = jnp.broadcast_to(gains_own[None], (16, gains_own.shape[0]))
    gains, qkv_full, out_full, gate_full, up_full, down_full = gather_all(
        n, (gains_own, qkv_own, w_out, w_gate, w_up, w_down)
    )
    depth = first_gain.shape[0]
    first_full = gains[:, 0, :depth].reshape(-1).astype(jnp.bfloat16)
    second_full = gains[:, 0, depth:].reshape(-1).astype(jnp.bfloat16)
    qkv_full = qkv_full.reshape(-1, qkv_full.shape[-1])
    q_wide, k_wide = w_query.shape[1], w_key.shape[1]
    query_full = qkv_full[:, :q_wide]
    key_full = qkv_full[:, q_wide : q_wide + k_wide]
    value_full = qkv_full[:, q_wide + k_wide :]
    gate_full = gate_full.reshape(-1, gate_full.shape[-1])
    up_full = up_full.reshape(-1, up_full.shape[-1])
    out_full = jnp.swapaxes(out_full, 0, 1).reshape(out_full.shape[1], -1)
    down_full = jnp.swapaxes(down_full, 0, 1).reshape(down_full.shape[1], -1)
    row_count = stream_in.shape[0]
    heads_local = query_full.shape[1] // FEAT
    head_width = value_full.shape[1] // heads_local
    dev_start = lax.axis_index("seq") * row_count
    positions = dev_start + jnp.arange(row_count, dtype=jnp.int32)
    starts = doc_starts(doc_lengths, positions)
    counter = jnp.arange(row_count, dtype=jnp.int32)
    allowed = (
        (counter[None, :] <= counter[:, None]) & (starts[None, :] == starts[:, None])
    ).astype(jnp.float32)
    carried = (starts < dev_start).astype(jnp.float32)
    keep = (starts == starts[row_count - 1]).astype(jnp.float32)
    closes = (starts[row_count - 1 :] >= dev_start).astype(jnp.float32)
    stream_f = stream_in.astype(jnp.float32)
    first_gf = first_full.astype(jnp.float32)
    second_gf = second_full.astype(jnp.float32)
    h_one = rms_scale(stream_f, first_gf).astype(jnp.bfloat16)
    query_b = jnp.dot(h_one, query_full, preferred_element_type=jnp.float32).astype(jnp.bfloat16)
    key_b = jnp.dot(h_one, key_full, preferred_element_type=jnp.float32).astype(jnp.bfloat16)
    value_b = jnp.dot(h_one, value_full, preferred_element_type=jnp.float32).astype(jnp.bfloat16)
    query_f = query_b.astype(jnp.float32).reshape(row_count, heads_local, FEAT)
    key_f = key_b.astype(jnp.float32).reshape(row_count, heads_local, FEAT)
    value_f = value_b.astype(jnp.float32).reshape(row_count, heads_local, head_width)
    state_loc, norm_loc = local_state(key_f, value_f, keep)
    identity = (jnp.zeros_like(state_loc), jnp.zeros_like(norm_loc), jnp.zeros((1,), jnp.float32))
    state_in, norm_in, _ = entering((state_loc, norm_loc, closes), "seq", chain, identity)

    def attend_local(queries, key_rows, value_rows, state_arg, norm_arg):
        return attend(queries, key_rows, value_rows, state_arg, norm_arg, allowed, carried)

    attn, attend_pull = jax.vjp(attend_local, query_f, key_f, value_f, state_in, norm_in)
    mixed_b = attn.reshape(row_count, heads_local * head_width).astype(jnp.bfloat16)
    attn_term = jnp.dot(mixed_b, out_full, preferred_element_type=jnp.float32)
    middle = stream_f + lax.psum(attn_term.astype(jnp.bfloat16), "tp").astype(jnp.float32)
    h_two = rms_scale(middle, second_gf).astype(jnp.bfloat16)
    gate = jnp.dot(h_two, gate_full, preferred_element_type=jnp.float32)
    up_proj = jnp.dot(h_two, up_full, preferred_element_type=jnp.float32)
    sigma = jax.nn.sigmoid(gate)
    silu_gate = gate * sigma
    hidden = (silu_gate * up_proj).astype(jnp.bfloat16)
    feed_term = jnp.dot(hidden, down_full, preferred_element_type=jnp.float32)
    grad_down = contract_rows(hidden, cotangent)
    dhidden = contract_cols(cotangent, down_full)
    dgate_b = (dhidden * up_proj * sigma * (1.0 + gate * (1.0 - sigma))).astype(jnp.bfloat16)
    dup_b = (dhidden * silu_gate).astype(jnp.bfloat16)
    grad_gate = contract_rows(h_two, dgate_b)
    grad_up = contract_rows(h_two, dup_b)
    dh_local_two = contract_cols(dgate_b, gate_full) + contract_cols(dup_b, up_full)
    activations = (
        middle + lax.psum(feed_term.astype(jnp.bfloat16), "tp").astype(jnp.float32)
    ).astype(jnp.bfloat16)
    dh_two = lax.psum(dh_local_two.astype(jnp.bfloat16), "tp").astype(jnp.float32)
    _, norm_two_pull = jax.vjp(rms_scale, middle, second_gf)
    dmid_norm, grad_second = norm_two_pull(dh_two)
    dmid = cotangent.astype(jnp.float32) + dmid_norm
    dmid_b = dmid.astype(jnp.bfloat16)
    grad_out = contract_rows(mixed_b, dmid_b)
    dattn = contract_cols(dmid_b, out_full).reshape(row_count, heads_local, head_width)
    dq_own, dk_own, dv_own, pull_state, pull_norm = attend_pull(dattn)
    back_state, back_norm, _ = entering_2((pull_state, pull_norm, closes), "seq", chain, identity)

    def state_local(key_rows, value_rows):
        return local_state(key_rows, value_rows, keep)

    _, state_pull = jax.vjp(state_local, key_f, value_f)
    dk_far, dv_far = state_pull((back_state, back_norm))
    dq_b = dq_own.reshape(row_count, heads_local * FEAT).astype(jnp.bfloat16)
    dk_b = (dk_own + dk_far).reshape(row_count, heads_local * FEAT).astype(jnp.bfloat16)
    dv_b = (dv_own + dv_far).reshape(row_count, heads_local * head_width).astype(jnp.bfloat16)
    grad_query = contract_rows(h_one, dq_b)
    grad_key = contract_rows(h_one, dk_b)
    grad_value = contract_rows(h_one, dv_b)
    dh_local = (
        contract_cols(dq_b, query_full)
        + contract_cols(dk_b, key_full)
        + contract_cols(dv_b, value_full)
    )
    dh_one = lax.psum(dh_local.astype(jnp.bfloat16), "tp").astype(jnp.float32)
    _, norm_one_pull = jax.vjp(rms_scale, stream_f, first_gf)
    dstream_norm, grad_first = norm_one_pull(dh_one)
    input_grad = dmid + dstream_norm
    def rows_of(g):
        return g.astype(jnp.bfloat16).reshape((n, g.shape[0] // n) + g.shape[1:])

    def cols_of(g):
        g = g.astype(jnp.bfloat16).reshape(g.shape[0], n, g.shape[1] // n)
        return jnp.swapaxes(g, 0, 1)

    grad_qkv = jnp.concatenate([grad_query, grad_key, grad_value], axis=1)
    gains_part = jnp.concatenate(
        [grad_first.reshape(n, 1, depth), grad_second.reshape(n, 1, depth)], axis=2
    )
    gains_part = jnp.broadcast_to(gains_part, (n, 16, 2 * depth))
    own_down, own_gate, own_up, own_out, own_qkv, own_gains = scatter_all(
        n,
        (
            cols_of(grad_down),
            rows_of(grad_gate),
            rows_of(grad_up),
            cols_of(grad_out),
            rows_of(grad_qkv),
            gains_part,
        ),
    )
    own_qkv = own_qkv.astype(jnp.float32)
    return (
        activations,
        input_grad,
        own_gains[0, :depth],
        own_qkv[:, :q_wide],
        own_qkv[:, q_wide : q_wide + k_wide],
        own_qkv[:, q_wide + k_wide :],
        own_out.astype(jnp.float32),
        own_gains[0, depth:],
        own_gate.astype(jnp.float32),
        own_up.astype(jnp.float32),
        own_down.astype(jnp.float32),
    )


def solution(mesh):
    placed = (
        P("seq", None),
        P(),
        P("seq"),
        P("seq", "tp"),
        P("seq", "tp"),
        P("seq", "tp"),
        P("tp", "seq"),
        P("seq"),
        P("seq", "tp"),
        P("seq", "tp"),
        P("tp", "seq"),
        P("seq", None),
    )
    return jax.shard_map(
        on_device,
        mesh=mesh,
        in_specs=placed,
        out_specs=(
            P("seq", None),
            P("seq", None),
            P("seq"),
            P("seq", "tp"),
            P("seq", "tp"),
            P("seq", "tp"),
            P("tp", "seq"),
            P("seq"),
            P("seq", "tp"),
            P("seq", "tp"),
            P("tp", "seq"),
        ),
        check_vma=False,
    )
```

```python
import functools

import jax
import jax.numpy as jnp
import numpy as np
from jax import lax
from jax.experimental import pallas as pl
from jax.experimental.pallas import tpu as pltpu
from jax.sharding import PartitionSpec as P

FEAT = 16
EPSILON = 1e-06
MESH = pl.DeviceIdType.MESH
MIB = 2**20


def remote(src, dst, send, recv, device):
    return pltpu.make_async_remote_copy(
        src_ref=src,
        dst_ref=dst,
        send_sem=send,
        recv_sem=recv,
        device_id=device,
        device_id_type=MESH,
    )


class Place:
    def __init__(self, n):
        self.n, self.m = n, n // 2
        self.s, self.t = lax.axis_index("seq"), lax.axis_index("tp")
        self.o, self.i = self.s // 2, lax.rem(self.s, 2)
        self.right, self.left = (self.s + 2, self.t), (self.s - 2, self.t)
        self.pair = (self.o * 2 + 1 - self.i, self.t)
        self.has_right, self.has_left = self.o < self.m - 1, self.o > 0
        self.balanced = self.m >= 4
        m, o = self.m, self.o
        self.end = (o == 0) | (o == m - 1)
        self.next = (o == 1) | (o == m - 2)
        self.partner = jnp.where(
            o == 0, 1, jnp.where(o == m - 1, m - 2, jnp.where(o == 1, 0, m - 1))
        )

    def greet(self, others=()):
        barrier = pltpu.get_barrier_semaphore()

        def signal(device):
            pl.semaphore_signal(barrier, inc=1, device_id=device, device_id_type=MESH)

        pl.when(self.has_right)(lambda: signal(self.right))
        pl.when(self.has_left)(lambda: signal(self.left))
        signal(self.pair)
        for other in others:
            signal(other)
        beside = self.has_right.astype(jnp.int32) + self.has_left.astype(jnp.int32)
        pl.semaphore_wait(barrier, beside + (1 + len(others)))


class Gather:
    def __init__(self, at, own, held, sems):
        self.at, self.own_ref, self.held = at, own, held
        self.send, self.recv, self.half_recv, self.local = sems

    @staticmethod
    def scratch(n):
        return [
            pltpu.SemaphoreType.DMA((3, n)),
            pltpu.SemaphoreType.DMA((n,)),
            pltpu.SemaphoreType.DMA((1,)),
            pltpu.SemaphoreType.DMA((1,)),
        ]

    def slot(self, slot, start=0, rows=None):
        if self.held.ndim == 3:
            return self.held.at[slot] if rows is None else self.held.at[slot, pl.ds(start, rows)]
        tall = self.own_ref.shape[0]
        first = pl.multiple_of(slot * tall, 16) + start
        return self.held.at[pl.ds(first, tall if rows is None else rows)]

    def copy(self, slot, way, own=False):
        at = self.at
        return remote(
            self.own_ref if own else self.slot(slot),
            self.slot(slot),
            self.send.at[way, slot],
            self.recv.at[slot],
            (at.right, at.left, at.pair)[way],
        )

    def half(self, slot, way, which):
        at, rows = self.at, self.own_ref.shape[0] // 2
        part = self.slot(slot, which * rows, rows)
        return remote(
            part,
            part,
            self.send.at[way, slot],
            self.recv.at[slot] if which == 0 else self.half_recv.at[0],
            (at.right, at.left, at.pair)[way],
        )

    def local_copy(self):
        return pltpu.make_async_copy(self.own_ref, self.slot(self.at.s), self.local.at[0])

    def own(self):
        at = self.at
        self.local_copy().start()
        pl.when(at.has_right)(lambda: self.copy(at.s, 0, True).start())
        pl.when(at.has_left)(lambda: self.copy(at.s, 1, True).start())
        self.copy(at.s, 2, True).start()

    def to_pair(self, slot, act):
        at = self.at
        if not at.balanced:
            act(self.copy(slot, 2))
            return
        partner = slot // 2 == at.partner
        pl.when(jnp.logical_not(partner & (at.end | at.next)))(lambda: act(self.copy(slot, 2)))
        pl.when(partner & at.end)(lambda: act(self.half(slot, 2, 0)))

    def step(self, k):
        at = self.at
        for way in (0, 1):
            slot = at.s - 2 * k if way == 0 else at.s + 2 * k
            there = at.o - k >= 0 if way == 0 else at.o + k < at.m
            on = at.has_right if way == 0 else at.has_left

            @pl.when(there)
            def _(slot=slot, on=on, way=way):
                self.copy(slot, 2).wait_recv()
                pl.when(on)(lambda: self.copy(slot, way).start())
                self.to_pair(slot, lambda c: c.start())

    def extra_copies(self, act):
        at = self.at
        slot = at.o * 2 + 1 - at.i
        pl.when(at.o == 0)(lambda: act(self.copy(slot, 0)))
        pl.when(at.o == at.m - 1)(lambda: act(self.copy(slot, 1)))
        pl.when(at.o == 1)(lambda: act(self.half(slot, 1, 1)))
        pl.when(at.o == at.m - 2)(lambda: act(self.half(slot, 0, 1)))

    def extra(self):
        at = self.at
        if at.balanced:
            slot = at.o * 2 + 1 - at.i
            pl.when(at.end | at.next)(lambda: self.copy(slot, 2).wait_recv())
            self.extra_copies(lambda c: c.start())

    def arrive(self):
        at = self.at
        self.local_copy().wait()
        for layer in range(at.m):
            slot = layer * 2 + 1 - at.i
            if not at.balanced:
                self.copy(slot, 2).wait_recv()
                continue
            met = (at.o == layer) & (at.end | at.next)
            halved = at.end & (at.partner == layer)
            pl.when(jnp.logical_not(met | halved))(lambda: self.copy(slot, 2).wait_recv())

            @pl.when(halved)
            def _():
                self.half(slot, 2, 0).wait_recv()
                self.half(slot, 2, 1).wait_recv()

    def drain(self):
        at = self.at
        pl.when(at.has_right)(lambda: self.copy(at.s, 0, True).wait_send())
        pl.when(at.has_left)(lambda: self.copy(at.s, 1, True).wait_send())
        self.copy(at.s, 2, True).wait_send()
        for k in range(1, at.m):
            for way in (0, 1):
                slot = at.s - 2 * k if way == 0 else at.s + 2 * k
                there = at.o - k >= 0 if way == 0 else at.o + k < at.m
                on = at.has_right if way == 0 else at.has_left

                @pl.when(there)
                def _(slot=slot, on=on, way=way):
                    pl.when(on)(lambda: self.copy(slot, way).wait_send())
                    self.to_pair(slot, lambda c: c.wait_send())

        if at.balanced:
            self.extra_copies(lambda c: c.wait_send())


def gather_events(groups):
    m = groups[0].at.m
    events = [groups[0].own]
    for g, group in enumerate(groups):
        for k in range(1, m):
            if k == max(1, m - 1) and g + 1 < len(groups):
                events.append(groups[g + 1].own)
            events.append(functools.partial(group.step, k))
            if k == 1 and g:
                events.append(groups[g - 1].extra)
    events.append(groups[-1].extra)
    return events


def add_rows(total, part, start, rows):
    step = next(size for size in (64, 32, 16, 8) if rows % size == 0)

    @pl.loop(0, rows // step)
    def _(j):
        at = pl.ds(pl.multiple_of(start + j * step, 8), step)
        both = total[at, :].astype(jnp.float32) + part[at, :].astype(jnp.float32)
        total[at, :] = both.astype(total.dtype)


class Scatter:
    def __init__(self, at, parts, out, landing, bufs, sems):
        self.at, self.parts, self.out = at, parts, out
        self.from_pair, self.from_line, self.shifted_in = landing
        self.mine, self.aside, self.stage = bufs
        (
            self.pair_send,
            self.pair_recv,
            self.line_send,
            self.line_recv,
            self.extra_send,
            self.extra_recv,
            self.local,
        ) = sems
        self.rows = self.mine.shape[1]

    @staticmethod
    def landing(n, shape, dtype):
        m = n // 2
        return [jax.ShapeDtypeStruct((size,) + shape, dtype) for size in (m, m + 1, 1)]

    @staticmethod
    def scratch(n, shape, dtype):
        m = n // 2
        return [pltpu.VMEM((size,) + shape, dtype) for size in (m, 1)] + [
            pltpu.SemaphoreType.DMA((m,)),
            pltpu.SemaphoreType.DMA((m,)),
            pltpu.SemaphoreType.DMA((m,)),
            pltpu.SemaphoreType.DMA((m + 1,)),
            pltpu.SemaphoreType.DMA((2,)),
            pltpu.SemaphoreType.DMA((2,)),
            pltpu.SemaphoreType.DMA((m + 4,)),
        ]

    def load(self, layer):
        return pltpu.make_async_copy(
            self.parts.at[layer * 2 + self.at.i], self.mine.at[layer], self.local.at[layer]
        )

    def load_aside(self):
        at = self.at
        return pltpu.make_async_copy(
            self.parts.at[at.o * 2 + 1 - at.i], self.aside.at[0], self.local.at[at.m]
        )

    def store(self):
        at = self.at
        return pltpu.make_async_copy(self.mine.at[at.o], self.out, self.local.at[at.m + 1])

    def to_stage(self, src, which, start=0, rows=None):
        part = pl.ds(start, self.rows if rows is None else rows)
        return pltpu.make_async_copy(
            src.at[part], self.stage.at[which, part], self.local.at[self.at.m + 2 + which]
        )

    def to_pair(self, layer):
        return remote(
            self.parts.at[layer * 2 + 1 - self.at.i],
            self.from_pair.at[layer],
            self.pair_send.at[layer],
            self.pair_recv.at[layer],
            self.at.pair,
        )

    def half_to_pair(self, layer, which, src):
        half = self.rows // 2
        part = pl.ds(which * half, half)
        return remote(
            src.at[part],
            self.from_pair.at[layer, part],
            self.pair_send.at[layer] if which == 0 else self.extra_send.at[1],
            self.pair_recv.at[layer] if which == 0 else self.extra_recv.at[1],
            self.at.pair,
        )

    def sum_to_pair(self):
        return remote(
            self.aside.at[0],
            self.from_pair.at[self.at.o],
            self.pair_send.at[self.at.o],
            self.pair_recv.at[self.at.o],
            self.at.pair,
        )

    def along(self, layer, way):
        at = self.at
        there = layer if way == 0 else jnp.where(layer == at.o - 1, at.m, layer)
        return remote(
            self.mine.at[layer],
            self.from_line.at[there],
            self.line_send.at[layer],
            self.line_recv.at[there],
            (at.right, at.left)[way],
        )

    def wait_line(self, place):
        remote(
            self.mine.at[0],
            self.from_line.at[place],
            self.line_send.at[0],
            self.line_recv.at[place],
            self.at.right,
        ).wait_recv()

    def shifted(self, way, which=None):
        at, half = self.at, self.rows // 2
        src, dst = self.parts.at[at.partner * 2 + 1 - at.i], self.shifted_in.at[0]
        if which is not None:
            src, dst = src.at[pl.ds(half, half)], dst.at[pl.ds(half, half)]
        return remote(
            src, dst, self.extra_send.at[0], self.extra_recv.at[0], (at.right, at.left)[way]
        )

    def far_first(self):
        at = self.at
        for d in range(at.m - 1, 0, -1):
            yield at.o + d, at.o + d < at.m
            yield at.o - d, at.o - d >= 0

    def pair_copies(self, act):
        at = self.at
        for layer, there in self.far_first():
            if not at.balanced:
                pl.when(there)(lambda: act(self.to_pair(layer)))
                continue
            partner = layer == at.partner
            pl.when(there & jnp.logical_not(partner & (at.end | at.next)))(
                lambda: act(self.to_pair(layer))
            )
            pl.when(there & partner & at.end)(
                lambda: act(self.half_to_pair(layer, 0, self.parts.at[layer * 2 + 1 - at.i]))
            )
        if not at.balanced:
            act(self.to_pair(at.o))
            return
        pl.when(jnp.logical_not(at.end | at.next))(lambda: act(self.to_pair(at.o)))
        pl.when(at.next)(
            lambda: act(self.half_to_pair(at.o, 0, self.parts.at[at.o * 2 + 1 - at.i]))
        )

    def shift_copies(self, act):
        at = self.at
        if at.balanced:
            pl.when(at.o == 0)(lambda: act(self.shifted(0, 1)))
            pl.when(at.o == at.m - 1)(lambda: act(self.shifted(1, 1)))
            pl.when(at.o == 1)(lambda: act(self.shifted(1)))
            pl.when(at.o == at.m - 2)(lambda: act(self.shifted(0)))

    def start(self):
        at = self.at
        self.shift_copies(lambda c: c.start())
        self.pair_copies(lambda c: c.start())
        for layer in range(at.m):
            self.load(layer).start()
        if at.balanced:
            self.load_aside().start()

    def extra(self):
        at = self.at
        if not at.balanced:
            return
        self.load_aside().wait()
        half, landed = self.rows // 2, self.shifted_in.at[0]

        @pl.when(at.end)
        def _():
            self.shifted(0).wait_recv()
            self.to_stage(landed, 0).start()
            self.to_stage(landed, 0).wait()
            add_rows(self.aside.at[0], self.stage.at[0], 0, self.rows)
            self.sum_to_pair().start()

        @pl.when(at.next)
        def _():
            self.shifted(0, 1).wait_recv()
            self.to_stage(landed, 0, half, half).start()
            self.to_stage(landed, 0, half, half).wait()
            add_rows(self.aside.at[0], self.stage.at[0], half, half)
            self.half_to_pair(at.o, 1, self.aside.at[0]).start()

    def wait_pair(self, layer):
        at = self.at
        if not at.balanced:
            self.to_pair(layer).wait_recv()
            return
        partner, own = layer == at.partner, layer == at.o
        parted = (partner & at.end) | (own & at.next)
        pl.when(jnp.logical_not((partner & (at.end | at.next)) | (own & at.next)))(
            lambda: self.to_pair(layer).wait_recv()
        )
        pl.when(parted)(lambda: self.half_to_pair(layer, 0, self.aside.at[0]).wait_recv())
        pl.when(own & at.next)(lambda: self.half_to_pair(layer, 1, self.aside.at[0]).wait_recv())

    def step(self, d):
        at = self.at
        for way in (0, 1):
            layer = at.o + d if way == 0 else at.o - d
            there = layer < at.m if way == 0 else layer >= 0
            behind = at.has_left if way == 0 else at.has_right

            @pl.when(there)
            def _(layer=layer, behind=behind, way=way):
                mine, paired, half = self.mine.at[layer], self.from_pair.at[layer], self.rows // 2
                self.load(layer).wait()
                self.wait_pair(layer)
                partner = (layer == at.partner) & at.balanced
                whole = jnp.logical_not(partner & (at.end | at.next))
                halved = partner & at.end
                pl.when(whole)(lambda: self.to_stage(paired, 0).start())
                pl.when(halved)(lambda: self.to_stage(paired, 0, 0, half).start())

                @pl.when(behind)
                def _():
                    self.wait_line(layer)
                    self.to_stage(self.from_line.at[layer], 1).start()

                @pl.when(whole)
                def _():
                    self.to_stage(paired, 0).wait()
                    add_rows(mine, self.stage.at[0], 0, self.rows)

                @pl.when(halved)
                def _():
                    self.to_stage(paired, 0, 0, half).wait()
                    add_rows(mine, self.stage.at[0], 0, half)

                @pl.when(behind)
                def _():
                    self.to_stage(self.from_line.at[layer], 1).wait()
                    add_rows(mine, self.stage.at[1], 0, self.rows)

                self.along(layer, way).start()

    def final(self):
        at = self.at
        mine = self.mine.at[at.o]
        self.load(at.o).wait()
        self.wait_pair(at.o)
        self.to_stage(self.from_pair.at[at.o], 0).start()

        @pl.when(at.has_left)
        def _():
            self.wait_line(at.o)
            self.to_stage(self.from_line.at[at.o], 1).start()

        self.to_stage(self.from_pair.at[at.o], 0).wait()
        add_rows(mine, self.stage.at[0], 0, self.rows)

        @pl.when(at.has_right)
        def _():
            self.wait_line(at.m)
            self.to_stage(self.from_line.at[at.m], 0).start()

        @pl.when(at.has_left)
        def _():
            self.to_stage(self.from_line.at[at.o], 1).wait()
            add_rows(mine, self.stage.at[1], 0, self.rows)

        @pl.when(at.has_right)
        def _():
            self.to_stage(self.from_line.at[at.m], 0).wait()
            add_rows(mine, self.stage.at[0], 0, self.rows)

        self.store().start()

    def drain(self):
        at = self.at
        self.pair_copies(lambda c: c.wait_send())
        if at.balanced:
            pl.when(at.end)(lambda: self.sum_to_pair().wait_send())
            pl.when(at.next)(lambda: self.half_to_pair(at.o, 1, self.aside.at[0]).wait_send())
        self.shift_copies(lambda c: c.wait_send())
        for d in range(1, at.m):
            pl.when(at.o + d < at.m)(lambda: self.along(at.o + d, 0).wait_send())
            pl.when(at.o - d >= 0)(lambda: self.along(at.o - d, 1).wait_send())
        self.store().wait()


def fetch(src, dst, sem):
    return pltpu.make_async_copy(src, dst, sem)


def dot(a, b, dims=((1,), (0,))):
    return lax.dot_general(a, b, (dims, ((), ())), preferred_element_type=jnp.float32)


ROWS, COLS, BOTH = ((1,), (0,)), ((1,), (1,)), ((0,), (0,))


def row_start(lengths, position):
    at, start = jnp.int32(0), jnp.zeros_like(position)
    for k in range(lengths.shape[0]):
        start = jnp.maximum(start, jnp.where(at <= position, at, 0))
        at = at + lengths[k]
    return start


def lanes(shape):
    return lax.broadcasted_iota(jnp.int32, shape, len(shape) - 1)


def feature_maps(width):
    count = FEAT + 1 + FEAT * (FEAT + 1) // 2
    wide = -(-count // 128) * 128
    first, second = np.zeros((width, wide), np.float32), np.zeros((width, wide), np.float32)
    plus = np.zeros((3, wide), np.float32)
    plus[:, 0] = 1.0
    heads = np.arange(width // FEAT) * FEAT
    for i in range(FEAT):
        first[heads + i, 1 + i] = 1.0
        plus[1:, 1 + i] = 1.0, 0.25
    at = 1 + FEAT
    for i in range(FEAT):
        for j in range(i, FEAT):
            first[heads + i, at] = 1.0
            second[heads + j, at] = 1.0
            plus[2, at] = 1 / 32 if i == j else 1 / 16
            at += 1
    tall = -(-count // 16) * 16
    return (
        jnp.asarray(np.stack([first, second]), jnp.bfloat16),
        jnp.asarray(np.stack([first.T, second.T])[:, :tall], jnp.bfloat16),
        jnp.asarray(np.repeat(plus[:, None], 8, 1)),
        jnp.asarray(np.repeat(plus[:, :tall, None], 128, 2)),
    )


class Team:
    def __init__(self, at, rows):
        self.at, self.half, self.quarter = at, rows // 2, rows // 4
        t = at.t
        low, high = lax.rem(t, 2), t // 2
        self.near, self.far = (at.s, t + 1 - 2 * low), (at.s, lax.rem(t + 2, 4))
        self.half_at, self.other_half_at = low * self.half, (1 - low) * self.half
        self.quarter_at = self.half_at + high * self.quarter
        self.other_quarter_at = self.half_at + (1 - high) * self.quarter
        self.in_half, self.other_in_half = high * self.quarter, (1 - high) * self.quarter
        self.near_quarter_at = self.other_half_at + high * self.quarter
        self.near_other_at = self.other_half_at + (1 - high) * self.quarter


class Sum:
    pieces = 4

    def __init__(self, team, part, from_near, from_far, sems):
        self.team, self.part, self.from_near, self.from_far = team, part, from_near, from_far
        self.near_send, self.near_recv, self.far_send, self.far_recv = sems
        self.wide = part.shape[1] // self.pieces

    @staticmethod
    def scratch(rows, columns):
        return [
            pltpu.VMEM((rows // 2, columns), jnp.bfloat16),
            pltpu.VMEM((rows // 4, columns), jnp.bfloat16),
        ] + [pltpu.SemaphoreType.DMA((Sum.pieces,))] * 4

    def near(self, j):
        team, columns = self.team, pl.ds(j * self.wide, self.wide)
        return remote(
            self.part.at[pl.ds(pl.multiple_of(team.other_half_at, team.half), team.half), columns],
            self.from_near.at[:, columns],
            self.near_send.at[j],
            self.near_recv.at[j],
            team.near,
        )

    def far(self, j):
        team, columns = self.team, pl.ds(j * self.wide, self.wide)
        at = pl.multiple_of(team.other_quarter_at, team.quarter)
        return remote(
            self.part.at[pl.ds(at, team.quarter), columns],
            self.from_far.at[:, columns],
            self.far_send.at[j],
            self.far_recv.at[j],
            team.far,
        )

    def fold(self, j):
        team, columns = self.team, pl.ds(j * self.wide, self.wide)
        self.near(j).wait_recv()
        step = 64

        @pl.loop(0, team.quarter // step)
        def _(r):
            to = pl.ds(pl.multiple_of(team.other_quarter_at + r * step, step), step)
            of = pl.ds(pl.multiple_of(team.other_in_half + r * step, step), step)
            both = self.part[to, columns].astype(jnp.float32)
            both = both + self.from_near[of, columns].astype(jnp.float32)
            self.part[to, columns] = both.astype(jnp.bfloat16)

        self.far(j).start()

    def arrive(self):
        for j in range(self.pieces):
            self.far(j).wait_recv()

    def rows(self, start, count):
        team = self.team
        a = self.part[pl.ds(pl.multiple_of(team.quarter_at + start, 16), count), :]
        b = self.from_near[pl.ds(pl.multiple_of(team.in_half + start, 16), count), :]
        c = self.from_far[pl.ds(pl.multiple_of(start, 16), count), :]
        return a.astype(jnp.float32) + b.astype(jnp.float32) + c.astype(jnp.float32)

    def drain(self):
        for j in range(self.pieces):
            self.near(j).wait_send()
            self.far(j).wait_send()


class Spread:
    pieces = 4

    def __init__(self, team, whole, sems):
        self.team, self.whole = team, whole
        self.far_send, self.far_recv, self.near_send, self.near_recv, self.on_send, self.on_recv = (
            sems
        )
        self.tall = team.quarter // self.pieces

    @staticmethod
    def scratch():
        return [pltpu.SemaphoreType.DMA((Spread.pieces,))] * 6

    def copy(self, start, j, send, recv, device):
        rows = self.whole.at[pl.ds(pl.multiple_of(start + j * self.tall, self.tall), self.tall)]
        return remote(rows, rows, send.at[j], recv.at[j], device)

    def far(self, j):
        team = self.team
        return self.copy(team.quarter_at, j, self.far_send, self.far_recv, team.far)

    def near(self, j):
        team = self.team
        return self.copy(team.quarter_at, j, self.near_send, self.near_recv, team.near)

    def on(self, j):
        team = self.team
        return self.copy(team.other_quarter_at, j, self.on_send, self.on_recv, team.near)

    def send(self, j):
        self.far(j).start()
        self.near(j).start()

    def pass_on(self, j):
        self.far(j).wait_recv()
        self.on(j).start()

    def arrive(self):
        for j in range(self.pieces):
            self.near(j).wait_recv()
            self.on(j).wait_recv()

    def drain(self):
        for j in range(self.pieces):
            self.far(j).wait_send()
            self.near(j).wait_send()
            self.on(j).wait_send()


class Pump:
    def __init__(self, events):
        self.events = list(events)

    def __call__(self, count):
        for _ in range(min(count, len(self.events))):
            self.events.pop(0)()

    def until(self, event):
        while event in self.events:
            self.events.pop(0)()

    def rest(self):
        self(len(self.events))


def gain_row(gains, which, row):
    n, depth = gains.shape[0], gains.shape[2] // 2
    for s in range(n):
        part = gains[s, 0:8, which * depth : (which + 1) * depth]
        row[:, s * depth : (s + 1) * depth] = part


def scores(query, key, mask):
    s = dot(query, key, COLS) * 0.25
    return 1.0 + s, jnp.where(mask, 1.0 + s + 0.5 * s * s, 0.0)


def pair_mask(row_starts, column_starts, first_row, first_column):
    shape = (row_starts.shape[0], column_starts.shape[1])
    rows = lax.broadcasted_iota(jnp.int32, shape, 0) + first_row
    columns = lax.broadcasted_iota(jnp.int32, shape, 1) + first_column
    return (row_starts == column_starts) & (columns <= rows)


def of_head(values, h):
    lane = lanes((1, values.shape[1]))
    mine = (lane >= h * FEAT) & (lane < (h + 1) * FEAT)
    return jnp.where(mine, values, jnp.zeros_like(values))


def with_ones(values):
    return jnp.concatenate([values, jnp.ones_like(values)], axis=1)


def forward_kernel(n, sizes, *refs):
    (
        lengths, stream_h, cot_h, maps, maps_t, plus, plus_t,
        gains_own, qkv_own, out_own, gate_own, up_own, down_own,
        gains_h, qkv_h, out_h, gate_h, up_h, down_h,
        h_one_h, heads_h, mixed_h, rden_h, state_h, mid_h, h_two_h, gate_v_h, up_v_h, hid_h, part_h,
        stream, h_one, heads, w_qkv, w_out, mixed, rden, numer, mid, h_two, w_ff,
        gate_v, up_v, hid, part, gains, gain,
        t_own, t_pair, t_line, t_next, state, t_send, t_recv, local, part_sem,
        *sems,
    ) = refs
    rows, width = stream.shape
    heads_here = mixed.shape[1] // 128
    q_wide = heads_here * FEAT
    at = Place(n)
    team = Team(at, rows)
    near_sum, sems = sems[:6], sems[6:]
    spread_sems, sems = sems[:6], sems[6:]
    shards = (gains_own, qkv_own, out_own, gate_own, up_own, down_own)
    wholes = (gains_h, qkv_h, out_h, gate_h, up_h, down_h)
    groups = [
        Gather(at, shards[g], wholes[g], sems[4 * g : 4 * g + 4]) for g in range(len(shards))
    ]
    g_gains, g_qkv, g_out, g_gate, g_up, g_down = groups
    at.greet((team.near, team.far))
    pump = Pump(gather_events(groups))
    cell = iter(range(local.shape[0]))
    copies = []

    def load(src, dst):
        copy = fetch(src, dst, local.at[next(cell)])
        copy.start()
        return copy

    def save(src, dst):
        copies.append(load(src, dst))

    get_stream = load(stream_h, stream)
    pump.until(g_gains.extra)
    g_gains.arrive()
    load(gains_h, gains).wait()
    gain_row(gains, 0, gain.at[0])
    gain_row(gains, 1, gain.at[1])
    get_stream.wait()

    @pl.loop(0, rows // 64)
    def _(j):
        here = pl.ds(pl.multiple_of(j * 64, 64), 64)
        x = stream[here, :].astype(jnp.float32)
        scale = lax.rsqrt(jnp.mean(x * x, axis=1, keepdims=True) + EPSILON)
        h_one[here, :] = (x * scale * gain[0, 0:1, :]).astype(jnp.bfloat16)

    save(h_one, h_one_h)
    pump.until(g_qkv.extra)
    g_qkv.arrive()
    load(qkv_h, w_qkv).wait()

    @pl.loop(0, rows // 256)
    def _(j):
        here = pl.ds(pl.multiple_of(j * 256, 256), 256)
        heads[here, :] = dot(h_one[here, :], w_qkv[...]).astype(jnp.bfloat16)

    save(heads, heads_h)
    pump(1)
    first = at.s * rows
    starts_col = row_start(lengths, first + lax.broadcasted_iota(jnp.int32, (rows, 1), 0))
    starts_row = row_start(lengths, first + lax.broadcasted_iota(jnp.int32, (1, rows), 1))
    last = row_start(lengths, first + rows - 1)
    keep = jnp.where(starts_row == last, 1.0, 0.0)
    tall = t_own.shape[1]

    def values_of(h):
        return pl.ds(pl.multiple_of(2 * q_wide + h * 128, 128), 128)

    t_sum = numer.at[0, 0:tall, 0:128]
    t_sum[...] = jnp.zeros((tall, 128), jnp.float32)

    @pl.loop(0, heads_here)
    def _(h):
        key = of_head(heads[:, q_wide : 2 * q_wide], h)
        one = dot(maps_t[0], key, COLS) + plus_t[0][:, 0:1]
        two = dot(maps_t[1], key, COLS) + plus_t[1][:, 0:1]
        phi = (one * two * keep).astype(jnp.bfloat16)
        total = dot(phi, with_ones(heads[:, values_of(h)]))
        t_own[h] = total[:, :128].astype(jnp.bfloat16)
        t_sum[...] += jnp.where(lanes((tall, 128)) == h, total[:, 128:], 0.0)

    t_own[heads_here] = t_sum[...].astype(jnp.bfloat16)
    to_pair = remote(t_own, t_pair, t_send.at[0], t_recv.at[0], at.pair)
    to_right = remote(t_next, t_line, t_send.at[1], t_recv.at[1], at.right)
    to_pair.start()
    pump(1)
    tile = 256

    @pl.loop(0, heads_here)
    def _(h):
        key = heads[:, q_wide : 2 * q_wide]
        for j in range(rows // tile):
            upto = (j + 1) * tile
            query = of_head(heads[j * tile : upto, 0:q_wide], h)
            mask = pair_mask(starts_col[j * tile : upto], starts_row[:, :upto], j * tile, 0)
            _, weights = scores(query, key[:upto], mask)
            values = with_ones(heads[0:upto, values_of(h)])
            numer[h, j * tile : upto, :] = dot(weights.astype(jnp.bfloat16), values)

    pump(1)

    def closed(s):
        return jnp.where(row_start(lengths, (s + 1) * rows - 1) >= s * rows, 0.0, 1.0)

    on_one, on_two = closed(at.o * 2), closed(at.o * 2 + 1)

    @pl.when(at.o == 0)
    def _():
        t_line[...] = jnp.zeros_like(t_line)

    to_pair.wait_recv()
    pl.when(at.has_left)(lambda: to_right.wait_recv())
    for h in range(heads_here + 1):
        mine, other = t_own[h].astype(jnp.float32), t_pair[h].astype(jnp.float32)
        t_one, t_two = jnp.where(at.i == 0, mine, other), jnp.where(at.i == 0, other, mine)
        come = t_line[h].astype(jnp.float32)
        middle = t_one + on_one * come
        t_next[h] = (t_two + on_two * middle).astype(jnp.bfloat16)
        state[h] = jnp.where(at.i == 0, come, middle).astype(jnp.bfloat16)
    pl.when(at.has_right)(lambda: to_right.start())
    save(state, state_h)
    pump(1)

    @pl.loop(0, heads_here)
    def _(h):
        own = lanes((tall, 128)) == h
        dens = jnp.sum(jnp.where(own, state[heads_here].astype(jnp.float32), 0.0), 1, keepdims=True)
        dens = jnp.broadcast_to(dens, (tall, 128)).astype(jnp.bfloat16)
        table = jnp.concatenate([state[h], dens], axis=1)
        table = jnp.concatenate(
            [table, jnp.zeros((maps.shape[2] - tall, 256), jnp.bfloat16)], axis=0
        )
        for j in range(rows // tile):
            here = slice(j * tile, (j + 1) * tile)
            query = of_head(heads[here, 0:q_wide], h)
            one = dot(query, maps[0]) + plus[0, 0:1, :]
            two = dot(query, maps[1]) + plus[1, 0:1, :]
            carried = jnp.where(starts_col[here] < first, 1.0, 0.0)
            phi = (one * two * plus[2, 0:1, :] * carried).astype(jnp.bfloat16)
            total = numer[h, here, :] + dot(phi, table)
            inverse = 1.0 / total[:, 128:]
            rden[h, here, :] = inverse
            mixed[here, pl.ds(pl.multiple_of(h * 128, 128), 128)] = (
                total[:, :128] * inverse
            ).astype(jnp.bfloat16)

    save(mixed, mixed_h)
    save(rden, rden_h)
    pump.until(g_out.extra)
    g_out.arrive()
    load(out_h, w_out).wait()
    for copy in copies:
        copy.wait()
    copies.clear()

    part_sum = Sum(team, h_one, *near_sum[:2], near_sum[2:])
    for j in range(Sum.pieces):
        columns = slice(j * part_sum.wide, (j + 1) * part_sum.wide)

        @pl.loop(0, rows // 256)
        def _(r):
            here = pl.ds(pl.multiple_of(r * 256, 256), 256)
            h_one[here, columns] = dot(mixed[here, :], w_out[columns, :], COLS).astype(jnp.bfloat16)

        part_sum.near(j).start()
        if j:
            part_sum.fold(j - 1)
            pump(1)
    part_sum.fold(Sum.pieces - 1)
    pump(1)
    part_sum.arrive()
    spread = Spread(team, h_two, spread_sems)
    for j in range(Spread.pieces):
        for k in range(spread.tall // 32):
            down = j * spread.tall + k * 32
            here = pl.ds(pl.multiple_of(team.quarter_at + down, 32), 32)
            x = part_sum.rows(down, 32) + stream[here, :].astype(jnp.float32)
            mid[down : down + 32, :] = x
            scale = lax.rsqrt(jnp.mean(x * x, axis=1, keepdims=True) + EPSILON)
            h_two[here, :] = (x * scale * gain[1, 0:1, :]).astype(jnp.bfloat16)
        spread.send(j)
    save(mid, mid_h)
    for j in range(Spread.pieces):
        pump(1)
        spread.pass_on(j)
    get_cot = load(cot_h, stream)
    spread.arrive()
    part_sum.drain()
    spread.drain()
    save(h_two, h_two_h)
    pump.until(g_gate.extra)
    g_gate.arrive()
    get_gate = load(gate_h, w_ff.at[0])
    pump.until(g_up.extra)
    g_up.arrive()
    load(up_h, w_ff.at[1]).wait()
    get_gate.wait()
    stages = 4
    for stage in range(stages):

        @pl.loop(0, rows // 128 // stages)
        def _(r):
            start = pl.multiple_of((stage * (rows // 128 // stages) + r) * 128, 128)
            here = pl.ds(start, 128)
            gate = dot(h_two[here, :], w_ff[0])
            up = dot(h_two[here, :], w_ff[1])
            hidden = gate * jax.nn.sigmoid(gate) * up
            gate_v[here, :] = gate.astype(jnp.bfloat16)
            up_v[here, :] = up.astype(jnp.bfloat16)
            hid[here, :] = hidden.astype(jnp.bfloat16)

        pump(1)
    save(gate_v, gate_v_h)
    save(up_v, up_v_h)
    save(hid, hid_h)
    get_cot.wait()
    deep = part.shape[1]
    for s in range(n):
        if s > 1:
            fetch(part.at[s % 2], part_h.at[s - 2], part_sem.at[s % 2]).wait()
        columns = stream[:, s * deep : (s + 1) * deep]
        for low in range(0, hid.shape[1], 512):
            high = min(hid.shape[1], low + 512)
            part[s % 2, :, low:high] = dot(columns, hid[:, low:high], BOTH).astype(jnp.bfloat16)
        fetch(part.at[s % 2], part_h.at[s], part_sem.at[s % 2]).start()
        if s % max(1, n // 4) == 0:
            pump(1)
    for s in range(n - 2, n):
        fetch(part.at[s % 2], part_h.at[s], part_sem.at[s % 2]).wait()
    pump.rest()
    g_down.arrive()
    for group in groups:
        group.drain()
    to_pair.wait_send()
    pl.when(at.has_right)(lambda: to_right.wait_send())
    for copy in copies:
        copy.wait()


def forward(n, lengths, stream, cot, maps, shards):
    rows, width = stream.shape
    gains, qkv, out, gate, up, down = shards
    hidden = gate.shape[1]
    values = out.shape[1]
    heads_here = values // 128
    tall = maps[1].shape[1]
    bf, f32 = jnp.bfloat16, jnp.float32
    shape = jax.ShapeDtypeStruct
    wholes = [
        shape((n,) + gains.shape, f32),
        shape((n * qkv.shape[0], qkv.shape[1]), bf),
        shape((width, values), bf),
        shape((width, hidden), bf),
        shape((width, hidden), bf),
        shape((width, hidden), bf),
    ]
    kept = [
        shape((rows, width), bf),
        shape((rows, qkv.shape[1]), bf),
        shape((rows, values), bf),
        shape((heads_here, rows, 128), f32),
        shape((heads_here + 1, tall, 128), bf),
        shape((rows // 4, width), f32),
        shape((rows, width), bf),
        shape((rows, hidden), bf),
        shape((rows, hidden), bf),
        shape((rows, hidden), bf),
        shape((n,) + down.shape, bf),
    ]
    state = (heads_here + 1, tall, 128)
    scratch = [
        pltpu.VMEM((rows, width), bf),
        pltpu.VMEM((rows, width), bf),
        pltpu.VMEM((rows, qkv.shape[1]), bf),
        pltpu.VMEM((width, qkv.shape[1]), bf),
        pltpu.VMEM((width, values), bf),
        pltpu.VMEM((rows, values), bf),
        pltpu.VMEM((heads_here, rows, 128), f32),
        pltpu.VMEM((heads_here, rows, 256), f32),
        pltpu.VMEM((rows // 4, width), f32),
        pltpu.VMEM((rows, width), bf),
        pltpu.VMEM((2, width, hidden), bf),
        pltpu.VMEM((rows, hidden), bf),
        pltpu.VMEM((rows, hidden), bf),
        pltpu.VMEM((rows, hidden), bf),
        pltpu.VMEM((2,) + down.shape, bf),
        pltpu.VMEM((n,) + gains.shape, f32),
        pltpu.VMEM((2, 8, width), f32),
        pltpu.VMEM(state, bf),
        pltpu.VMEM(state, bf),
        pltpu.VMEM(state, bf),
        pltpu.VMEM(state, bf),
        pltpu.VMEM(state, bf),
        pltpu.SemaphoreType.DMA((2,)),
        pltpu.SemaphoreType.DMA((2,)),
        pltpu.SemaphoreType.DMA((24,)),
        pltpu.SemaphoreType.DMA((2,)),
    ]
    scratch += Sum.scratch(rows, width) + Spread.scratch() + Gather.scratch(n) * len(shards)
    anywhere, inside = pl.BlockSpec(memory_space=pl.ANY), pl.BlockSpec(memory_space=pltpu.VMEM)
    result = pl.pallas_call(
        functools.partial(forward_kernel, n, None),
        out_shape=wholes + kept,
        in_specs=[pl.BlockSpec(memory_space=pltpu.SMEM), anywhere, anywhere]
        + [inside] * 4
        + [anywhere] * 6,
        out_specs=[anywhere] * (len(wholes) + len(kept)),
        scratch_shapes=scratch,
        compiler_params=pltpu.CompilerParams(
            collective_id=0, has_side_effects=True, vmem_limit_bytes=62 * MIB
        ),
    )(lengths, stream, cot, *maps, *shards)
    return result[: len(wholes)], result[len(wholes) :]


class SpreadOut(Spread):
    def __init__(self, team, quarter, whole, sems):
        super().__init__(team, whole, sems[:-1])
        self.own, self.kept = quarter, sems[-1]

    @staticmethod
    def scratch():
        return Spread.scratch() + [pltpu.SemaphoreType.DMA((1,))]

    def own_copy(self, j, send, recv, device):
        start = self.team.quarter_at + j * self.tall
        rows = self.whole.at[pl.ds(pl.multiple_of(start, self.tall), self.tall)]
        src = self.own.at[pl.ds(j * self.tall, self.tall)]
        return remote(src, rows, send.at[j], recv.at[j], device)

    def far(self, j):
        return self.own_copy(j, self.far_send, self.far_recv, self.team.far)

    def near(self, j):
        return self.own_copy(j, self.near_send, self.near_recv, self.team.near)

    def keep(self):
        team = self.team
        rows = self.whole.at[pl.ds(pl.multiple_of(team.quarter_at, team.quarter), team.quarter)]
        return pltpu.make_async_copy(self.own, rows, self.kept.at[0])


def backward_kernel(n, *refs):
    (
        lengths, maps, maps_t, plus, plus_t,
        stream_h, cot_h, gains_h, qkv_h, out_h, gate_h, up_h, down_h,
        h_one_h, heads_h, mixed_h, rden_h, state_h, mid_h, h_two_h, gate_v_h, up_v_h, hid_h, part_h,
        *refs,
    ) = refs
    act_h, ig_h, *refs = refs
    outs, refs = refs[:6], refs[6:]
    parts, refs = [part_h] + refs[:5], refs[5:]
    landings, refs = refs[:18], refs[18:]
    (
        part, arena, d_mid, dm, gains, gain, gain_sum, gain_near, gain_far, gain_parts,
        t_own, t_pair, t_line, t_next, state, back, t_send, t_recv, gain_send, gain_recv, local,
        stage_g, stage_o, stage_q, stage_n,
        *sems,
    ) = refs
    rows, width = arena.shape
    hidden = gate_v_h.shape[1]
    values_wide = mixed_h.shape[1]
    heads_here = values_wide // 128
    q_wide = heads_here * FEAT
    at = Place(n)
    team = Team(at, rows)

    def take(count):
        nonlocal sems
        taken, sems = sems[:count], sems[count:]
        return taken

    sums = [take(6) for _ in range(2)]
    first_sems = take(4)
    dm_sems, act_sems, ig_sems = take(6), take(7), take(7)
    stages = (stage_g, stage_g, stage_g, stage_o, stage_q, stage_n)
    groups = []
    for g in range(6):
        mine, aside, *own_sems = take(9)
        groups.append(
            Scatter(
                at,
                parts[g],
                outs[g],
                landings[3 * g : 3 * g + 3],
                (mine, aside, stages[g]),
                own_sems,
            )
        )
    s_down, s_gate, s_up, s_out, s_qkv, s_gains = groups
    at.greet((team.near, team.far))
    cell = iter(range(local.shape[0]))

    def load(src, dst):
        copy = fetch(src, dst, local.at[next(cell)])
        copy.start()
        return copy

    pump = Pump([])
    begun = []

    def begin(group):
        group.start()
        last = begun[-1] if begun else None
        begun.append(group)
        for d in range(at.m - 1, 0, -1):
            pump.events.append(functools.partial(group.step, d))
            if d == max(1, at.m - 2) and last is not None:
                pump.events.append(last.final)
        pump.events.append(group.extra)

    begin(s_down)
    get_gains = load(gains_h, gains)
    get_mid = load(mid_h, d_mid)
    part_sum = Sum(team, part, *sums[0][:2], sums[0][2:])
    feed_sum = Sum(team, part, *sums[1][:2], sums[1][2:])
    first_sum = Sum(team, part, *sums[0][:2], first_sems)
    spread = Spread(team, dm, dm_sems)
    ig_rows, act_rows = team.quarter, 2 * team.quarter
    ig_spread = SpreadOut(team, arena.at[pl.ds(ig_rows, team.quarter)], ig_h, ig_sems)
    act_spread = SpreadOut(team, arena.at[pl.ds(act_rows, team.quarter)], act_h, act_sems)
    piece = part_sum.wide

    def staged(count, sem, tile, parts_h, compute, between):
        for s in range(count):
            if s > 1:
                fetch(tile.at[s % 2], parts_h.at[s - 2], sem.at[s % 2]).wait()
            compute(s, tile.at[s % 2])
            fetch(tile.at[s % 2], parts_h.at[s], sem.at[s % 2]).start()
            between(s)
        for s in range(count - 2, count):
            fetch(tile.at[s % 2], parts_h.at[s], sem.at[s % 2]).wait()

    def now_and_then(s):
        if s % max(1, n // 4) == n // 4 - 1:
            pump(1)

    def norm_back(x, grad, gain_ref, which):
        scale = lax.rsqrt(jnp.mean(x * x, axis=1, keepdims=True) + EPSILON)
        unit = x * scale
        total = jnp.sum((grad * unit).reshape(-1, 8, width), axis=0)
        gain_sum[8 * which : 8 * which + 8, :] += total
        scaled = grad * gain_ref[0:1, :]
        return scale * (scaled - unit * jnp.mean(scaled * unit, axis=1, keepdims=True))

    gain_sum[...] = jnp.zeros_like(gain_sum)

    def feed_forward(w_down, w_ff, ff, w_sem, tile_sem):
        get_cot, get_down = load(cot_h, arena), load(down_h, w_down)
        get_gate, get_up = load(gate_v_h, ff.at[0]), load(up_v_h, ff.at[1])
        tall = w_ff.shape[2]

        def weights(j, which):
            here = pl.ds(j * tall, tall)
            return fetch(
                (gate_h, up_h)[which].at[here], w_ff.at[j % 2, which], w_sem.at[j % 2, which]
            )

        for which in (0, 1):
            weights(0, which).start()
        get_cot.wait()
        get_down.wait()
        get_gate.wait()
        get_up.wait()
        block = 256
        for low in range(0, hidden, 512):
            high = min(hidden, low + 512)

            @pl.loop(0, rows // block)
            def _(r):
                here = pl.ds(pl.multiple_of(r * block, block), block)
                grad = dot(arena[here, :], w_down[:, low:high])
                gate = ff[0, here, low:high].astype(jnp.float32)
                sigma = jax.nn.sigmoid(gate)
                silu = gate * sigma
                up = ff[1, here, low:high].astype(jnp.float32)
                ff[0, here, low:high] = (grad * up * (sigma + silu * (1.0 - sigma))).astype(
                    jnp.bfloat16
                )
                ff[1, here, low:high] = (grad * silu).astype(jnp.bfloat16)

            pump(1)
        get_two = load(h_two_h, arena)
        count = width // tall
        for j in range(count):
            for which in (0, 1):
                if j + 1 < count:
                    weights(j + 1, which).start()
                weights(j, which).wait()

            @pl.loop(0, rows // 256)
            def _(r):
                here = pl.ds(pl.multiple_of(r * 256, 256), 256)
                grad = dot(ff[0, here, :], w_ff[j % 2, 0], COLS)
                grad += dot(ff[1, here, :], w_ff[j % 2, 1], COLS)
                part[here, j * tall : (j + 1) * tall] = grad.astype(jnp.bfloat16)

            if (j + 1) * tall % piece == 0:
                p = (j + 1) * tall // piece - 1
                part_sum.near(p).start()
                if p:
                    part_sum.fold(p - 1)
            if j % 4 == 3:
                pump(1)
        part_sum.fold(Sum.pieces - 1)
        get_two.wait()
        pump(1)
        down = width // n
        tile = w_ff.at[0, :, 0:down]

        def grads(which):
            def compute(s, to):
                columns = arena[:, s * down : (s + 1) * down]
                for low in range(0, hidden, 512):
                    high = min(hidden, low + 512)
                    grad = dot(columns, ff[which, :, low:high], BOTH)
                    to[:, low:high] = grad.astype(jnp.bfloat16)

            return compute

        staged(n, tile_sem, tile, parts[1], grads(0), now_and_then)
        begin(s_gate)
        get_gains.wait()
        gain_row(gains, 0, gain.at[0])
        gain_row(gains, 1, gain.at[1])
        get_mid.wait()
        part_sum.arrive()
        for j in range(Spread.pieces):
            for k in range(spread.tall // 32):
                down_at = j * spread.tall + k * 32
                here = pl.ds(pl.multiple_of(team.quarter_at + down_at, 32), 32)
                x = d_mid[down_at : down_at + 32, :]
                grad = norm_back(x, part_sum.rows(down_at, 32), gain.at[1], 1)
                d_mid[down_at : down_at + 32, :] = grad
        quarter = pl.ds(pl.multiple_of(team.quarter_at, team.quarter), team.quarter)
        get = load(cot_h.at[quarter], dm.at[quarter])
        get.wait()
        for j in range(Spread.pieces):
            for k in range(spread.tall // 32):
                down_at = j * spread.tall + k * 32
                here = pl.ds(pl.multiple_of(team.quarter_at + down_at, 32), 32)
                grad = d_mid[down_at : down_at + 32, :]
                grad = grad + dm[here, :].astype(jnp.float32)
                d_mid[down_at : down_at + 32, :] = grad
                dm[here, :] = grad.astype(jnp.bfloat16)
            spread.send(j)
        part_sum.drain()
        staged(n, tile_sem, tile, parts[2], grads(1), now_and_then)
        begin(s_up)
        get_hid = load(hid_h, ff.at[0])
        get_hid.wait()
        for j in range(Sum.pieces):
            columns = slice(j * piece, (j + 1) * piece)

            @pl.loop(0, rows // 256)
            def _(r):
                here = pl.ds(pl.multiple_of(r * 256, 256), 256)
                feed = dot(ff[0, here, :], w_down[columns, :], COLS)
                part[here, columns] = feed.astype(jnp.bfloat16)

            feed_sum.near(j).start()
            spread.pass_on(j)

    pl.run_scoped(
        feed_forward,
        pltpu.VMEM(down_h.shape, jnp.bfloat16),
        pltpu.VMEM((2, 2, 256, hidden), jnp.bfloat16),
        pltpu.VMEM((2, rows, hidden), jnp.bfloat16),
        pltpu.SemaphoreType.DMA((2, 2)),
        pltpu.SemaphoreType.DMA((2,)),
    )

    def attention(
        heads, d_heads, mixed, w_out, w_qkv, delta, g, delta_row, d_query, d_key,
        dens, tile_o, tile_q, tile_sem, d_values,
    ):
        gets = [
            load(heads_h, heads),
            load(mixed_h, mixed),
            load(out_h, w_out),
            load(rden_h, delta),
            load(qkv_h, w_qkv),
            load(state_h, state),
        ]
        get_one = load(h_one_h, arena)
        for get in gets:
            get.wait()
        spread.arrive()

        @pl.loop(0, rows // 256)
        def _(r):
            here = pl.ds(pl.multiple_of(r * 256, 256), 256)
            d_values[here, :] = dot(dm[here, :], w_out[...])

        for j in range(Sum.pieces):
            feed_sum.fold(j)

        @pl.loop(0, heads_here)
        def _(h):
            across = pl.ds(pl.multiple_of(h * 128, 128), 128)
            grad = d_values[:, across] * delta[h]
            g[h] = grad.astype(jnp.bfloat16)
            sums_of = jnp.sum(grad * mixed[:, across].astype(jnp.float32), axis=1, keepdims=True)
            wide = jnp.broadcast_to(sums_of, (rows, 128))
            delta[h] = wide
            delta_row[h] = wide.T[0:8]

        pump(1)
        first = at.s * rows
        starts_col = row_start(lengths, first + lax.broadcasted_iota(jnp.int32, (rows, 1), 0))
        starts_row = row_start(lengths, first + lax.broadcasted_iota(jnp.int32, (1, rows), 1))
        last = row_start(lengths, first + rows - 1)
        tall = t_own.shape[1]
        wide = maps.shape[2]
        carried_row = jnp.where(starts_row < first, 1.0, 0.0)
        dens[1, 0:tall, 0:128] = jnp.zeros((tall, 128), jnp.float32)

        def values_of(h):
            return pl.ds(pl.multiple_of(2 * q_wide + h * 128, 128), 128)

        def head_at(h):
            return pl.ds(pl.multiple_of(h * 128, 128), 128)

        @pl.loop(0, heads_here)
        def _(h):
            query = of_head(heads[:, 0:q_wide], h)
            one = dot(maps_t[0], query, COLS) + plus_t[0][:, 0:1]
            two = dot(maps_t[1], query, COLS) + plus_t[1][:, 0:1]
            phi = one * two * plus_t[2][:, 0:1] * carried_row
            t_own[h] = dot(phi.astype(jnp.bfloat16), g[h]).astype(jnp.bfloat16)
            below = -jnp.sum(phi * delta_row[h][0:1, :], axis=1, keepdims=True)
            dens[1, 0:tall, 0:128] += jnp.where(lanes((tall, 128)) == h, below, 0.0)

        t_own[heads_here] = dens[1, 0:tall, 0:128].astype(jnp.bfloat16)
        to_pair = remote(t_own, t_pair, t_send.at[0], t_recv.at[0], at.pair)
        to_left = remote(t_next, t_line, t_send.at[1], t_recv.at[1], at.left)
        to_pair.start()
        pump(1)

        d_query[...] = jnp.zeros_like(d_query)
        tile = 128

        def intra(h):
            key, query = of_head(heads[:, q_wide : 2 * q_wide], h), of_head(heads[:, 0:q_wide], h)
            across = values_of(h)
            for j in range(rows // tile):
                here, upto = slice(j * tile, (j + 1) * tile), (j + 1) * tile
                mask = pair_mask(starts_col[here], starts_row[:, :upto], j * tile, 0)
                more, _ = scores(query[here], key[:upto], mask)
                d_weight = dot(g[h, here, :], heads[0:upto, across], COLS) - delta[h, here, 0:1]
                d_score = jnp.where(mask, d_weight * more, 0.0).astype(jnp.bfloat16)
                d_query[here, :] += dot(d_score, key[:upto]) * 0.25
            for j in range(rows // tile):
                here, after = slice(j * tile, (j + 1) * tile), j * tile
                shape = (tile, rows - after)
                key_at = lax.broadcasted_iota(jnp.int32, shape, 0)
                query_at = lax.broadcasted_iota(jnp.int32, shape, 1)
                mask = (starts_col[here] == starts_row[:, after:]) & (key_at <= query_at)
                more, weight = scores(key[here], query[after:], mask)
                d_weight = dot(heads[here, across], g[h, after:, :], COLS)
                d_weight = d_weight - delta_row[h, 0:1, after:]
                d_score = jnp.where(mask, d_weight * more, 0.0).astype(jnp.bfloat16)
                d_values[here, head_at(h)] = dot(weight.astype(jnp.bfloat16), g[h, after:, :])
                grad = dot(d_score, query[after:]) * 0.25
                d_key[here, :] = jnp.where(h == 0, grad, d_key[here, :] + grad)

        d_key[...] = jnp.zeros_like(d_key)
        per = max(1, heads_here // 2)
        for part_of in range(0, heads_here, per):

            @pl.loop(part_of, part_of + per)
            def _(h):
                intra(h)

            pump(1)

        def closed(s):
            return jnp.where(row_start(lengths, (s + 1) * rows - 1) >= s * rows, 0.0, 1.0)

        on_one, on_two = closed(at.o * 2), closed(at.o * 2 + 1)

        @pl.when(at.o == at.m - 1)
        def _():
            t_line[...] = jnp.zeros_like(t_line)

        to_pair.wait_recv()
        pl.when(at.has_right)(lambda: to_left.wait_recv())
        for h in range(heads_here + 1):
            mine, other = t_own[h].astype(jnp.float32), t_pair[h].astype(jnp.float32)
            t_one, t_two = jnp.where(at.i == 0, mine, other), jnp.where(at.i == 0, other, mine)
            come = t_line[h].astype(jnp.float32)
            middle = t_two + on_two * come
            t_next[h] = (t_one + on_one * middle).astype(jnp.bfloat16)
            back[h] = jnp.where(at.i == 0, middle, come).astype(jnp.bfloat16)
        pl.when(at.has_left)(lambda: to_left.start())
        pump(1)

        dens[0] = jnp.zeros_like(dens[0])
        dens[1] = jnp.zeros_like(dens[1])
        dens[0, 0:128, 0:tall] = state[heads_here].astype(jnp.float32).T
        dens[1, 0:128, 0:tall] = back[heads_here].astype(jnp.float32).T
        filler = jnp.zeros((wide - tall, 128), jnp.bfloat16)

        def through(u, h, grad):
            one = dot(u, maps[0]) + plus[0, 0:1, :]
            two = dot(u, maps[1]) + plus[1, 0:1, :]
            grad = grad()
            left = dot((grad * two).astype(jnp.bfloat16), maps[0], COLS)
            left += dot((grad * one).astype(jnp.bfloat16), maps[1], COLS)
            return one * two, of_head(left, h)

        for j in range(rows // tile):
            here = slice(j * tile, (j + 1) * tile)
            carried = jnp.where(starts_col[here] < first, 1.0, 0.0)
            keep = jnp.where(starts_col[here] == last, 1.0, 0.0)

            @pl.loop(0, heads_here)
            def _(h):
                table = jnp.concatenate([state[h], filler], axis=0)
                below = dens[0, pl.ds(h, 1), :]

                def grad_query():
                    grad = dot(g[h, here, :], table, COLS) - delta[h, here, 0:1] * below
                    return grad * plus[2, 0:1, :] * carried

                _, grad = through(of_head(heads[here, 0:q_wide], h), h, grad_query)
                d_query[here, :] += grad
                table_back = jnp.concatenate([back[h], filler], axis=0)
                below_back = dens[1, pl.ds(h, 1), :]

                def grad_key():
                    return (dot(heads[here, values_of(h)], table_back, COLS) + below_back) * keep

                phi, grad = through(of_head(heads[here, q_wide : 2 * q_wide], h), h, grad_key)
                d_key[here, :] += grad
                far = dot((phi * keep).astype(jnp.bfloat16), table_back)
                d_heads[here, values_of(h)] = (d_values[here, head_at(h)] + far).astype(
                    jnp.bfloat16
                )

            d_heads[here, 0:q_wide] = d_query[here, :].astype(jnp.bfloat16)
            d_heads[here, q_wide : 2 * q_wide] = d_key[here, :].astype(jnp.bfloat16)
        pump(1)

        feed_sum.arrive()
        feed_sum.drain()
        for start in range(0, team.quarter, 32):
            feed_sum.from_far[start : start + 32, :] = feed_sum.rows(start, 32).astype(bf)
        for j in range(Sum.pieces):
            columns = slice(j * piece, (j + 1) * piece)

            @pl.loop(0, rows // 256)
            def _(r):
                here = pl.ds(pl.multiple_of(r * 256, 256), 256)
                grad = dot(d_heads[here, :], w_qkv[columns, :], COLS)
                part[here, columns] = grad.astype(jnp.bfloat16)

            first_sum.near(j).start()
            if j:
                first_sum.fold(j - 1)
        first_sum.fold(Sum.pieces - 1)

        down = width // n

        def grad_out(s, to):
            columns = dm[:, s * down : (s + 1) * down]
            to[...] = dot(columns, mixed[...], BOTH).astype(jnp.bfloat16)

        staged(n, tile_sem, tile_o, parts[3], grad_out, lambda s: None)
        begin(s_out)
        pump(1)
        get_one.wait()

        def grad_qkv(s, to):
            columns = arena[:, s * down : (s + 1) * down]
            to[...] = dot(columns, d_heads[...], BOTH).astype(jnp.bfloat16)

        staged(n, tile_sem, tile_q, parts[4], grad_qkv, lambda s: None)
        begin(s_qkv)
        to_pair.wait_send()
        pl.when(at.has_left)(lambda: to_left.wait_send())

    bf, f32 = jnp.bfloat16, jnp.float32
    pl.run_scoped(
        attention,
        pltpu.VMEM((rows, heads_h.shape[1]), bf),
        pltpu.VMEM((rows, heads_h.shape[1]), bf),
        pltpu.VMEM((rows, values_wide), bf),
        pltpu.VMEM(out_h.shape, bf),
        pltpu.VMEM(qkv_h.shape, bf),
        pltpu.VMEM((heads_here, rows, 128), f32),
        pltpu.VMEM((heads_here, rows, 128), bf),
        pltpu.VMEM((heads_here, 8, rows), f32),
        pltpu.VMEM((rows, q_wide), f32),
        pltpu.VMEM((rows, q_wide), f32),
        pltpu.VMEM((2, maps.shape[2], maps.shape[2]), f32),
        pltpu.VMEM((2, width // n, values_wide), bf),
        pltpu.VMEM((2, width // n, heads_h.shape[1]), bf),
        pltpu.SemaphoreType.DMA((2,)),
        pltpu.VMEM((rows, values_wide), f32),
    )

    quarter = pl.ds(pl.multiple_of(team.quarter_at, team.quarter), team.quarter)
    stream_q = arena.at[0 : team.quarter]
    get_stream = load(stream_h.at[quarter], stream_q)
    get_stream.wait()
    first_sum.arrive()
    for j in range(Spread.pieces):
        for k in range(ig_spread.tall // 32):
            down_at = j * ig_spread.tall + k * 32
            here = slice(down_at, down_at + 32)
            x = arena[here, :].astype(f32)
            grad = norm_back(x, first_sum.rows(down_at, 32), gain.at[0], 0)
            to = slice(ig_rows + down_at, ig_rows + down_at + 32)
            arena[to, :] = (d_mid[here, :] + grad).astype(bf)
        ig_spread.send(j)
    ig_spread.keep().start()
    gain_to_near = remote(gain_sum, gain_near, gain_send.at[0], gain_recv.at[0], team.near)
    gain_to_near.start()
    load(mid_h, d_mid).wait()
    for j in range(Spread.pieces):
        for k in range(act_spread.tall // 32):
            down_at = j * act_spread.tall + k * 32
            here = slice(down_at, down_at + 32)
            to = slice(act_rows + down_at, act_rows + down_at + 32)
            arena[to, :] = (d_mid[here, :] + feed_sum.from_far[here, :].astype(f32)).astype(bf)
        act_spread.send(j)
    act_spread.keep().start()
    gain_to_near.wait()
    gain_sum[...] += gain_near[...]
    gain_to_far = remote(gain_sum, gain_far, gain_send.at[1], gain_recv.at[1], team.far)
    gain_to_far.start()
    pump(1)
    gain_to_far.wait()
    gain_near[...] = gain_sum[...] + gain_far[...]
    deep = width // n
    for s in range(n):
        gain_parts[s] = gain_near[:, s * deep : (s + 1) * deep]
    load(gain_parts, parts[5]).wait()
    begin(s_gains)
    for j in range(Spread.pieces):
        pump(1)
        ig_spread.pass_on(j)
    for j in range(Spread.pieces):
        pump(1)
        act_spread.pass_on(j)
    pump.rest()
    s_gains.final()
    for spread_of in (ig_spread, act_spread):
        spread_of.arrive()
        spread_of.drain()
        spread_of.keep().wait()
    spread.drain()
    first_sum.drain()
    for group in groups:
        group.drain()


def backward(n, lengths, maps, stream, cot, wholes, kept):
    rows, width = stream.shape
    gains, qkv, out, gate, up, down = wholes
    heads_here = out.shape[1] // 128
    hidden = gate.shape[1]
    tall = maps[1].shape[1]
    bf, f32 = jnp.bfloat16, jnp.float32
    shape = jax.ShapeDtypeStruct
    deep = width // n
    kinds = [
        ((deep, hidden), bf),
        ((deep, hidden), bf),
        ((deep, hidden), bf),
        ((deep, out.shape[1]), bf),
        ((deep, qkv.shape[1]), bf),
        ((16, deep), f32),
    ]
    results = [shape((rows, width), bf)] * 2 + [shape(*kind) for kind in kinds]
    work = [shape((n,) + size, kind) for size, kind in kinds[1:]]
    work += sum((Scatter.landing(n, *kind) for kind in kinds), [])
    state = (heads_here + 1, tall, 128)
    scratch = [
        pltpu.VMEM((rows, width), bf),
        pltpu.VMEM((rows, width), bf),
        pltpu.VMEM((rows // 4, width), f32),
        pltpu.VMEM((rows, width), bf),
        pltpu.VMEM(gains.shape, f32),
        pltpu.VMEM((2, 8, width), f32),
        pltpu.VMEM((16, width), f32),
        pltpu.VMEM((16, width), f32),
        pltpu.VMEM((16, width), f32),
        pltpu.VMEM((n, 16, deep), f32),
    ]
    scratch += [pltpu.VMEM(state, bf)] * 6
    scratch += [pltpu.SemaphoreType.DMA((2,))] * 4
    scratch += [pltpu.SemaphoreType.DMA((24,))]
    scratch += [pltpu.VMEM((2,) + kinds[k][0], kinds[k][1]) for k in (0, 3, 4, 5)]
    scratch += Sum.scratch(rows, width) * 2 + Sum.scratch(rows, width)[2:] + Spread.scratch() + SpreadOut.scratch() * 2
    scratch += sum((Scatter.scratch(n, *kind) for kind in kinds), [])
    anywhere, inside = pl.BlockSpec(memory_space=pl.ANY), pl.BlockSpec(memory_space=pltpu.VMEM)
    given = [stream, cot, *wholes, *kept]
    result = pl.pallas_call(
        functools.partial(backward_kernel, n),
        out_shape=results + work,
        in_specs=[pl.BlockSpec(memory_space=pltpu.SMEM)] + [inside] * 4 + [anywhere] * len(given),
        out_specs=[anywhere] * (len(results) + len(work)),
        scratch_shapes=scratch,
        compiler_params=pltpu.CompilerParams(
            collective_id=1, has_side_effects=True, vmem_limit_bytes=63 * MIB
        ),
    )(lengths, *maps, *given)
    return result[: len(results)]


def on_device(
    stream_in,
    doc_lengths,
    first_gain,
    w_query,
    w_key,
    w_value,
    w_out,
    second_gain,
    w_gate,
    w_up,
    w_down,
    cotangent,
):
    n = lax.axis_size("seq")
    f32 = jnp.float32
    q_wide, k_wide = w_query.shape[1], w_key.shape[1]
    qkv_own = jnp.concatenate([w_query, w_key, w_value], axis=1)
    gains_own = jnp.concatenate([first_gain, second_gain]).astype(f32)
    gains_own = jnp.broadcast_to(gains_own[None], (16, gains_own.shape[0]))
    maps = feature_maps(q_wide)
    shards = (gains_own, qkv_own, w_out.T, w_gate, w_up, w_down.T)
    wholes, kept = forward(n, doc_lengths, stream_in, cotangent, maps, shards)
    activations, input_grad, g_down, g_gate, g_up, g_out, g_qkv, g_gains = backward(
        n, doc_lengths, maps, stream_in, cotangent, wholes, kept
    )
    g_qkv = g_qkv.astype(f32)
    return (
        activations,
        input_grad.astype(f32),
        jnp.sum(g_gains[:8], axis=0),
        g_qkv[:, :q_wide],
        g_qkv[:, q_wide : q_wide + k_wide],
        g_qkv[:, q_wide + k_wide :],
        g_out.astype(f32).T,
        jnp.sum(g_gains[8:], axis=0),
        g_gate.astype(f32),
        g_up.astype(f32),
        g_down.astype(f32).T,
    )


def solution(mesh):
    placed = (
        P("seq", None),
        P(),
        P("seq"),
        P("seq", "tp"),
        P("seq", "tp"),
        P("seq", "tp"),
        P("tp", "seq"),
        P("seq"),
        P("seq", "tp"),
        P("seq", "tp"),
        P("tp", "seq"),
        P("seq", None),
    )
    return jax.shard_map(
        on_device,
        mesh=mesh,
        in_specs=placed,
        out_specs=(
            P("seq", None),
            P("seq", None),
            P("seq"),
            P("seq", "tp"),
            P("seq", "tp"),
            P("seq", "tp"),
            P("tp", "seq"),
            P("seq"),
            P("seq", "tp"),
            P("seq", "tp"),
            P("tp", "seq"),
        ),
        check_vma=False,
    )
```

```python
import functools

import jax
import jax.numpy as jnp
import numpy as np
from jax import lax
from jax.experimental import pallas as pl
from jax.experimental.pallas import tpu as pltpu
from jax.sharding import PartitionSpec as P

FEAT = 16
EPSILON = 1e-06
MESH = pl.DeviceIdType.MESH
MIB = 2**20


def remote(src, dst, send, recv, device):
    return pltpu.make_async_remote_copy(
        src_ref=src,
        dst_ref=dst,
        send_sem=send,
        recv_sem=recv,
        device_id=device,
        device_id_type=MESH,
    )


class Place:
    def __init__(self, n):
        self.n, self.m = n, n // 2
        self.s, self.t = lax.axis_index("seq"), lax.axis_index("tp")
        self.o, self.i = self.s // 2, lax.rem(self.s, 2)
        self.right, self.left = (self.s + 2, self.t), (self.s - 2, self.t)
        self.pair = (self.o * 2 + 1 - self.i, self.t)
        self.has_right, self.has_left = self.o < self.m - 1, self.o > 0
        self.balanced = self.m >= 4
        m, o = self.m, self.o
        self.end = (o == 0) | (o == m - 1)
        self.next = (o == 1) | (o == m - 2)
        self.partner = jnp.where(
            o == 0, 1, jnp.where(o == m - 1, m - 2, jnp.where(o == 1, 0, m - 1))
        )

    def greet(self, others=()):
        barrier = pltpu.get_barrier_semaphore()

        def signal(device):
            pl.semaphore_signal(barrier, inc=1, device_id=device, device_id_type=MESH)

        pl.when(self.has_right)(lambda: signal(self.right))
        pl.when(self.has_left)(lambda: signal(self.left))
        signal(self.pair)
        for other in others:
            signal(other)
        beside = self.has_right.astype(jnp.int32) + self.has_left.astype(jnp.int32)
        pl.semaphore_wait(barrier, beside + (1 + len(others)))


class Gather:
    def __init__(self, at, own, held, sems):
        self.at, self.own_ref, self.held = at, own, held
        self.send, self.recv, self.half_recv, self.local = sems

    @staticmethod
    def scratch(n):
        return [
            pltpu.SemaphoreType.DMA((3, n)),
            pltpu.SemaphoreType.DMA((n,)),
            pltpu.SemaphoreType.DMA((1,)),
            pltpu.SemaphoreType.DMA((1,)),
        ]

    def slot(self, slot, start=0, rows=None):
        if self.held.ndim == 3:
            return self.held.at[slot] if rows is None else self.held.at[slot, pl.ds(start, rows)]
        tall = self.own_ref.shape[0]
        first = pl.multiple_of(slot * tall, 16) + start
        return self.held.at[pl.ds(first, tall if rows is None else rows)]

    def copy(self, slot, way, own=False):
        at = self.at
        return remote(
            self.own_ref if own else self.slot(slot),
            self.slot(slot),
            self.send.at[way, slot],
            self.recv.at[slot],
            (at.right, at.left, at.pair)[way],
        )

    def half(self, slot, way, which):
        at, rows = self.at, self.own_ref.shape[0] // 2
        part = self.slot(slot, which * rows, rows)
        return remote(
            part,
            part,
            self.send.at[way, slot],
            self.recv.at[slot] if which == 0 else self.half_recv.at[0],
            (at.right, at.left, at.pair)[way],
        )

    def local_copy(self):
        return pltpu.make_async_copy(self.own_ref, self.slot(self.at.s), self.local.at[0])

    def own(self):
        at = self.at
        self.local_copy().start()
        pl.when(at.has_right)(lambda: self.copy(at.s, 0, True).start())
        pl.when(at.has_left)(lambda: self.copy(at.s, 1, True).start())
        self.copy(at.s, 2, True).start()

    def to_pair(self, slot, act):
        at = self.at
        if not at.balanced:
            act(self.copy(slot, 2))
            return
        partner = slot // 2 == at.partner
        pl.when(jnp.logical_not(partner & (at.end | at.next)))(lambda: act(self.copy(slot, 2)))
        pl.when(partner & at.end)(lambda: act(self.half(slot, 2, 0)))

    def step(self, k):
        at = self.at
        for way in (0, 1):
            slot = at.s - 2 * k if way == 0 else at.s + 2 * k
            there = at.o - k >= 0 if way == 0 else at.o + k < at.m
            on = at.has_right if way == 0 else at.has_left

            @pl.when(there)
            def _(slot=slot, on=on, way=way):
                self.copy(slot, 2).wait_recv()
                pl.when(on)(lambda: self.copy(slot, way).start())
                self.to_pair(slot, lambda c: c.start())

    def extra_copies(self, act):
        at = self.at
        slot = at.o * 2 + 1 - at.i
        pl.when(at.o == 0)(lambda: act(self.copy(slot, 0)))
        pl.when(at.o == at.m - 1)(lambda: act(self.copy(slot, 1)))
        pl.when(at.o == 1)(lambda: act(self.half(slot, 1, 1)))
        pl.when(at.o == at.m - 2)(lambda: act(self.half(slot, 0, 1)))

    def extra(self):
        at = self.at
        if at.balanced:
            slot = at.o * 2 + 1 - at.i
            pl.when(at.end | at.next)(lambda: self.copy(slot, 2).wait_recv())
            self.extra_copies(lambda c: c.start())

    def arrive(self):
        at = self.at
        self.local_copy().wait()
        for layer in range(at.m):
            slot = layer * 2 + 1 - at.i
            if not at.balanced:
                self.copy(slot, 2).wait_recv()
                continue
            met = (at.o == layer) & (at.end | at.next)
            halved = at.end & (at.partner == layer)
            pl.when(jnp.logical_not(met | halved))(lambda: self.copy(slot, 2).wait_recv())

            @pl.when(halved)
            def _():
                self.half(slot, 2, 0).wait_recv()
                self.half(slot, 2, 1).wait_recv()

    def drain(self):
        at = self.at
        pl.when(at.has_right)(lambda: self.copy(at.s, 0, True).wait_send())
        pl.when(at.has_left)(lambda: self.copy(at.s, 1, True).wait_send())
        self.copy(at.s, 2, True).wait_send()
        for k in range(1, at.m):
            for way in (0, 1):
                slot = at.s - 2 * k if way == 0 else at.s + 2 * k
                there = at.o - k >= 0 if way == 0 else at.o + k < at.m
                on = at.has_right if way == 0 else at.has_left

                @pl.when(there)
                def _(slot=slot, on=on, way=way):
                    pl.when(on)(lambda: self.copy(slot, way).wait_send())
                    self.to_pair(slot, lambda c: c.wait_send())

        if at.balanced:
            self.extra_copies(lambda c: c.wait_send())


def gather_events(groups):
    m = groups[0].at.m
    events = [groups[0].own]
    for g, group in enumerate(groups):
        for k in range(1, m):
            if k == max(1, m - 1) and g + 1 < len(groups):
                events.append(groups[g + 1].own)
            events.append(functools.partial(group.step, k))
            if k == 1 and g:
                events.append(groups[g - 1].extra)
    events.append(groups[-1].extra)
    return events


def add_rows(total, part, start, rows):
    step = next(size for size in (64, 32, 16, 8) if rows % size == 0)

    @pl.loop(0, rows // step)
    def _(j):
        at = pl.ds(pl.multiple_of(start + j * step, 8), step)
        both = total[at, :].astype(jnp.float32) + part[at, :].astype(jnp.float32)
        total[at, :] = both.astype(total.dtype)


class Scatter:
    def __init__(self, at, parts, out, landing, bufs, sems):
        self.at, self.parts, self.out = at, parts, out
        self.from_pair, self.from_line, self.shifted_in = landing
        self.mine, self.aside, self.stage = bufs
        (
            self.pair_send,
            self.pair_recv,
            self.line_send,
            self.line_recv,
            self.extra_send,
            self.extra_recv,
            self.local,
        ) = sems
        self.rows = self.mine.shape[1]

    @staticmethod
    def landing(n, shape, dtype):
        m = n // 2
        return [jax.ShapeDtypeStruct((size,) + shape, dtype) for size in (m, m + 1, 1)]

    @staticmethod
    def scratch(n, shape, dtype):
        m = n // 2
        return [pltpu.VMEM((size,) + shape, dtype) for size in (m, 1)] + [
            pltpu.SemaphoreType.DMA((m,)),
            pltpu.SemaphoreType.DMA((m,)),
            pltpu.SemaphoreType.DMA((m,)),
            pltpu.SemaphoreType.DMA((m + 1,)),
            pltpu.SemaphoreType.DMA((2,)),
            pltpu.SemaphoreType.DMA((2,)),
            pltpu.SemaphoreType.DMA((m + 4,)),
        ]

    def slot(self, slot):
        if self.parts.ndim == 3:
            return self.parts.at[slot]
        return self.parts.at[pl.ds(pl.multiple_of(slot * self.rows, 16), self.rows)]

    def load(self, layer):
        return pltpu.make_async_copy(
            self.slot(layer * 2 + self.at.i), self.mine.at[layer], self.local.at[layer]
        )

    def load_aside(self):
        at = self.at
        return pltpu.make_async_copy(
            self.slot(at.o * 2 + 1 - at.i), self.aside.at[0], self.local.at[at.m]
        )

    def store(self):
        at = self.at
        return pltpu.make_async_copy(self.mine.at[at.o], self.out, self.local.at[at.m + 1])

    def to_stage(self, src, which, start=0, rows=None):
        part = pl.ds(start, self.rows if rows is None else rows)
        return pltpu.make_async_copy(
            src.at[part], self.stage.at[which, part], self.local.at[self.at.m + 2 + which]
        )

    def to_pair(self, layer):
        return remote(
            self.slot(layer * 2 + 1 - self.at.i),
            self.from_pair.at[layer],
            self.pair_send.at[layer],
            self.pair_recv.at[layer],
            self.at.pair,
        )

    def half_to_pair(self, layer, which, src):
        half = self.rows // 2
        part = pl.ds(which * half, half)
        return remote(
            src.at[part],
            self.from_pair.at[layer, part],
            self.pair_send.at[layer] if which == 0 else self.extra_send.at[1],
            self.pair_recv.at[layer] if which == 0 else self.extra_recv.at[1],
            self.at.pair,
        )

    def sum_to_pair(self):
        return remote(
            self.aside.at[0],
            self.from_pair.at[self.at.o],
            self.pair_send.at[self.at.o],
            self.pair_recv.at[self.at.o],
            self.at.pair,
        )

    def along(self, layer, way):
        at = self.at
        there = layer if way == 0 else jnp.where(layer == at.o - 1, at.m, layer)
        return remote(
            self.mine.at[layer],
            self.from_line.at[there],
            self.line_send.at[layer],
            self.line_recv.at[there],
            (at.right, at.left)[way],
        )

    def wait_line(self, place):
        remote(
            self.mine.at[0],
            self.from_line.at[place],
            self.line_send.at[0],
            self.line_recv.at[place],
            self.at.right,
        ).wait_recv()

    def shifted(self, way, which=None):
        at, half = self.at, self.rows // 2
        src, dst = self.slot(at.partner * 2 + 1 - at.i), self.shifted_in.at[0]
        if which is not None:
            src, dst = src.at[pl.ds(half, half)], dst.at[pl.ds(half, half)]
        return remote(
            src, dst, self.extra_send.at[0], self.extra_recv.at[0], (at.right, at.left)[way]
        )

    def far_first(self):
        at = self.at
        for d in range(at.m - 1, 0, -1):
            yield at.o + d, at.o + d < at.m
            yield at.o - d, at.o - d >= 0

    def pair_copies(self, act):
        at = self.at
        for layer, there in self.far_first():
            if not at.balanced:
                pl.when(there)(lambda: act(self.to_pair(layer)))
                continue
            partner = layer == at.partner
            pl.when(there & jnp.logical_not(partner & (at.end | at.next)))(
                lambda: act(self.to_pair(layer))
            )
            pl.when(there & partner & at.end)(
                lambda: act(self.half_to_pair(layer, 0, self.slot(layer * 2 + 1 - at.i)))
            )
        if not at.balanced:
            act(self.to_pair(at.o))
            return
        pl.when(jnp.logical_not(at.end | at.next))(lambda: act(self.to_pair(at.o)))
        pl.when(at.next)(
            lambda: act(self.half_to_pair(at.o, 0, self.slot(at.o * 2 + 1 - at.i)))
        )

    def shift_copies(self, act):
        at = self.at
        if at.balanced:
            pl.when(at.o == 0)(lambda: act(self.shifted(0, 1)))
            pl.when(at.o == at.m - 1)(lambda: act(self.shifted(1, 1)))
            pl.when(at.o == 1)(lambda: act(self.shifted(1)))
            pl.when(at.o == at.m - 2)(lambda: act(self.shifted(0)))

    def start(self):
        at = self.at
        self.shift_copies(lambda c: c.start())
        self.pair_copies(lambda c: c.start())
        for layer in range(at.m):
            self.load(layer).start()
        if at.balanced:
            self.load_aside().start()

    def extra(self):
        at = self.at
        if not at.balanced:
            return
        self.load_aside().wait()
        half, landed = self.rows // 2, self.shifted_in.at[0]

        @pl.when(at.end)
        def _():
            self.shifted(0).wait_recv()
            self.to_stage(landed, 0).start()
            self.to_stage(landed, 0).wait()
            add_rows(self.aside.at[0], self.stage.at[0], 0, self.rows)
            self.sum_to_pair().start()

        @pl.when(at.next)
        def _():
            self.shifted(0, 1).wait_recv()
            self.to_stage(landed, 0, half, half).start()
            self.to_stage(landed, 0, half, half).wait()
            add_rows(self.aside.at[0], self.stage.at[0], half, half)
            self.half_to_pair(at.o, 1, self.aside.at[0]).start()

    def wait_pair(self, layer):
        at = self.at
        if not at.balanced:
            self.to_pair(layer).wait_recv()
            return
        partner, own = layer == at.partner, layer == at.o
        parted = (partner & at.end) | (own & at.next)
        pl.when(jnp.logical_not((partner & (at.end | at.next)) | (own & at.next)))(
            lambda: self.to_pair(layer).wait_recv()
        )
        pl.when(parted)(lambda: self.half_to_pair(layer, 0, self.aside.at[0]).wait_recv())
        pl.when(own & at.next)(lambda: self.half_to_pair(layer, 1, self.aside.at[0]).wait_recv())

    def step(self, d):
        at = self.at
        for way in (0, 1):
            layer = at.o + d if way == 0 else at.o - d
            there = layer < at.m if way == 0 else layer >= 0
            behind = at.has_left if way == 0 else at.has_right

            @pl.when(there)
            def _(layer=layer, behind=behind, way=way):
                mine, paired, half = self.mine.at[layer], self.from_pair.at[layer], self.rows // 2
                self.load(layer).wait()
                self.wait_pair(layer)
                partner = (layer == at.partner) & at.balanced
                whole = jnp.logical_not(partner & (at.end | at.next))
                halved = partner & at.end
                pl.when(whole)(lambda: self.to_stage(paired, 0).start())
                pl.when(halved)(lambda: self.to_stage(paired, 0, 0, half).start())

                @pl.when(behind)
                def _():
                    self.wait_line(layer)
                    self.to_stage(self.from_line.at[layer], 1).start()

                @pl.when(whole)
                def _():
                    self.to_stage(paired, 0).wait()
                    add_rows(mine, self.stage.at[0], 0, self.rows)

                @pl.when(halved)
                def _():
                    self.to_stage(paired, 0, 0, half).wait()
                    add_rows(mine, self.stage.at[0], 0, half)

                @pl.when(behind)
                def _():
                    self.to_stage(self.from_line.at[layer], 1).wait()
                    add_rows(mine, self.stage.at[1], 0, self.rows)

                self.along(layer, way).start()

    def final(self):
        at = self.at
        mine = self.mine.at[at.o]
        self.load(at.o).wait()
        self.wait_pair(at.o)
        self.to_stage(self.from_pair.at[at.o], 0).start()

        @pl.when(at.has_left)
        def _():
            self.wait_line(at.o)
            self.to_stage(self.from_line.at[at.o], 1).start()

        self.to_stage(self.from_pair.at[at.o], 0).wait()
        add_rows(mine, self.stage.at[0], 0, self.rows)

        @pl.when(at.has_right)
        def _():
            self.wait_line(at.m)
            self.to_stage(self.from_line.at[at.m], 0).start()

        @pl.when(at.has_left)
        def _():
            self.to_stage(self.from_line.at[at.o], 1).wait()
            add_rows(mine, self.stage.at[1], 0, self.rows)

        @pl.when(at.has_right)
        def _():
            self.to_stage(self.from_line.at[at.m], 0).wait()
            add_rows(mine, self.stage.at[0], 0, self.rows)

        self.store().start()

    def drain(self):
        at = self.at
        self.pair_copies(lambda c: c.wait_send())
        if at.balanced:
            pl.when(at.end)(lambda: self.sum_to_pair().wait_send())
            pl.when(at.next)(lambda: self.half_to_pair(at.o, 1, self.aside.at[0]).wait_send())
        self.shift_copies(lambda c: c.wait_send())
        for d in range(1, at.m):
            pl.when(at.o + d < at.m)(lambda: self.along(at.o + d, 0).wait_send())
            pl.when(at.o - d >= 0)(lambda: self.along(at.o - d, 1).wait_send())
        self.store().wait()


def fetch(src, dst, sem):
    return pltpu.make_async_copy(src, dst, sem)


def dot(a, b, dims=((1,), (0,))):
    return lax.dot_general(a, b, (dims, ((), ())), preferred_element_type=jnp.float32)


ROWS, COLS, BOTH = ((1,), (0,)), ((1,), (1,)), ((0,), (0,))


def row_start(lengths, position):
    at, start = jnp.int32(0), jnp.zeros_like(position)
    for k in range(lengths.shape[0]):
        start = jnp.maximum(start, jnp.where(at <= position, at, 0))
        at = at + lengths[k]
    return start


def lanes(shape):
    return lax.broadcasted_iota(jnp.int32, shape, len(shape) - 1)


def feature_maps(width):
    count = FEAT + 1 + FEAT * (FEAT + 1) // 2
    wide = -(-count // 128) * 128
    first, second = np.zeros((width, wide), np.float32), np.zeros((width, wide), np.float32)
    plus = np.zeros((3, wide), np.float32)
    plus[:, 0] = 1.0
    heads = np.arange(width // FEAT) * FEAT
    for i in range(FEAT):
        first[heads + i, 1 + i] = 1.0
        plus[1:, 1 + i] = 1.0, 0.25
    at = 1 + FEAT
    for i in range(FEAT):
        for j in range(i, FEAT):
            first[heads + i, at] = 1.0
            second[heads + j, at] = 1.0
            plus[2, at] = 1 / 32 if i == j else 1 / 16
            at += 1
    tall = -(-count // 16) * 16
    return (
        jnp.asarray(np.stack([first, second]), jnp.bfloat16),
        jnp.asarray(np.stack([first.T, second.T])[:, :tall], jnp.bfloat16),
        jnp.asarray(np.repeat(plus[:, None], 8, 1)),
        jnp.asarray(np.repeat(plus[:, :tall, None], 128, 2)),
    )


class Team:
    def __init__(self, at, rows):
        self.at, self.half, self.quarter = at, rows // 2, rows // 4
        t = at.t
        low, high = lax.rem(t, 2), t // 2
        self.near, self.far = (at.s, t + 1 - 2 * low), (at.s, lax.rem(t + 2, 4))
        self.half_at, self.other_half_at = low * self.half, (1 - low) * self.half
        self.quarter_at = self.half_at + high * self.quarter
        self.other_quarter_at = self.half_at + (1 - high) * self.quarter
        self.in_half, self.other_in_half = high * self.quarter, (1 - high) * self.quarter
        self.near_quarter_at = self.other_half_at + high * self.quarter
        self.near_other_at = self.other_half_at + (1 - high) * self.quarter


class Sum:
    pieces = 4

    def __init__(self, team, part, from_near, from_far, sems):
        self.team, self.part, self.from_near, self.from_far = team, part, from_near, from_far
        self.near_send, self.near_recv, self.far_send, self.far_recv = sems
        self.wide = part.shape[1] // self.pieces

    @staticmethod
    def scratch(rows, columns):
        return [
            pltpu.VMEM((rows // 2, columns), jnp.bfloat16),
            pltpu.VMEM((rows // 4, columns), jnp.bfloat16),
        ] + [pltpu.SemaphoreType.DMA((Sum.pieces,))] * 4

    def near(self, j):
        team, columns = self.team, pl.ds(j * self.wide, self.wide)
        return remote(
            self.part.at[pl.ds(pl.multiple_of(team.other_half_at, team.half), team.half), columns],
            self.from_near.at[:, columns],
            self.near_send.at[j],
            self.near_recv.at[j],
            team.near,
        )

    def far(self, j):
        team, columns = self.team, pl.ds(j * self.wide, self.wide)
        at = pl.multiple_of(team.other_quarter_at, team.quarter)
        return remote(
            self.part.at[pl.ds(at, team.quarter), columns],
            self.from_far.at[:, columns],
            self.far_send.at[j],
            self.far_recv.at[j],
            team.far,
        )

    def fold(self, j):
        team, columns = self.team, pl.ds(j * self.wide, self.wide)
        self.near(j).wait_recv()
        step = 64

        @pl.loop(0, team.quarter // step)
        def _(r):
            to = pl.ds(pl.multiple_of(team.other_quarter_at + r * step, step), step)
            of = pl.ds(pl.multiple_of(team.other_in_half + r * step, step), step)
            both = self.part[to, columns].astype(jnp.float32)
            both = both + self.from_near[of, columns].astype(jnp.float32)
            self.part[to, columns] = both.astype(jnp.bfloat16)

        self.far(j).start()

    def arrive(self):
        for j in range(self.pieces):
            self.far(j).wait_recv()

    def rows(self, start, count):
        team = self.team
        a = self.part[pl.ds(pl.multiple_of(team.quarter_at + start, 16), count), :]
        b = self.from_near[pl.ds(pl.multiple_of(team.in_half + start, 16), count), :]
        c = self.from_far[pl.ds(pl.multiple_of(start, 16), count), :]
        return a.astype(jnp.float32) + b.astype(jnp.float32) + c.astype(jnp.float32)

    def drain(self):
        for j in range(self.pieces):
            self.near(j).wait_send()
            self.far(j).wait_send()


class Spread:
    pieces = 4

    def __init__(self, team, whole, sems):
        self.team, self.whole = team, whole
        self.far_send, self.far_recv, self.near_send, self.near_recv, self.on_send, self.on_recv = (
            sems
        )
        self.tall = team.quarter // self.pieces

    @staticmethod
    def scratch():
        return [pltpu.SemaphoreType.DMA((Spread.pieces,))] * 6

    def copy(self, start, j, send, recv, device):
        rows = self.whole.at[pl.ds(pl.multiple_of(start + j * self.tall, self.tall), self.tall)]
        return remote(rows, rows, send.at[j], recv.at[j], device)

    def far(self, j):
        team = self.team
        return self.copy(team.quarter_at, j, self.far_send, self.far_recv, team.far)

    def near(self, j):
        team = self.team
        return self.copy(team.quarter_at, j, self.near_send, self.near_recv, team.near)

    def on(self, j):
        team = self.team
        return self.copy(team.other_quarter_at, j, self.on_send, self.on_recv, team.near)

    def send(self, j):
        self.far(j).start()
        self.near(j).start()

    def pass_on(self, j):
        self.far(j).wait_recv()
        self.on(j).start()

    def arrive(self):
        for j in range(self.pieces):
            self.near(j).wait_recv()
            self.on(j).wait_recv()

    def drain(self):
        for j in range(self.pieces):
            self.far(j).wait_send()
            self.near(j).wait_send()
            self.on(j).wait_send()


class Pump:
    def __init__(self, events):
        self.events = list(events)

    def __call__(self, count):
        for _ in range(min(count, len(self.events))):
            self.events.pop(0)()

    def until(self, event):
        while event in self.events:
            self.events.pop(0)()

    def rest(self):
        self(len(self.events))


def gain_row(gains, which, row):
    n, depth = gains.shape[0], gains.shape[2] // 2
    for s in range(n):
        part = gains[s, 0:8, which * depth : (which + 1) * depth]
        row[:, s * depth : (s + 1) * depth] = part


def scores(query, key, mask):
    s = dot(query, key, COLS) * 0.25
    return 1.0 + s, jnp.where(mask, 1.0 + s + 0.5 * s * s, 0.0)


def pair_mask(row_starts, column_starts, first_row, first_column):
    shape = (row_starts.shape[0], column_starts.shape[1])
    rows = lax.broadcasted_iota(jnp.int32, shape, 0) + first_row
    columns = lax.broadcasted_iota(jnp.int32, shape, 1) + first_column
    return (row_starts == column_starts) & (columns <= rows)


def of_head(values, h):
    lane = lanes((1, values.shape[1]))
    mine = (lane >= h * FEAT) & (lane < (h + 1) * FEAT)
    return jnp.where(mine, values, jnp.zeros_like(values))


def column(values, h):
    return jnp.sum(jnp.where(lanes((1, 128)) == h, values, 0.0), axis=1, keepdims=True)


def with_ones(values):
    return jnp.concatenate([values, jnp.ones_like(values)], axis=1)


def forward_kernel(n, sizes, *refs):
    (
        lengths, stream_h, cot_h, maps, maps_t, plus, plus_t,
        gains_own, query_h, key_h, value_h, out_raw_h, gate_raw_h, up_raw_h, down_raw_h,
        gains_h, qkv_h, out_h, gate_h, up_h, down_h,
        h_one_h, heads_h, mixed_h, rden_h, state_h, mid_h, h_two_h, gate_v_h, up_v_h, hid_h, part_h,
        query_own, key_own, value_own, out_raw, gate_raw, up_raw, down_raw,
        qkv_own, out_own, gate_own, up_own, down_own,
        stream, h_one, heads, w_qkv, w_out, mixed, rden, numer, mid, h_two, w_ff,
        gate_v, up_v, hid, part, gains, gain,
        t_own, t_pair, t_line, t_next, state, t_send, t_recv, local, part_sem,
        *sems,
    ) = refs
    rows, width = stream.shape
    heads_here = mixed.shape[1] // 128
    q_wide = heads_here * FEAT
    at = Place(n)
    team = Team(at, rows)
    near_sum, sems = sems[:6], sems[6:]
    spread_sems, sems = sems[:6], sems[6:]
    shards = (gains_own, qkv_own, out_own, gate_own, up_own, down_own)
    wholes = (gains_h, qkv_h, out_h, gate_h, up_h, down_h)
    groups = [
        Gather(at, shards[g], wholes[g], sems[4 * g : 4 * g + 4]) for g in range(len(shards))
    ]
    g_gains, g_qkv, g_out, g_gate, g_up, g_down = groups
    cell = iter(range(local.shape[0]))
    copies = []

    def load(src, dst):
        copy = fetch(src, dst, local.at[next(cell)])
        copy.start()
        return copy

    def save(src, dst):
        copies.append(load(src, dst))

    raw = [
        load(query_h, query_own),
        load(key_h, key_own),
        load(value_h, value_own),
        load(out_raw_h, out_raw),
        load(gate_raw_h, gate_raw),
        load(up_raw_h, up_raw),
        load(down_raw_h, down_raw),
    ]
    get_stream = load(stream_h, stream)
    at.greet((team.near, team.far))
    pump = Pump(gather_events(groups))
    pump(1)
    for copy in raw[:3]:
        copy.wait()
    qkv_own[:, 0:q_wide] = query_own[...].T
    qkv_own[:, q_wide : 2 * q_wide] = key_own[...].T
    qkv_own[:, 2 * q_wide :] = value_own[...]
    pump.until(g_qkv.own)
    for copy, turned, own in zip(
        raw[3:], (out_raw, gate_raw, up_raw, down_raw), (out_own, gate_own, up_own, down_own)
    ):
        copy.wait()
        own[...] = turned[...].T
    pump.until(g_gains.extra)
    g_gains.arrive()
    load(gains_h, gains).wait()
    gain_row(gains, 0, gain.at[0])
    gain_row(gains, 1, gain.at[1])
    get_stream.wait()

    @pl.loop(0, rows // 64)
    def _(j):
        here = pl.ds(pl.multiple_of(j * 64, 64), 64)
        x = stream[here, :].astype(jnp.float32)
        scale = lax.rsqrt(jnp.mean(x * x, axis=1, keepdims=True) + EPSILON)
        h_one[here, :] = (x * scale * gain[0, 0:1, :]).astype(jnp.bfloat16)

    save(h_one, h_one_h)
    pump.until(g_qkv.extra)
    g_qkv.arrive()
    load(qkv_h, w_qkv).wait()

    @pl.loop(0, rows // 256)
    def _(j):
        here = pl.ds(pl.multiple_of(j * 256, 256), 256)
        heads[here, :] = dot(h_one[here, :], w_qkv[...]).astype(jnp.bfloat16)

    save(heads, heads_h)
    pump(1)
    first = at.s * rows
    starts_col = row_start(lengths, first + lax.broadcasted_iota(jnp.int32, (rows, 1), 0))
    starts_row = row_start(lengths, first + lax.broadcasted_iota(jnp.int32, (1, rows), 1))
    last = row_start(lengths, first + rows - 1)
    keep = jnp.where(starts_row == last, 1.0, 0.0)
    tall = t_own.shape[1]

    def values_of(h):
        return pl.ds(pl.multiple_of(2 * q_wide + h * 128, 128), 128)

    t_sum = numer.at[0, 0:tall, 0:128]
    t_sum[...] = jnp.zeros((tall, 128), jnp.float32)

    @pl.loop(0, heads_here)
    def _(h):
        key = of_head(heads[:, q_wide : 2 * q_wide], h)
        one = dot(maps_t[0], key, COLS) + plus_t[0][:, 0:1]
        two = dot(maps_t[1], key, COLS) + plus_t[1][:, 0:1]
        phi = (one * two * keep).astype(jnp.bfloat16)
        total = dot(phi, with_ones(heads[:, values_of(h)]))
        t_own[h] = total[:, :128].astype(jnp.bfloat16)
        t_sum[...] += jnp.where(lanes((tall, 128)) == h, total[:, 128:], 0.0)

    t_own[heads_here] = t_sum[...].astype(jnp.bfloat16)
    to_pair = remote(t_own, t_pair, t_send.at[0], t_recv.at[0], at.pair)
    to_right = remote(t_next, t_line, t_send.at[1], t_recv.at[1], at.right)
    to_pair.start()
    pump(1)
    tile = 256

    @pl.loop(0, heads_here)
    def _(h):
        key = heads[:, q_wide : 2 * q_wide]
        for j in range(rows // tile):
            upto = (j + 1) * tile
            query = of_head(heads[j * tile : upto, 0:q_wide], h)
            mask = pair_mask(starts_col[j * tile : upto], starts_row[:, :upto], j * tile, 0)
            _, weights = scores(query, key[:upto], mask)
            values = with_ones(heads[0:upto, values_of(h)])
            numer[h, j * tile : upto, :] = dot(weights.astype(jnp.bfloat16), values)

    pump(1)

    def closed(s):
        return jnp.where(row_start(lengths, (s + 1) * rows - 1) >= s * rows, 0.0, 1.0)

    on_one, on_two = closed(at.o * 2), closed(at.o * 2 + 1)

    @pl.when(at.o == 0)
    def _():
        t_line[...] = jnp.zeros_like(t_line)

    to_pair.wait_recv()
    pl.when(at.has_left)(lambda: to_right.wait_recv())
    for h in range(heads_here + 1):
        mine, other = t_own[h].astype(jnp.float32), t_pair[h].astype(jnp.float32)
        t_one, t_two = jnp.where(at.i == 0, mine, other), jnp.where(at.i == 0, other, mine)
        come = t_line[h].astype(jnp.float32)
        middle = t_one + on_one * come
        t_next[h] = (t_two + on_two * middle).astype(jnp.bfloat16)
        state[h] = jnp.where(at.i == 0, come, middle).astype(jnp.bfloat16)
    pl.when(at.has_right)(lambda: to_right.start())
    save(state, state_h)
    pump(1)

    rden[...] = jnp.zeros_like(rden)
    @pl.loop(0, heads_here)
    def _(h):
        own = lanes((tall, 128)) == h
        dens = jnp.sum(jnp.where(own, state[heads_here].astype(jnp.float32), 0.0), 1, keepdims=True)
        dens = jnp.broadcast_to(dens, (tall, 128)).astype(jnp.bfloat16)
        table = jnp.concatenate([state[h], dens], axis=1)
        table = jnp.concatenate(
            [table, jnp.zeros((maps.shape[2] - tall, 256), jnp.bfloat16)], axis=0
        )
        for j in range(rows // tile):
            here = slice(j * tile, (j + 1) * tile)
            query = of_head(heads[here, 0:q_wide], h)
            one = dot(query, maps[0]) + plus[0, 0:1, :]
            two = dot(query, maps[1]) + plus[1, 0:1, :]
            carried = jnp.where(starts_col[here] < first, 1.0, 0.0)
            phi = (one * two * plus[2, 0:1, :] * carried).astype(jnp.bfloat16)
            total = numer[h, here, :] + dot(phi, table)
            inverse = 1.0 / total[:, 128:]
            rden[here, :] = jnp.where(lanes((1, 128)) == h, inverse, rden[here, :])
            mixed[here, pl.ds(pl.multiple_of(h * 128, 128), 128)] = (
                total[:, :128] * inverse
            ).astype(jnp.bfloat16)

    save(mixed, mixed_h)
    save(rden, rden_h)
    pump.until(g_out.extra)
    g_out.arrive()
    load(out_h, w_out).wait()
    for copy in copies:
        copy.wait()
    copies.clear()

    part_sum = Sum(team, h_one, *near_sum[:2], near_sum[2:])
    for j in range(Sum.pieces):
        columns = slice(j * part_sum.wide, (j + 1) * part_sum.wide)

        @pl.loop(0, rows // 256)
        def _(r):
            here = pl.ds(pl.multiple_of(r * 256, 256), 256)
            h_one[here, columns] = dot(mixed[here, :], w_out[columns, :], COLS).astype(jnp.bfloat16)

        part_sum.near(j).start()
        if j:
            part_sum.fold(j - 1)
            pump(1)
    part_sum.fold(Sum.pieces - 1)
    pump(1)
    part_sum.arrive()
    spread = Spread(team, h_two, spread_sems)
    for j in range(Spread.pieces):
        for k in range(spread.tall // 32):
            down = j * spread.tall + k * 32
            here = pl.ds(pl.multiple_of(team.quarter_at + down, 32), 32)
            x = part_sum.rows(down, 32) + stream[here, :].astype(jnp.float32)
            mid[down : down + 32, :] = x
            scale = lax.rsqrt(jnp.mean(x * x, axis=1, keepdims=True) + EPSILON)
            h_two[here, :] = (x * scale * gain[1, 0:1, :]).astype(jnp.bfloat16)
        spread.send(j)
    save(mid, mid_h)
    for j in range(Spread.pieces):
        pump(1)
        spread.pass_on(j)
    get_cot = load(cot_h, stream)
    spread.arrive()
    part_sum.drain()
    spread.drain()
    save(h_two, h_two_h)
    pump.until(g_gate.extra)
    g_gate.arrive()
    get_gate = load(gate_h, w_ff.at[0])
    pump.until(g_up.extra)
    g_up.arrive()
    load(up_h, w_ff.at[1]).wait()
    get_gate.wait()
    stages = 4
    for stage in range(stages):

        @pl.loop(0, rows // 128 // stages)
        def _(r):
            start = pl.multiple_of((stage * (rows // 128 // stages) + r) * 128, 128)
            here = pl.ds(start, 128)
            gate = dot(h_two[here, :], w_ff[0])
            up = dot(h_two[here, :], w_ff[1])
            hidden = gate * jax.nn.sigmoid(gate) * up
            gate_v[here, :] = gate.astype(jnp.bfloat16)
            up_v[here, :] = up.astype(jnp.bfloat16)
            hid[here, :] = hidden.astype(jnp.bfloat16)

        pump(1)
    save(gate_v, gate_v_h)
    save(up_v, up_v_h)
    save(hid, hid_h)
    get_cot.wait()
    def to_hbm(s, slot):
        here = pl.ds(pl.multiple_of(s * 256, 256), 256)
        return fetch(part.at[slot], part_h.at[here], part_sem.at[slot])

    count = width // 256
    for half in range(2):

        @pl.loop(half * (count // 2), (half + 1) * (count // 2))
        def _(s):
            slot = lax.rem(s, 2)
            pl.when(s > 1)(lambda: to_hbm(s - 2, slot).wait())
            columns = pl.ds(pl.multiple_of(s * 256, 256), 256)
            part[slot] = dot(stream[:, columns], hid[...], BOTH).astype(jnp.bfloat16)
            to_hbm(s, slot).start()

        pump(1)
    for s in range(count - 2, count):
        to_hbm(s, s % 2).wait()
    pump.rest()
    g_down.arrive()
    for group in groups:
        group.drain()
    to_pair.wait_send()
    pl.when(at.has_right)(lambda: to_right.wait_send())
    for copy in copies:
        copy.wait()


def forward(n, lengths, stream, cot, maps, shards):
    rows, width = stream.shape
    gains, query, key, value, out, gate, up, down = shards
    hidden, deep = gate.shape
    values = out.shape[0]
    qkv_wide = 2 * query.shape[0] + values
    heads_here = values // 128
    tall = maps[1].shape[1]
    bf, f32 = jnp.bfloat16, jnp.float32
    shape = jax.ShapeDtypeStruct
    wholes = [
        shape((n,) + gains.shape, f32),
        shape((width, qkv_wide), bf),
        shape((width, values), bf),
        shape((width, hidden), bf),
        shape((width, hidden), bf),
        shape((width, hidden), bf),
    ]
    kept = [
        shape((rows, width), bf),
        shape((rows, qkv_wide), bf),
        shape((rows, values), bf),
        shape((rows, 128), f32),
        shape((heads_here + 1, tall, 128), bf),
        shape((rows // 4, width), f32),
        shape((rows, width), bf),
        shape((rows, hidden), bf),
        shape((rows, hidden), bf),
        shape((rows, hidden), bf),
        shape((width, hidden), bf),
    ]
    state = (heads_here + 1, tall, 128)
    scratch = [pltpu.VMEM(a.shape, bf) for a in shards[1:]]
    scratch += [pltpu.VMEM((deep, wide), bf) for wide in (qkv_wide, values, hidden, hidden, hidden)]
    scratch += [
        pltpu.VMEM((rows, width), bf),
        pltpu.VMEM((rows, width), bf),
        pltpu.VMEM((rows, qkv_wide), bf),
        pltpu.VMEM((width, qkv_wide), bf),
        pltpu.VMEM((width, values), bf),
        pltpu.VMEM((rows, values), bf),
        pltpu.VMEM((rows, 128), f32),
        pltpu.VMEM((heads_here, rows, 256), f32),
        pltpu.VMEM((rows // 4, width), f32),
        pltpu.VMEM((rows, width), bf),
        pltpu.VMEM((2, width, hidden), bf),
        pltpu.VMEM((rows, hidden), bf),
        pltpu.VMEM((rows, hidden), bf),
        pltpu.VMEM((rows, hidden), bf),
        pltpu.VMEM((2, 256, hidden), bf),
        pltpu.VMEM((n,) + gains.shape, f32),
        pltpu.VMEM((2, 8, width), f32),
        pltpu.VMEM(state, bf),
        pltpu.VMEM(state, bf),
        pltpu.VMEM(state, bf),
        pltpu.VMEM(state, bf),
        pltpu.VMEM(state, bf),
        pltpu.SemaphoreType.DMA((2,)),
        pltpu.SemaphoreType.DMA((2,)),
        pltpu.SemaphoreType.DMA((32,)),
        pltpu.SemaphoreType.DMA((2,)),
    ]
    scratch += Sum.scratch(rows, width) + Spread.scratch() + Gather.scratch(n) * len(wholes)
    anywhere, inside = pl.BlockSpec(memory_space=pl.ANY), pl.BlockSpec(memory_space=pltpu.VMEM)
    result = pl.pallas_call(
        functools.partial(forward_kernel, n, None),
        out_shape=wholes + kept,
        in_specs=[pl.BlockSpec(memory_space=pltpu.SMEM), anywhere, anywhere]
        + [inside] * 4
        + [anywhere] * len(shards),
        out_specs=[anywhere] * (len(wholes) + len(kept)),
        scratch_shapes=scratch,
        compiler_params=pltpu.CompilerParams(
            collective_id=0, has_side_effects=True, vmem_limit_bytes=62 * MIB
        ),
    )(lengths, stream, cot, *maps, *shards)
    return result[: len(wholes)], result[len(wholes) :]


class SpreadOut(Spread):
    def __init__(self, team, quarter, whole, sems):
        super().__init__(team, whole, sems[:-1])
        self.own, self.kept = quarter, sems[-1]

    @staticmethod
    def scratch():
        return Spread.scratch() + [pltpu.SemaphoreType.DMA((1,))]

    def own_copy(self, j, send, recv, device):
        start = self.team.quarter_at + j * self.tall
        rows = self.whole.at[pl.ds(pl.multiple_of(start, self.tall), self.tall)]
        src = self.own.at[pl.ds(j * self.tall, self.tall)]
        return remote(src, rows, send.at[j], recv.at[j], device)

    def far(self, j):
        return self.own_copy(j, self.far_send, self.far_recv, self.team.far)

    def near(self, j):
        return self.own_copy(j, self.near_send, self.near_recv, self.team.near)

    def keep(self):
        team = self.team
        rows = self.whole.at[pl.ds(pl.multiple_of(team.quarter_at, team.quarter), team.quarter)]
        return pltpu.make_async_copy(self.own, rows, self.kept.at[0])


def backward_kernel(n, *refs):
    (
        lengths, maps, maps_t, plus, plus_t,
        stream_h, cot_h, gains_h, qkv_h, out_h, gate_h, up_h, down_h,
        h_one_h, heads_h, mixed_h, rden_h, state_h, mid_h, h_two_h, gate_v_h, up_v_h, hid_h, part_h,
        *refs,
    ) = refs
    act_h, ig_h, *refs = refs
    outs, refs = refs[:6], refs[6:]
    parts, refs = [part_h] + refs[:5], refs[5:]
    landings, refs = refs[:18], refs[18:]
    (
        part, arena, d_mid, dm, gains, gain, gain_sum, gain_near, gain_far, gain_parts,
        t_own, t_pair, t_line, t_next, state, back, t_send, t_recv, gain_send, gain_recv, local,
        stage_g, stage_o, stage_q, stage_n,
        *sems,
    ) = refs
    rows, width = arena.shape
    hidden = gate_v_h.shape[1]
    values_wide = mixed_h.shape[1]
    heads_here = values_wide // 128
    q_wide = heads_here * FEAT
    at = Place(n)
    team = Team(at, rows)

    def take(count):
        nonlocal sems
        taken, sems = sems[:count], sems[count:]
        return taken

    sums = [take(6) for _ in range(2)]
    first_sems = take(4)
    dm_sems, act_sems, ig_sems = take(6), take(7), take(7)
    stages = (stage_g, stage_g, stage_g, stage_o, stage_q, stage_n)
    groups = []
    for g in range(6):
        mine, aside, *own_sems = take(9)
        groups.append(
            Scatter(
                at,
                parts[g],
                outs[g],
                landings[3 * g : 3 * g + 3],
                (mine, aside, stages[g]),
                own_sems,
            )
        )
    s_down, s_gate, s_up, s_out, s_qkv, s_gains = groups
    at.greet((team.near, team.far))
    cell = iter(range(local.shape[0]))

    def load(src, dst):
        copy = fetch(src, dst, local.at[next(cell)])
        copy.start()
        return copy

    pump = Pump([])

    def begin(group):
        group.start()
        for d in range(at.m - 1, 0, -1):
            pump.events.append(functools.partial(group.step, d))
        pump.events.append(group.extra)

    begin(s_down)
    get_gains = load(gains_h, gains)
    get_mid = load(mid_h, d_mid)
    part_sum = Sum(team, part, *sums[0][:2], sums[0][2:])
    feed_sum = Sum(team, part, *sums[1][:2], sums[1][2:])
    first_sum = Sum(team, part, *sums[0][:2], first_sems)
    spread = Spread(team, dm, dm_sems)
    ig_rows = team.quarter
    ig_spread = SpreadOut(team, arena.at[pl.ds(ig_rows, team.quarter)], ig_h, ig_sems)
    act_spread = SpreadOut(team, feed_sum.from_far, act_h, act_sems)
    piece = part_sum.wide

    def staged(sem, tile, parts_h, compute):
        count = width // 256

        def to_hbm(s, slot):
            here = pl.ds(pl.multiple_of(s * 256, 256), 256)
            return fetch(tile.at[slot], parts_h.at[here], sem.at[slot])

        @pl.loop(0, count)
        def _(s):
            slot = lax.rem(s, 2)
            pl.when(s > 1)(lambda: to_hbm(s - 2, slot).wait())
            columns = pl.ds(pl.multiple_of(s * 256, 256), 256)
            tile[slot] = compute(columns).astype(jnp.bfloat16)
            to_hbm(s, slot).start()

        for s in range(count - 2, count):
            to_hbm(s, s % 2).wait()

    def norm_back(x, grad, gain_ref, which):
        scale = lax.rsqrt(jnp.mean(x * x, axis=1, keepdims=True) + EPSILON)
        unit = x * scale
        total = jnp.sum((grad * unit).reshape(-1, 8, width), axis=0)
        gain_sum[8 * which : 8 * which + 8, :] += total
        scaled = grad * gain_ref[0:1, :]
        return scale * (scaled - unit * jnp.mean(scaled * unit, axis=1, keepdims=True))

    gain_sum[...] = jnp.zeros_like(gain_sum)

    def feed_forward(w_down, w_ff, ff, w_sem, tile_sem):
        get_cot, get_down = load(cot_h, arena), load(down_h, w_down)
        get_gate, get_up = load(gate_v_h, ff.at[0]), load(up_v_h, ff.at[1])
        tall = w_ff.shape[2]

        def weights(j, which):
            here = pl.ds(j * tall, tall)
            return fetch(
                (gate_h, up_h)[which].at[here], w_ff.at[j % 2, which], w_sem.at[j % 2, which]
            )

        for which in (0, 1):
            weights(0, which).start()
        get_cot.wait()
        get_down.wait()
        get_gate.wait()
        get_up.wait()
        block = 256
        for low in range(0, hidden, 512):
            high = min(hidden, low + 512)

            @pl.loop(0, rows // block)
            def _(r):
                here = pl.ds(pl.multiple_of(r * block, block), block)
                grad = dot(arena[here, :], w_down[:, low:high])
                gate = ff[0, here, low:high].astype(jnp.float32)
                sigma = jax.nn.sigmoid(gate)
                silu = gate * sigma
                up = ff[1, here, low:high].astype(jnp.float32)
                ff[0, here, low:high] = (grad * up * (sigma + silu * (1.0 - sigma))).astype(
                    jnp.bfloat16
                )
                ff[1, here, low:high] = (grad * silu).astype(jnp.bfloat16)

        pump(1)
        get_two = load(h_two_h, arena)
        count = width // tall
        for j in range(count):
            for which in (0, 1):
                if j + 1 < count:
                    weights(j + 1, which).start()
                weights(j, which).wait()

            @pl.loop(0, rows // 512)
            def _(r):
                here = pl.ds(pl.multiple_of(r * 512, 512), 512)
                grad = dot(ff[0, here, :], w_ff[j % 2, 0], COLS)
                grad += dot(ff[1, here, :], w_ff[j % 2, 1], COLS)
                part[here, j * tall : (j + 1) * tall] = grad.astype(jnp.bfloat16)

            if (j + 1) * tall % piece == 0:
                p = (j + 1) * tall // piece - 1
                part_sum.near(p).start()
                if p:
                    part_sum.fold(p - 1)
        part_sum.fold(Sum.pieces - 1)
        get_two.wait()
        pump(1)
        tile = w_ff.at[0]

        def grads(which):
            return lambda columns: dot(arena[:, columns], ff[which], BOTH)

        staged(tile_sem, tile, parts[1], grads(0))
        begin(s_gate)
        get_gains.wait()
        gain_row(gains, 0, gain.at[0])
        gain_row(gains, 1, gain.at[1])
        get_mid.wait()
        part_sum.arrive()
        quarter = pl.ds(pl.multiple_of(team.quarter_at, team.quarter), team.quarter)
        load(cot_h.at[quarter], dm.at[quarter]).wait()
        for j in range(Spread.pieces):

            @pl.loop(0, spread.tall // 32)
            def _(r):
                start = pl.multiple_of(j * spread.tall + r * 32, 32)
                here = pl.ds(pl.multiple_of(team.quarter_at + start, 32), 32)
                x = d_mid[pl.ds(start, 32), :]
                grad = norm_back(x, part_sum.rows(start, 32), gain.at[1], 1)
                grad = grad + dm[here, :].astype(jnp.float32)
                d_mid[pl.ds(start, 32), :] = grad
                dm[here, :] = grad.astype(jnp.bfloat16)

            spread.send(j)
        part_sum.drain()
        pump(1)
        staged(tile_sem, tile, parts[2], grads(1))
        pump(1)
        get_hid = load(hid_h, ff.at[0])
        get_hid.wait()
        for j in range(Sum.pieces):
            columns = slice(j * piece, (j + 1) * piece)

            @pl.loop(0, rows // 512)
            def _(r):
                here = pl.ds(pl.multiple_of(r * 512, 512), 512)
                feed = dot(ff[0, here, :], w_down[columns, :], COLS)
                part[here, columns] = feed.astype(jnp.bfloat16)

            feed_sum.near(j).start()
            spread.pass_on(j)
            if j == Sum.pieces - 2:
                pump(1)


    pl.run_scoped(
        feed_forward,
        pltpu.VMEM(down_h.shape, jnp.bfloat16),
        pltpu.VMEM((2, 2, 256, hidden), jnp.bfloat16),
        pltpu.VMEM((2, rows, hidden), jnp.bfloat16),
        pltpu.SemaphoreType.DMA((2, 2)),
        pltpu.SemaphoreType.DMA((2,)),
    )

    def attention(
        heads, d_heads, mixed, w_out, w_qkv, delta, g, delta_row, d_query, d_key,
        dens, tile_o, tile_q, tile_sem, d_values, mid_part, mid_sem, qkv_sem,
    ):
        gets = [
            load(heads_h, heads),
            load(mixed_h, mixed),
            load(out_h, w_out),
            load(rden_h, delta),
            load(state_h, state),
        ]
        get_one = load(h_one_h, arena)

        def mid_rows(j):
            here = pl.ds(j * act_spread.tall, act_spread.tall)
            return fetch(mid_h.at[here], mid_part.at[j % 2], mid_sem.at[j % 2])

        def qkv_rows(j):
            here = pl.ds(j * piece, piece)
            return fetch(qkv_h.at[here], w_qkv.at[j % 2], qkv_sem.at[j % 2])

        for j in range(2):
            mid_rows(j).start()
            qkv_rows(j).start()
        for get in gets:
            get.wait()
        spread.arrive()

        @pl.loop(0, rows // 256)
        def _(r):
            here = pl.ds(pl.multiple_of(r * 256, 256), 256)
            d_values[here, :] = dot(dm[here, :], w_out[...])

        for j in range(Sum.pieces):
            feed_sum.fold(j)

        @pl.loop(0, heads_here)
        def _(h):
            across = pl.ds(pl.multiple_of(h * 128, 128), 128)
            grad = d_values[:, across] * column(delta[...], h)
            g[h] = grad.astype(jnp.bfloat16)
            sums_of = jnp.sum(grad * mixed[:, across].astype(jnp.float32), axis=1, keepdims=True)
            wide = jnp.broadcast_to(sums_of, (rows, 128))
            delta[...] = jnp.where(lanes((1, 128)) == h, wide, delta[...])
            delta_row[h] = wide.T[0:8]

        first = at.s * rows
        starts_col = row_start(lengths, first + lax.broadcasted_iota(jnp.int32, (rows, 1), 0))
        starts_row = row_start(lengths, first + lax.broadcasted_iota(jnp.int32, (1, rows), 1))
        last = row_start(lengths, first + rows - 1)
        tall = t_own.shape[1]
        wide = maps.shape[2]
        carried_row = jnp.where(starts_row < first, 1.0, 0.0)
        dens[1, 0:tall, 0:128] = jnp.zeros((tall, 128), jnp.float32)

        def values_of(h):
            return pl.ds(pl.multiple_of(2 * q_wide + h * 128, 128), 128)

        def head_at(h):
            return pl.ds(pl.multiple_of(h * 128, 128), 128)

        @pl.loop(0, heads_here)
        def _(h):
            query = of_head(heads[:, 0:q_wide], h)
            one = dot(maps_t[0], query, COLS) + plus_t[0][:, 0:1]
            two = dot(maps_t[1], query, COLS) + plus_t[1][:, 0:1]
            phi = one * two * plus_t[2][:, 0:1] * carried_row
            t_own[h] = dot(phi.astype(jnp.bfloat16), g[h]).astype(jnp.bfloat16)
            below = -jnp.sum(phi * delta_row[h][0:1, :], axis=1, keepdims=True)
            dens[1, 0:tall, 0:128] += jnp.where(lanes((tall, 128)) == h, below, 0.0)

        t_own[heads_here] = dens[1, 0:tall, 0:128].astype(jnp.bfloat16)
        to_pair = remote(t_own, t_pair, t_send.at[0], t_recv.at[0], at.pair)
        to_left = remote(t_next, t_line, t_send.at[1], t_recv.at[1], at.left)
        to_pair.start()
        begin(s_up)

        @pl.when(at.o == at.m - 1)
        def _():
            t_line[...] = jnp.zeros_like(t_line)

        def closed(s):
            return jnp.where(row_start(lengths, (s + 1) * rows - 1) >= s * rows, 0.0, 1.0)

        on_one, on_two = closed(at.o * 2), closed(at.o * 2 + 1)

        def relay():
            to_pair.wait_recv()
            pl.when(at.has_right)(lambda: to_left.wait_recv())

            @pl.loop(0, heads_here + 1)
            def _(h):
                mine, other = t_own[h].astype(jnp.float32), t_pair[h].astype(jnp.float32)
                t_one, t_two = jnp.where(at.i == 0, mine, other), jnp.where(at.i == 0, other, mine)
                come = t_line[h].astype(jnp.float32)
                middle = t_two + on_two * come
                t_next[h] = (t_one + on_one * middle).astype(jnp.bfloat16)
                back[h] = jnp.where(at.i == 0, middle, come).astype(jnp.bfloat16)

            pl.when(at.has_left)(lambda: to_left.start())

        turns = min(4, at.m)

        def turn(p):
            mine = at.o == at.m - 1 - p if p < turns - 1 else at.o <= at.m - turns
            pl.when(mine)(relay)

        d_query[...] = jnp.zeros_like(d_query)
        d_key[...] = jnp.zeros_like(d_key)
        tile = 128

        def intra(h):
            key, query = of_head(heads[:, q_wide : 2 * q_wide], h), of_head(heads[:, 0:q_wide], h)
            across = values_of(h)
            for j in range(rows // tile):
                here, upto = slice(j * tile, (j + 1) * tile), (j + 1) * tile
                mask = pair_mask(starts_col[here], starts_row[:, :upto], j * tile, 0)
                more, _ = scores(query[here], key[:upto], mask)
                d_weight = dot(g[h, here, :], heads[0:upto, across], COLS) - column(delta[here, :], h)
                d_score = jnp.where(mask, d_weight * more, 0.0).astype(jnp.bfloat16)
                d_query[here, :] += dot(d_score, key[:upto]) * 0.25
            for j in range(rows // tile):
                here, after = slice(j * tile, (j + 1) * tile), j * tile
                shape = (tile, rows - after)
                key_at = lax.broadcasted_iota(jnp.int32, shape, 0)
                query_at = lax.broadcasted_iota(jnp.int32, shape, 1)
                mask = (starts_col[here] == starts_row[:, after:]) & (key_at <= query_at)
                more, weight = scores(key[here], query[after:], mask)
                d_weight = dot(heads[here, across], g[h, after:, :], COLS)
                d_weight = d_weight - delta_row[h, 0:1, after:]
                d_score = jnp.where(mask, d_weight * more, 0.0).astype(jnp.bfloat16)
                d_values[here, head_at(h)] = dot(weight.astype(jnp.bfloat16), g[h, after:, :])
                grad = dot(d_score, query[after:]) * 0.25
                d_key[here, :] = jnp.where(h == 0, grad, d_key[here, :] + grad)

        for half in range(2):
            @pl.loop(half * heads_here // 2, (half + 1) * heads_here // 2)
            def _(h):
                intra(h)

        turn(0)
        pump(1)

        def through(u, h, grad):
            one = dot(u, maps[0]) + plus[0, 0:1, :]
            two = dot(u, maps[1]) + plus[1, 0:1, :]
            grad = grad()
            left = dot((grad * two).astype(jnp.bfloat16), maps[0], COLS)
            left += dot((grad * one).astype(jnp.bfloat16), maps[1], COLS)
            return one * two, of_head(left, h)

        wider = 256

        def each_tile(body):
            @pl.loop(0, heads_here)
            def _(h):
                @pl.loop(0, rows // wider)
                def _(j):
                    here = pl.ds(pl.multiple_of(j * wider, wider), wider)
                    at_row = first + j * wider + lax.broadcasted_iota(jnp.int32, (wider, 1), 0)
                    body(h, here, row_start(lengths, at_row))

        filler = jnp.zeros((wide - tall, 128), jnp.bfloat16)
        dens[0] = jnp.zeros_like(dens[0])
        dens[0, 0:128, 0:tall] = state[heads_here].astype(jnp.float32).T

        def through_in(h, here, starts):
            carried = jnp.where(starts < first, 1.0, 0.0)

            def grad_phi():
                table = jnp.concatenate([state[h], filler], axis=0)
                grad = dot(g[h, here, :], table, COLS)
                grad = grad - column(delta[here, :], h) * dens[0, pl.ds(h, 1), :]
                return grad * plus[2, 0:1, :] * carried

            _, grad = through(of_head(heads[here, 0:q_wide], h), h, grad_phi)
            d_query[here, :] += grad

        each_tile(through_in)
        turn(1)

        def grad_out(columns):
            return dot(dm[:, columns], mixed[...], BOTH)

        staged(tile_sem, tile_o, parts[3], grad_out)
        begin(s_out)
        turn(2)
        pump(1)
        feed_sum.arrive()
        for j in range(Spread.pieces):
            mid_rows(j).wait()

            @pl.loop(0, act_spread.tall // 32)
            def _(r):
                start = pl.multiple_of(j * act_spread.tall + r * 32, 32)
                x = mid_part[j % 2, pl.ds(pl.multiple_of(r * 32, 32), 32), :]
                x = x + feed_sum.rows(start, 32)
                feed_sum.from_far[pl.ds(start, 32), :] = x.astype(bf)

            if j + 2 < Spread.pieces:
                mid_rows(j + 2).start()
            act_spread.send(j)
        act_spread.keep().start()
        feed_sum.drain()
        pump(2)
        for p in range(3, turns):
            turn(p)

        dens[1] = jnp.zeros_like(dens[1])
        dens[1, 0:128, 0:tall] = back[heads_here].astype(jnp.float32).T

        def through_out(h, here, starts):
            keep = jnp.where(starts == last, 1.0, 0.0)
            table = jnp.concatenate([back[h], filler], axis=0)

            def grad_phi():
                grad = dot(heads[here, values_of(h)], table, COLS)
                return (grad + dens[1, pl.ds(h, 1), :]) * keep

            phi, grad = through(of_head(heads[here, q_wide : 2 * q_wide], h), h, grad_phi)
            d_key[here, :] += grad
            far = dot((phi * keep).astype(jnp.bfloat16), table)
            d_heads[here, values_of(h)] = (d_values[here, head_at(h)] + far).astype(jnp.bfloat16)

        each_tile(through_out)
        d_heads[:, 0:q_wide] = d_query[...].astype(jnp.bfloat16)
        d_heads[:, q_wide : 2 * q_wide] = d_key[...].astype(jnp.bfloat16)
        pump(1)
        for j in range(Sum.pieces):
            columns = slice(j * piece, (j + 1) * piece)
            qkv_rows(j).wait()

            @pl.loop(0, rows // 256)
            def _(r):
                here = pl.ds(pl.multiple_of(r * 256, 256), 256)
                grad = dot(d_heads[here, :], w_qkv[j % 2], COLS)
                part[here, columns] = grad.astype(jnp.bfloat16)

            first_sum.near(j).start()
            if j + 2 < Sum.pieces:
                qkv_rows(j + 2).start()
            if j:
                first_sum.fold(j - 1)
        first_sum.fold(Sum.pieces - 1)

        pump(1)
        get_one.wait()

        def grad_qkv(columns):
            return dot(arena[:, columns], d_heads[...], BOTH)

        staged(tile_sem, tile_q, parts[4], grad_qkv)
        begin(s_qkv)
        s_down.final()
        pump(2)
        for j in range(Spread.pieces):
            act_spread.pass_on(j)
        to_pair.wait_send()
        pl.when(at.has_left)(lambda: to_left.wait_send())

    bf, f32 = jnp.bfloat16, jnp.float32
    pl.run_scoped(
        attention,
        pltpu.VMEM((rows, heads_h.shape[1]), bf),
        pltpu.VMEM((rows, heads_h.shape[1]), bf),
        pltpu.VMEM((rows, values_wide), bf),
        pltpu.VMEM(out_h.shape, bf),
        pltpu.VMEM((2, piece, qkv_h.shape[1]), bf),
        pltpu.VMEM((rows, 128), f32),
        pltpu.VMEM((heads_here, rows, 128), bf),
        pltpu.VMEM((heads_here, 8, rows), f32),
        pltpu.VMEM((rows, q_wide), f32),
        pltpu.VMEM((rows, q_wide), f32),
        pltpu.VMEM((2, maps.shape[2], maps.shape[2]), f32),
        pltpu.VMEM((2, 256, values_wide), bf),
        pltpu.VMEM((2, 256, heads_h.shape[1]), bf),
        pltpu.SemaphoreType.DMA((2,)),
        pltpu.VMEM((rows, values_wide), f32),
        pltpu.VMEM((2, act_spread.tall, width), f32),
        pltpu.SemaphoreType.DMA((2,)),
        pltpu.SemaphoreType.DMA((2,)),
    )

    quarter = pl.ds(pl.multiple_of(team.quarter_at, team.quarter), team.quarter)
    load(stream_h.at[quarter], arena.at[0 : team.quarter]).wait()
    first_sum.arrive()
    @pl.loop(0, team.quarter // 32)
    def _(r):
        start = pl.multiple_of(r * 32, 32)
        here = pl.ds(start, 32)
        x = arena[here, :].astype(f32)
        grad = norm_back(x, first_sum.rows(start, 32), gain.at[0], 0)
        arena[pl.ds(ig_rows + start, 32), :] = (d_mid[here, :] + grad).astype(bf)

    pump(1)
    gain_to_near = remote(gain_sum, gain_near, gain_send.at[0], gain_recv.at[0], team.near)
    gain_to_near.start()
    gain_to_near.wait()
    gain_sum[...] += gain_near[...]
    gain_to_far = remote(gain_sum, gain_far, gain_send.at[1], gain_recv.at[1], team.far)
    gain_to_far.start()
    for j in range(Spread.pieces):
        ig_spread.send(j)
    ig_spread.keep().start()
    gain_to_far.wait()
    gain_near[...] = gain_sum[...] + gain_far[...]
    deep = width // n
    for s in range(n):
        gain_parts[s] = gain_near[:, s * deep : (s + 1) * deep]
    load(gain_parts, parts[5]).wait()
    begin(s_gains)
    for j in range(Spread.pieces):
        pump(2)
        if j < 2:
            groups[1 + j].final()
        ig_spread.pass_on(j)
    pump.rest()
    for group in groups[3:]:
        group.final()
    for spread_of in (ig_spread, act_spread):
        spread_of.arrive()
        spread_of.drain()
        spread_of.keep().wait()
    spread.drain()
    first_sum.drain()
    for group in groups:
        group.drain()


def backward(n, lengths, maps, stream, cot, wholes, kept):
    rows, width = stream.shape
    gains, qkv, out, gate, up, down = wholes
    heads_here = out.shape[1] // 128
    hidden = gate.shape[1]
    tall = maps[1].shape[1]
    bf, f32 = jnp.bfloat16, jnp.float32
    shape = jax.ShapeDtypeStruct
    deep = width // n
    kinds = [
        ((deep, hidden), bf),
        ((deep, hidden), bf),
        ((deep, hidden), bf),
        ((deep, out.shape[1]), bf),
        ((deep, qkv.shape[1]), bf),
        ((16, deep), f32),
    ]
    results = [shape((rows, width), bf)] * 2 + [shape(*kind) for kind in kinds]
    work = [shape((width, size[1]), kind) for size, kind in kinds[1:-1]]
    work += [shape((n,) + kinds[-1][0], f32)]
    work += sum((Scatter.landing(n, *kind) for kind in kinds), [])
    state = (heads_here + 1, tall, 128)
    scratch = [
        pltpu.VMEM((rows, width), bf),
        pltpu.VMEM((rows, width), bf),
        pltpu.VMEM((rows // 4, width), f32),
        pltpu.VMEM((rows, width), bf),
        pltpu.VMEM(gains.shape, f32),
        pltpu.VMEM((2, 8, width), f32),
        pltpu.VMEM((16, width), f32),
        pltpu.VMEM((16, width), f32),
        pltpu.VMEM((16, width), f32),
        pltpu.VMEM((n, 16, deep), f32),
    ]
    scratch += [pltpu.VMEM(state, bf)] * 6
    scratch += [pltpu.SemaphoreType.DMA((2,))] * 4
    scratch += [pltpu.SemaphoreType.DMA((24,))]
    scratch += [pltpu.VMEM((2,) + kinds[k][0], kinds[k][1]) for k in (0, 3, 4, 5)]
    scratch += Sum.scratch(rows, width) * 2 + Sum.scratch(rows, width)[2:] + Spread.scratch() + SpreadOut.scratch() * 2
    scratch += sum((Scatter.scratch(n, *kind) for kind in kinds), [])
    anywhere, inside = pl.BlockSpec(memory_space=pl.ANY), pl.BlockSpec(memory_space=pltpu.VMEM)
    given = [stream, cot, *wholes, *kept]
    result = pl.pallas_call(
        functools.partial(backward_kernel, n),
        out_shape=results + work,
        in_specs=[pl.BlockSpec(memory_space=pltpu.SMEM)] + [inside] * 4 + [anywhere] * len(given),
        out_specs=[anywhere] * (len(results) + len(work)),
        scratch_shapes=scratch,
        compiler_params=pltpu.CompilerParams(
            collective_id=1, has_side_effects=True, vmem_limit_bytes=63 * MIB
        ),
    )(lengths, *maps, *given)
    return result[: len(results)]


def finish_kernel(q_wide, *refs):
    act_h, ig_h, down_h, gate_h, up_h, out_h, qkv_h, *refs = refs
    act_o, ig_o, query_o, key_o, value_o, out_o, gate_o, up_o, down_o, *refs = refs
    act, ig, down, gate, up, out, qkv, *refs = refs
    ig_f, down_f, gate_f, up_f, out_f, query_f, key_f, value_f, get_sem, put_sem = refs
    parts = 8
    rows = ig.shape[0] // parts

    def get_rows(j):
        here = pl.ds(j * rows, rows)
        return fetch(ig_h.at[here], ig.at[here], get_sem.at[j])

    def put_rows(j):
        here = pl.ds(j * rows, rows)
        return fetch(ig_f.at[here], ig_o.at[here], put_sem.at[j])

    get_act, put_act = fetch(act_h, act, get_sem.at[parts]), fetch(act, act_o, get_sem.at[parts])
    gets = [
        fetch(src, dst, get_sem.at[parts + 1 + k])
        for k, (src, dst) in enumerate(
            ((down_h, down), (gate_h, gate), (up_h, up), (out_h, out), (qkv_h, qkv))
        )
    ]
    for j in range(parts):
        get_rows(j).start()
    for get in gets:
        get.start()
    get_act.start()
    for j in range(parts):
        get_rows(j).wait()

        @pl.loop(0, rows // 32)
        def _(r):
            here = pl.ds(pl.multiple_of(j * rows + r * 32, 32), 32)
            ig_f[here, :] = ig[here, :].astype(jnp.float32)

        put_rows(j).start()
    get_act.wait()
    put_act.start()
    puts = []

    def put(src, dst):
        puts.append(fetch(src, dst, put_sem.at[parts + len(puts)]))
        puts[-1].start()

    for get, src, mid, dst in zip(
        gets, (down, gate, up, out), (down_f, gate_f, up_f, out_f), (down_o, gate_o, up_o, out_o)
    ):
        get.wait()
        mid[...] = src[...].astype(jnp.float32).T
        put(mid, dst)
    gets[4].wait()
    query_f[...] = qkv[:, 0:q_wide].astype(jnp.float32).T
    key_f[...] = qkv[:, q_wide : 2 * q_wide].astype(jnp.float32).T
    value_f[...] = qkv[:, 2 * q_wide :].astype(jnp.float32)
    put(query_f, query_o)
    put(key_f, key_o)
    put(value_f, value_o)
    for j in range(parts):
        put_rows(j).wait()
    for copy in puts:
        copy.wait()
    put_act.wait()


def finish(q_wide, act, ig, down, gate, up, out, qkv):
    f32 = jnp.float32
    deep, hidden = gate.shape
    values = out.shape[1]
    shapes = [
        ig.shape,
        (q_wide, deep),
        (q_wide, deep),
        (deep, values),
        (values, deep),
        (hidden, deep),
        (hidden, deep),
        (hidden, deep),
    ]
    anywhere = pl.BlockSpec(memory_space=pl.ANY)
    given = (act, ig, down, gate, up, out, qkv)
    order = (0, 7, 5, 6, 4, 1, 2, 3)
    return pl.pallas_call(
        functools.partial(finish_kernel, q_wide),
        out_shape=[jax.ShapeDtypeStruct(act.shape, act.dtype)]
        + [jax.ShapeDtypeStruct(a, f32) for a in shapes],
        in_specs=[anywhere] * len(given),
        out_specs=[anywhere] * 9,
        scratch_shapes=[pltpu.VMEM(a.shape, a.dtype) for a in given]
        + [pltpu.VMEM(shapes[k], f32) for k in order]
        + [pltpu.SemaphoreType.DMA((16,)), pltpu.SemaphoreType.DMA((16,))],
        compiler_params=pltpu.CompilerParams(vmem_limit_bytes=56 * MIB),
    )(*given)


def on_device(
    stream_in,
    doc_lengths,
    first_gain,
    w_query,
    w_key,
    w_value,
    w_out,
    second_gain,
    w_gate,
    w_up,
    w_down,
    cotangent,
):
    n = lax.axis_size("seq")
    f32 = jnp.float32
    q_wide = w_query.shape[1]
    gains_own = jnp.concatenate([first_gain, second_gain]).astype(f32)
    gains_own = jnp.broadcast_to(gains_own[None], (16, gains_own.shape[0]))
    maps = feature_maps(q_wide)
    shards = (gains_own, w_query.T, w_key.T, w_value, w_out, w_gate.T, w_up.T, w_down)
    wholes, kept = forward(n, doc_lengths, stream_in, cotangent, maps, shards)
    *results, g_gains = backward(n, doc_lengths, maps, stream_in, cotangent, wholes, kept)
    activations, input_grad, query, key, value, out, gate, up, down = finish(q_wide, *results)
    return (
        activations,
        input_grad,
        jnp.sum(g_gains[:8], axis=0),
        query.T,
        key.T,
        value,
        out,
        jnp.sum(g_gains[8:], axis=0),
        gate.T,
        up.T,
        down,
    )


def solution(mesh):
    placed = (
        P("seq", None),
        P(),
        P("seq"),
        P("seq", "tp"),
        P("seq", "tp"),
        P("seq", "tp"),
        P("tp", "seq"),
        P("seq"),
        P("seq", "tp"),
        P("seq", "tp"),
        P("tp", "seq"),
        P("seq", None),
    )
    return jax.shard_map(
        on_device,
        mesh=mesh,
        in_specs=placed,
        out_specs=(
            P("seq", None),
            P("seq", None),
            P("seq"),
            P("seq", "tp"),
            P("seq", "tp"),
            P("seq", "tp"),
            P("tp", "seq"),
            P("seq"),
            P("seq", "tp"),
            P("seq", "tp"),
            P("tp", "seq"),
        ),
        check_vma=False,
    )
```

```python
import functools

import jax
import jax.numpy as jnp
import numpy as np
from jax import lax
from jax.experimental import pallas as pl
from jax.experimental.pallas import tpu as pltpu
from jax.sharding import PartitionSpec as P

FEAT = 16
EPSILON = 1e-06
MESH = pl.DeviceIdType.MESH
MIB = 2**20
GATHER_CUT, SCATTER_CUT = 4, 4


def remote(src, dst, send, recv, device):
    return pltpu.make_async_remote_copy(
        src_ref=src,
        dst_ref=dst,
        send_sem=send,
        recv_sem=recv,
        device_id=device,
        device_id_type=MESH,
    )


class Place:
    def __init__(self, n):
        self.n, self.m = n, n // 2
        self.s, self.t = lax.axis_index("seq"), lax.axis_index("tp")
        self.o, self.i = self.s // 2, lax.rem(self.s, 2)
        self.right, self.left = (self.s + 2, self.t), (self.s - 2, self.t)
        self.pair = (self.o * 2 + 1 - self.i, self.t)
        self.has_right, self.has_left = self.o < self.m - 1, self.o > 0
        self.balanced = self.m >= 4
        m, o = self.m, self.o
        self.end = (o == 0) | (o == m - 1)
        self.next = (o == 1) | (o == m - 2)
        self.partner = jnp.where(
            o == 0, 1, jnp.where(o == m - 1, m - 2, jnp.where(o == 1, 0, m - 1))
        )

    def greet(self, others=()):
        barrier = pltpu.get_barrier_semaphore()

        def signal(device):
            pl.semaphore_signal(barrier, inc=1, device_id=device, device_id_type=MESH)

        pl.when(self.has_right)(lambda: signal(self.right))
        pl.when(self.has_left)(lambda: signal(self.left))
        signal(self.pair)
        for other in others:
            signal(other)
        beside = self.has_right.astype(jnp.int32) + self.has_left.astype(jnp.int32)
        pl.semaphore_wait(barrier, beside + (1 + len(others)))


class Gather:
    def __init__(self, at, own, held, sems, balanced):
        self.at, self.own_ref, self.held = at, own, held
        self.balanced = at.balanced and balanced
        self.send, self.recv, self.half_recv, self.local = sems

    @staticmethod
    def scratch(n):
        return [
            pltpu.SemaphoreType.DMA((3, n)),
            pltpu.SemaphoreType.DMA((n,)),
            pltpu.SemaphoreType.DMA((1,)),
            pltpu.SemaphoreType.DMA((1,)),
        ]

    def slot(self, slot, start=0, rows=None):
        if self.held.ndim == 3:
            return self.held.at[slot] if rows is None else self.held.at[slot, pl.ds(start, rows)]
        tall = self.own_ref.shape[0]
        first = pl.multiple_of(slot * tall, 16) + start
        return self.held.at[pl.ds(first, tall if rows is None else rows)]

    def copy(self, slot, way, own=False):
        at = self.at
        return remote(
            self.own_ref if own else self.slot(slot),
            self.slot(slot),
            self.send.at[way, slot],
            self.recv.at[slot],
            (at.right, at.left, at.pair)[way],
        )

    def half(self, slot, way, which):
        at, rows = self.at, self.own_ref.shape[0]
        cut = rows * GATHER_CUT // 8
        part = self.slot(slot, which * cut, (cut, rows - cut)[which])
        return remote(
            part,
            part,
            self.send.at[way, slot],
            self.recv.at[slot] if which == 0 else self.half_recv.at[0],
            (at.right, at.left, at.pair)[way],
        )

    def local_copy(self):
        return pltpu.make_async_copy(self.own_ref, self.slot(self.at.s), self.local.at[0])

    def own(self):
        at = self.at
        self.local_copy().start()
        pl.when(at.has_right)(lambda: self.copy(at.s, 0, True).start())
        pl.when(at.has_left)(lambda: self.copy(at.s, 1, True).start())
        self.copy(at.s, 2, True).start()

    def to_pair(self, slot, act):
        at = self.at
        if not self.balanced:
            act(self.copy(slot, 2))
            return
        partner = slot // 2 == at.partner
        pl.when(jnp.logical_not(partner & (at.end | at.next)))(lambda: act(self.copy(slot, 2)))
        pl.when(partner & at.end)(lambda: act(self.half(slot, 2, 0)))

    def step(self, k):
        at = self.at
        for way in (0, 1):
            slot = at.s - 2 * k if way == 0 else at.s + 2 * k
            there = at.o - k >= 0 if way == 0 else at.o + k < at.m
            on = at.has_right if way == 0 else at.has_left

            @pl.when(there)
            def _(slot=slot, on=on, way=way):
                self.copy(slot, 2).wait_recv()
                pl.when(on)(lambda: self.copy(slot, way).start())
                self.to_pair(slot, lambda c: c.start())

    def extra_copies(self, act):
        at = self.at
        slot = at.o * 2 + 1 - at.i
        pl.when(at.o == 0)(lambda: act(self.copy(slot, 0)))
        pl.when(at.o == at.m - 1)(lambda: act(self.copy(slot, 1)))
        pl.when(at.o == 1)(lambda: act(self.half(slot, 1, 1)))
        pl.when(at.o == at.m - 2)(lambda: act(self.half(slot, 0, 1)))

    def extra(self):
        at = self.at
        if self.balanced:
            slot = at.o * 2 + 1 - at.i
            pl.when(at.end | at.next)(lambda: self.copy(slot, 2).wait_recv())
            self.extra_copies(lambda c: c.start())

    def arrive(self):
        at = self.at
        self.local_copy().wait()
        for layer in range(at.m):
            slot = layer * 2 + 1 - at.i
            if not self.balanced:
                self.copy(slot, 2).wait_recv()
                continue
            met = (at.o == layer) & (at.end | at.next)
            halved = at.end & (at.partner == layer)
            pl.when(jnp.logical_not(met | halved))(lambda: self.copy(slot, 2).wait_recv())

            @pl.when(halved)
            def _():
                self.half(slot, 2, 0).wait_recv()
                self.half(slot, 2, 1).wait_recv()

    def drain(self):
        at = self.at
        pl.when(at.has_right)(lambda: self.copy(at.s, 0, True).wait_send())
        pl.when(at.has_left)(lambda: self.copy(at.s, 1, True).wait_send())
        self.copy(at.s, 2, True).wait_send()
        for k in range(1, at.m):
            for way in (0, 1):
                slot = at.s - 2 * k if way == 0 else at.s + 2 * k
                there = at.o - k >= 0 if way == 0 else at.o + k < at.m
                on = at.has_right if way == 0 else at.has_left

                @pl.when(there)
                def _(slot=slot, on=on, way=way):
                    pl.when(on)(lambda: self.copy(slot, way).wait_send())
                    self.to_pair(slot, lambda c: c.wait_send())

        if self.balanced:
            self.extra_copies(lambda c: c.wait_send())


def add_rows(total, part, start, rows):
    step = next(size for size in (64, 32, 16, 8) if rows % size == 0)

    @pl.loop(0, rows // step)
    def _(j):
        at = pl.ds(pl.multiple_of(start + j * step, 8), step)
        both = total[at, :].astype(jnp.float32) + part[at, :].astype(jnp.float32)
        total[at, :] = both.astype(total.dtype)


class Scatter:
    def __init__(self, at, parts, out, landing, bufs, sems, balanced):
        self.at, self.parts, self.out = at, parts, out
        self.balanced = at.balanced and balanced
        self.from_pair, self.from_line, self.shifted_in = landing
        self.mine, self.aside, self.stage = bufs
        (
            self.pair_send,
            self.pair_recv,
            self.line_send,
            self.line_recv,
            self.extra_send,
            self.extra_recv,
            self.local,
        ) = sems
        self.rows = self.mine.shape[1]
        self.cut = self.rows * SCATTER_CUT // 8

    @staticmethod
    def landing(n, shape, dtype):
        m = n // 2
        return [jax.ShapeDtypeStruct((size,) + shape, dtype) for size in (m, m + 1, 1)]

    @staticmethod
    def scratch(n, shape, dtype):
        m = n // 2
        return [pltpu.VMEM((size,) + shape, dtype) for size in (m, 1)] + [
            pltpu.SemaphoreType.DMA((m,)),
            pltpu.SemaphoreType.DMA((m,)),
            pltpu.SemaphoreType.DMA((m,)),
            pltpu.SemaphoreType.DMA((m + 1,)),
            pltpu.SemaphoreType.DMA((2,)),
            pltpu.SemaphoreType.DMA((2,)),
            pltpu.SemaphoreType.DMA((m + 4,)),
        ]

    def slot(self, slot):
        if self.parts.ndim == 3:
            return self.parts.at[slot]
        return self.parts.at[pl.ds(pl.multiple_of(slot * self.rows, 16), self.rows)]

    def load(self, layer):
        return pltpu.make_async_copy(
            self.slot(layer * 2 + self.at.i), self.mine.at[layer], self.local.at[layer]
        )

    def load_aside(self):
        at = self.at
        return pltpu.make_async_copy(
            self.slot(at.o * 2 + 1 - at.i), self.aside.at[0], self.local.at[at.m]
        )

    def store(self):
        at = self.at
        return pltpu.make_async_copy(self.mine.at[at.o], self.out, self.local.at[at.m + 1])

    def to_stage(self, src, which, start=0, rows=None):
        part = pl.ds(start, self.rows if rows is None else rows)
        return pltpu.make_async_copy(
            src.at[part], self.stage.at[which, part], self.local.at[self.at.m + 2 + which]
        )

    def to_pair(self, layer):
        return remote(
            self.slot(layer * 2 + 1 - self.at.i),
            self.from_pair.at[layer],
            self.pair_send.at[layer],
            self.pair_recv.at[layer],
            self.at.pair,
        )

    def half_to_pair(self, layer, which, src):
        cut = self.cut
        part = pl.ds(which * cut, (cut, self.rows - cut)[which])
        return remote(
            src.at[part],
            self.from_pair.at[layer, part],
            self.pair_send.at[layer] if which == 0 else self.extra_send.at[1],
            self.pair_recv.at[layer] if which == 0 else self.extra_recv.at[1],
            self.at.pair,
        )

    def sum_to_pair(self):
        return remote(
            self.aside.at[0],
            self.from_pair.at[self.at.o],
            self.pair_send.at[self.at.o],
            self.pair_recv.at[self.at.o],
            self.at.pair,
        )

    def along(self, layer, way):
        at = self.at
        there = layer if way == 0 else jnp.where(layer == at.o - 1, at.m, layer)
        return remote(
            self.mine.at[layer],
            self.from_line.at[there],
            self.line_send.at[layer],
            self.line_recv.at[there],
            (at.right, at.left)[way],
        )

    def wait_line(self, place):
        remote(
            self.mine.at[0],
            self.from_line.at[place],
            self.line_send.at[0],
            self.line_recv.at[place],
            self.at.right,
        ).wait_recv()

    def shifted(self, way, which=None):
        at, cut = self.at, self.cut
        src, dst = self.slot(at.partner * 2 + 1 - at.i), self.shifted_in.at[0]
        if which is not None:
            part = pl.ds(cut, self.rows - cut)
            src, dst = src.at[part], dst.at[part]
        return remote(
            src, dst, self.extra_send.at[0], self.extra_recv.at[0], (at.right, at.left)[way]
        )

    def far_first(self):
        at = self.at
        for d in range(at.m - 1, 0, -1):
            yield at.o + d, at.o + d < at.m
            yield at.o - d, at.o - d >= 0

    def pair_copies(self, act):
        at = self.at
        for layer, there in self.far_first():
            if not self.balanced:
                pl.when(there)(lambda: act(self.to_pair(layer)))
                continue
            partner = layer == at.partner
            pl.when(there & jnp.logical_not(partner & (at.end | at.next)))(
                lambda: act(self.to_pair(layer))
            )
            pl.when(there & partner & at.end)(
                lambda: act(self.half_to_pair(layer, 0, self.slot(layer * 2 + 1 - at.i)))
            )
        if not self.balanced:
            act(self.to_pair(at.o))
            return
        pl.when(jnp.logical_not(at.end | at.next))(lambda: act(self.to_pair(at.o)))
        pl.when(at.next)(
            lambda: act(self.half_to_pair(at.o, 0, self.slot(at.o * 2 + 1 - at.i)))
        )

    def shift_copies(self, act):
        at = self.at
        if self.balanced:
            pl.when(at.o == 0)(lambda: act(self.shifted(0, 1)))
            pl.when(at.o == at.m - 1)(lambda: act(self.shifted(1, 1)))
            pl.when(at.o == 1)(lambda: act(self.shifted(1)))
            pl.when(at.o == at.m - 2)(lambda: act(self.shifted(0)))

    def start(self):
        at = self.at
        self.shift_copies(lambda c: c.start())
        self.pair_copies(lambda c: c.start())
        for layer in range(at.m):
            self.load(layer).start()
        if self.balanced:
            self.load_aside().start()

    def extra(self):
        at = self.at
        if not self.balanced:
            return
        self.load_aside().wait()
        cut, landed = self.cut, self.shifted_in.at[0]
        left = self.rows - cut

        @pl.when(at.end)
        def _():
            self.shifted(0).wait_recv()
            self.to_stage(landed, 0).start()
            self.to_stage(landed, 0).wait()
            add_rows(self.aside.at[0], self.stage.at[0], 0, self.rows)
            self.sum_to_pair().start()

        @pl.when(at.next)
        def _():
            self.shifted(0, 1).wait_recv()
            self.to_stage(landed, 0, cut, left).start()
            self.to_stage(landed, 0, cut, left).wait()
            add_rows(self.aside.at[0], self.stage.at[0], cut, left)
            self.half_to_pair(at.o, 1, self.aside.at[0]).start()

    def wait_pair(self, layer):
        at = self.at
        if not self.balanced:
            self.to_pair(layer).wait_recv()
            return
        partner, own = layer == at.partner, layer == at.o
        parted = (partner & at.end) | (own & at.next)
        pl.when(jnp.logical_not((partner & (at.end | at.next)) | (own & at.next)))(
            lambda: self.to_pair(layer).wait_recv()
        )
        pl.when(parted)(lambda: self.half_to_pair(layer, 0, self.aside.at[0]).wait_recv())
        pl.when(own & at.next)(lambda: self.half_to_pair(layer, 1, self.aside.at[0]).wait_recv())

    def step(self, d):
        at = self.at
        for way in (0, 1):
            layer = at.o + d if way == 0 else at.o - d
            there = layer < at.m if way == 0 else layer >= 0
            behind = at.has_left if way == 0 else at.has_right

            @pl.when(there)
            def _(layer=layer, behind=behind, way=way):
                mine, paired, half = self.mine.at[layer], self.from_pair.at[layer], self.cut
                self.load(layer).wait()
                self.wait_pair(layer)
                partner = (layer == at.partner) & self.balanced
                whole = jnp.logical_not(partner & (at.end | at.next))
                halved = partner & at.end
                pl.when(whole)(lambda: self.to_stage(paired, 0).start())
                pl.when(halved)(lambda: self.to_stage(paired, 0, 0, half).start())

                @pl.when(behind)
                def _():
                    self.wait_line(layer)
                    self.to_stage(self.from_line.at[layer], 1).start()

                @pl.when(whole)
                def _():
                    self.to_stage(paired, 0).wait()
                    add_rows(mine, self.stage.at[0], 0, self.rows)

                @pl.when(halved)
                def _():
                    self.to_stage(paired, 0, 0, half).wait()
                    add_rows(mine, self.stage.at[0], 0, half)

                @pl.when(behind)
                def _():
                    self.to_stage(self.from_line.at[layer], 1).wait()
                    add_rows(mine, self.stage.at[1], 0, self.rows)

                self.along(layer, way).start()

    def final(self):
        at = self.at
        mine = self.mine.at[at.o]
        self.load(at.o).wait()
        self.wait_pair(at.o)
        self.to_stage(self.from_pair.at[at.o], 0).start()

        @pl.when(at.has_left)
        def _():
            self.wait_line(at.o)
            self.to_stage(self.from_line.at[at.o], 1).start()

        self.to_stage(self.from_pair.at[at.o], 0).wait()
        add_rows(mine, self.stage.at[0], 0, self.rows)

        @pl.when(at.has_right)
        def _():
            self.wait_line(at.m)
            self.to_stage(self.from_line.at[at.m], 0).start()

        @pl.when(at.has_left)
        def _():
            self.to_stage(self.from_line.at[at.o], 1).wait()
            add_rows(mine, self.stage.at[1], 0, self.rows)

        @pl.when(at.has_right)
        def _():
            self.to_stage(self.from_line.at[at.m], 0).wait()
            add_rows(mine, self.stage.at[0], 0, self.rows)

        self.store().start()

    def drain(self):
        at = self.at
        self.pair_copies(lambda c: c.wait_send())
        if self.balanced:
            pl.when(at.end)(lambda: self.sum_to_pair().wait_send())
            pl.when(at.next)(lambda: self.half_to_pair(at.o, 1, self.aside.at[0]).wait_send())
        self.shift_copies(lambda c: c.wait_send())
        for d in range(1, at.m):
            pl.when(at.o + d < at.m)(lambda: self.along(at.o + d, 0).wait_send())
            pl.when(at.o - d >= 0)(lambda: self.along(at.o - d, 1).wait_send())
        self.store().wait()


def fetch(src, dst, sem):
    return pltpu.make_async_copy(src, dst, sem)


def dot(a, b, dims=((1,), (0,))):
    return lax.dot_general(a, b, (dims, ((), ())), preferred_element_type=jnp.float32)


ROWS, COLS, BOTH = ((1,), (0,)), ((1,), (1,)), ((0,), (0,))


def row_start(lengths, position):
    at, start = jnp.int32(0), jnp.zeros_like(position)
    for k in range(lengths.shape[0]):
        start = jnp.maximum(start, jnp.where(at <= position, at, 0))
        at = at + lengths[k]
    return start


def lanes(shape):
    return lax.broadcasted_iota(jnp.int32, shape, len(shape) - 1)


def feature_maps(width):
    count = FEAT + 1 + FEAT * (FEAT + 1) // 2
    wide = -(-count // 128) * 128
    first, second = np.zeros((width, wide), np.float32), np.zeros((width, wide), np.float32)
    plus = np.zeros((3, wide), np.float32)
    plus[:, 0] = 1.0
    heads = np.arange(width // FEAT) * FEAT
    for i in range(FEAT):
        first[heads + i, 1 + i] = 1.0
        plus[1:, 1 + i] = 1.0, 0.25
    at = 1 + FEAT
    for i in range(FEAT):
        for j in range(i, FEAT):
            first[heads + i, at] = 1.0
            second[heads + j, at] = 1.0
            plus[2, at] = 1 / 32 if i == j else 1 / 16
            at += 1
    tall = -(-count // 16) * 16
    return (
        jnp.asarray(np.stack([first, second]), jnp.bfloat16),
        jnp.asarray(np.stack([first.T, second.T])[:, :tall], jnp.bfloat16),
        jnp.asarray(np.repeat(plus[:, None], 8, 1)),
        jnp.asarray(np.repeat(plus[:, :tall, None], 128, 2)),
    )


class Team:
    def __init__(self, at, rows):
        self.at, self.half, self.quarter = at, rows // 2, rows // 4
        t = at.t
        low, high = lax.rem(t, 2), t // 2
        self.near, self.far = (at.s, t + 1 - 2 * low), (at.s, lax.rem(t + 2, 4))
        self.half_at, self.other_half_at = low * self.half, (1 - low) * self.half
        self.quarter_at = self.half_at + high * self.quarter
        self.other_quarter_at = self.half_at + (1 - high) * self.quarter
        self.in_half, self.other_in_half = high * self.quarter, (1 - high) * self.quarter
        self.near_quarter_at = self.other_half_at + high * self.quarter
        self.near_other_at = self.other_half_at + (1 - high) * self.quarter


class Sum:
    pieces = 4

    def __init__(self, team, part, from_near, from_far, sems):
        self.team, self.part, self.from_near, self.from_far = team, part, from_near, from_far
        self.near_send, self.near_recv, self.far_send, self.far_recv = sems
        self.wide = part.shape[1] // self.pieces

    @staticmethod
    def scratch(rows, columns):
        return [
            pltpu.VMEM((rows // 2, columns), jnp.bfloat16),
            pltpu.VMEM((rows // 4, columns), jnp.bfloat16),
        ] + [pltpu.SemaphoreType.DMA((Sum.pieces,))] * 4

    def near(self, j):
        team, columns = self.team, pl.ds(j * self.wide, self.wide)
        return remote(
            self.part.at[pl.ds(pl.multiple_of(team.other_half_at, team.half), team.half), columns],
            self.from_near.at[:, columns],
            self.near_send.at[j],
            self.near_recv.at[j],
            team.near,
        )

    def far(self, j):
        team, columns = self.team, pl.ds(j * self.wide, self.wide)
        at = pl.multiple_of(team.other_quarter_at, team.quarter)
        return remote(
            self.part.at[pl.ds(at, team.quarter), columns],
            self.from_far.at[:, columns],
            self.far_send.at[j],
            self.far_recv.at[j],
            team.far,
        )

    def fold(self, j):
        team, columns = self.team, pl.ds(j * self.wide, self.wide)
        self.near(j).wait_recv()
        step = 64

        @pl.loop(0, team.quarter // step)
        def _(r):
            to = pl.ds(pl.multiple_of(team.other_quarter_at + r * step, step), step)
            of = pl.ds(pl.multiple_of(team.other_in_half + r * step, step), step)
            both = self.part[to, columns].astype(jnp.float32)
            both = both + self.from_near[of, columns].astype(jnp.float32)
            self.part[to, columns] = both.astype(jnp.bfloat16)

        self.far(j).start()

    def arrive(self):
        for j in range(self.pieces):
            self.far(j).wait_recv()

    def rows(self, start, count):
        team = self.team
        a = self.part[pl.ds(pl.multiple_of(team.quarter_at + start, 16), count), :]
        b = self.from_near[pl.ds(pl.multiple_of(team.in_half + start, 16), count), :]
        c = self.from_far[pl.ds(pl.multiple_of(start, 16), count), :]
        return a.astype(jnp.float32) + b.astype(jnp.float32) + c.astype(jnp.float32)

    def drain(self):
        for j in range(self.pieces):
            self.near(j).wait_send()
            self.far(j).wait_send()


class Spread:
    pieces = 4

    def __init__(self, team, whole, sems):
        self.team, self.whole = team, whole
        self.far_send, self.far_recv, self.near_send, self.near_recv, self.on_send, self.on_recv = (
            sems
        )
        self.tall = team.quarter // self.pieces

    @staticmethod
    def scratch():
        return [pltpu.SemaphoreType.DMA((Spread.pieces,))] * 6

    def copy(self, start, j, send, recv, device):
        rows = self.whole.at[pl.ds(pl.multiple_of(start + j * self.tall, self.tall), self.tall)]
        return remote(rows, rows, send.at[j], recv.at[j], device)

    def far(self, j):
        team = self.team
        return self.copy(team.quarter_at, j, self.far_send, self.far_recv, team.far)

    def near(self, j):
        team = self.team
        return self.copy(team.quarter_at, j, self.near_send, self.near_recv, team.near)

    def on(self, j):
        team = self.team
        return self.copy(team.other_quarter_at, j, self.on_send, self.on_recv, team.near)

    def send(self, j):
        self.far(j).start()
        self.near(j).start()

    def pass_on(self, j):
        self.far(j).wait_recv()
        self.on(j).start()

    def arrive(self):
        for j in range(self.pieces):
            self.near(j).wait_recv()
            self.on(j).wait_recv()

    def drain(self):
        for j in range(self.pieces):
            self.far(j).wait_send()
            self.near(j).wait_send()
            self.on(j).wait_send()


class Pump:
    def __init__(self, events):
        self.events = list(events)

    def __call__(self, count):
        for _ in range(min(count, len(self.events))):
            self.events.pop(0)()

    def until(self, event):
        while event in self.events:
            self.events.pop(0)()

    def rest(self):
        self(len(self.events))


def gain_row(gains, which, row):
    n, depth = gains.shape[0], gains.shape[2] // 2
    for s in range(n):
        part = gains[s, 0:8, which * depth : (which + 1) * depth]
        row[:, s * depth : (s + 1) * depth] = part


def scores(query, key, mask):
    s = dot(query, key, COLS) * 0.25
    return 1.0 + s, jnp.where(mask, 1.0 + s + 0.5 * s * s, 0.0)


def pair_mask(row_starts, column_starts, first_row, first_column):
    shape = (row_starts.shape[0], column_starts.shape[1])
    rows = lax.broadcasted_iota(jnp.int32, shape, 0) + first_row
    columns = lax.broadcasted_iota(jnp.int32, shape, 1) + first_column
    return (row_starts == column_starts) & (columns <= rows)


def of_head(values, h):
    lane = lanes((1, values.shape[1]))
    mine = (lane >= h * FEAT) & (lane < (h + 1) * FEAT)
    return jnp.where(mine, values, jnp.zeros_like(values))


def column(values, h):
    return jnp.sum(jnp.where(lanes((1, 128)) == h, values, 0.0), axis=1, keepdims=True)


def with_ones(values):
    return jnp.concatenate([values, jnp.ones_like(values)], axis=1)


def forward_kernel(n, sizes, *refs):
    (
        lengths, stream_h, cot_h, maps, maps_t, plus, plus_t,
        gains_own, query_h, key_h, value_h, out_raw_h, gate_raw_h, up_raw_h, down_raw_h,
        gains_h, qkv_h, out_h, gate_h, up_h, down_h,
        h_one_h, heads_h, mixed_h, rden_h, state_h, mid_h, h_two_h, gate_v_h, up_v_h, hid_h, part_h,
        query_own, key_own, value_own, out_raw, gate_raw, up_raw, down_raw,
        qkv_own, out_own, gate_own, up_own, down_own,
        stream, h_one, heads, w_qkv, w_out, mixed, rden, numer, mid, h_two, w_ff,
        gate_v, up_v, hid, part, gains, gain,
        t_own, t_pair, t_line, t_next, state, t_send, t_recv, local, part_sem,
        *sems,
    ) = refs
    rows, width = stream.shape
    heads_here = mixed.shape[1] // 128
    q_wide = heads_here * FEAT
    at = Place(n)
    team = Team(at, rows)
    near_sum, sems = sems[:6], sems[6:]
    spread_sems, sems = sems[:6], sems[6:]
    shards = (gains_own, qkv_own, out_own, gate_own, up_own, down_own)
    wholes = (gains_h, qkv_h, out_h, gate_h, up_h, down_h)
    groups = [
        Gather(at, shards[g], wholes[g], sems[4 * g : 4 * g + 4], g > 0)
        for g in range(len(shards))
    ]
    g_gains, g_qkv, g_out, g_gate, g_up, g_down = groups
    cell = iter(range(local.shape[0]))
    copies = []

    def load(src, dst):
        copy = fetch(src, dst, local.at[next(cell)])
        copy.start()
        return copy

    def save(src, dst):
        copies.append(load(src, dst))

    raw = [
        load(query_h, query_own),
        load(key_h, key_own),
        load(value_h, value_own),
        load(out_raw_h, out_raw),
        load(gate_raw_h, gate_raw),
        load(up_raw_h, up_raw),
        load(down_raw_h, down_raw),
    ]
    get_stream = load(stream_h, stream)
    at.greet((team.near, team.far))
    pump = Pump([])

    def queue(group, *steps):
        for k in steps:
            pump.events.append(functools.partial(group.step, k) if isinstance(k, int) else k)

    last = at.m - 1
    def values_here():
        pass

    queue(g_gains, 1)
    for k in range(2, last + 1):
        queue(g_gains, k)
        queue(g_qkv, k - 1)
        if k == 2:
            queue(g_qkv, g_qkv.extra)
    queue(g_gains, g_gains.extra, g_out.own)
    queue(g_qkv, last, values_here)
    queue(g_out, 1, *range(2, last), g_out.extra, last)

    def feed_forward_here():
        pass

    queue(g_gate, 1, g_gate.extra)
    for k in range(2, last + 1):
        queue(g_gate, k)
        queue(g_up, k - 1)
        if k == 2:
            queue(g_up, g_up.extra)
    queue(g_down, g_down.own)
    queue(g_up, last, feed_forward_here)
    queue(g_down, 1, g_down.extra, *range(2, last + 1))
    g_gains.own()
    for copy in raw[:3]:
        copy.wait()
    qkv_own[:, 0:q_wide] = query_own[...].T
    qkv_own[:, q_wide : 2 * q_wide] = key_own[...].T
    qkv_own[:, 2 * q_wide :] = value_own[...]
    g_qkv.own()
    for copy, turned, own in zip(
        raw[3:], (out_raw, gate_raw, up_raw, down_raw), (out_own, gate_own, up_own, down_own)
    ):
        copy.wait()
        own[...] = turned[...].T
    pump.until(g_gains.extra)
    g_gains.arrive()
    load(gains_h, gains).wait()
    gain_row(gains, 0, gain.at[0])
    gain_row(gains, 1, gain.at[1])
    get_stream.wait()

    @pl.loop(0, rows // 64)
    def _(j):
        here = pl.ds(pl.multiple_of(j * 64, 64), 64)
        x = stream[here, :].astype(jnp.float32)
        scale = lax.rsqrt(jnp.mean(x * x, axis=1, keepdims=True) + EPSILON)
        h_one[here, :] = (x * scale * gain[0, 0:1, :]).astype(jnp.bfloat16)

    save(h_one, h_one_h)
    pump.until(values_here)
    pump(1)
    g_gate.own()
    g_qkv.arrive()
    load(qkv_h, w_qkv).wait()

    @pl.loop(0, rows // 256)
    def _(j):
        here = pl.ds(pl.multiple_of(j * 256, 256), 256)
        heads[here, :] = dot(h_one[here, :], w_qkv[...]).astype(jnp.bfloat16)

    save(heads, heads_h)
    pump(1)
    first = at.s * rows
    starts_col = row_start(lengths, first + lax.broadcasted_iota(jnp.int32, (rows, 1), 0))
    starts_row = row_start(lengths, first + lax.broadcasted_iota(jnp.int32, (1, rows), 1))
    last = row_start(lengths, first + rows - 1)
    keep = jnp.where(starts_row == last, 1.0, 0.0)
    tall = t_own.shape[1]

    def values_of(h):
        return pl.ds(pl.multiple_of(2 * q_wide + h * 128, 128), 128)

    t_sum = numer.at[0, 0:tall, 0:128]
    t_sum[...] = jnp.zeros((tall, 128), jnp.float32)

    @pl.loop(0, heads_here)
    def _(h):
        key = of_head(heads[:, q_wide : 2 * q_wide], h)
        one = dot(maps_t[0], key, COLS) + plus_t[0][:, 0:1]
        two = dot(maps_t[1], key, COLS) + plus_t[1][:, 0:1]
        phi = (one * two * keep).astype(jnp.bfloat16)
        total = dot(phi, with_ones(heads[:, values_of(h)]))
        t_own[h] = total[:, :128].astype(jnp.bfloat16)
        t_sum[...] += jnp.where(lanes((tall, 128)) == h, total[:, 128:], 0.0)

    t_own[heads_here] = t_sum[...].astype(jnp.bfloat16)
    to_pair = remote(t_own, t_pair, t_send.at[0], t_recv.at[0], at.pair)
    to_right = remote(t_next, t_line, t_send.at[1], t_recv.at[1], at.right)
    to_pair.start()
    pump(1)
    tile = 256

    @pl.loop(0, heads_here)
    def _(h):
        key = heads[:, q_wide : 2 * q_wide]
        for j in range(rows // tile):
            upto = (j + 1) * tile
            query = of_head(heads[j * tile : upto, 0:q_wide], h)
            mask = pair_mask(starts_col[j * tile : upto], starts_row[:, :upto], j * tile, 0)
            _, weights = scores(query, key[:upto], mask)
            values = with_ones(heads[0:upto, values_of(h)])
            numer[h, j * tile : upto, :] = dot(weights.astype(jnp.bfloat16), values)

    pump(2)

    def closed(s):
        return jnp.where(row_start(lengths, (s + 1) * rows - 1) >= s * rows, 0.0, 1.0)

    on_one, on_two = closed(at.o * 2), closed(at.o * 2 + 1)

    @pl.when(at.o == 0)
    def _():
        t_line[...] = jnp.zeros_like(t_line)

    to_pair.wait_recv()
    pl.when(at.has_left)(lambda: to_right.wait_recv())
    for h in range(heads_here + 1):
        mine, other = t_own[h].astype(jnp.float32), t_pair[h].astype(jnp.float32)
        t_one, t_two = jnp.where(at.i == 0, mine, other), jnp.where(at.i == 0, other, mine)
        come = t_line[h].astype(jnp.float32)
        middle = t_one + on_one * come
        t_next[h] = (t_two + on_two * middle).astype(jnp.bfloat16)
        state[h] = jnp.where(at.i == 0, come, middle).astype(jnp.bfloat16)
    pl.when(at.has_right)(lambda: to_right.start())
    g_up.own()
    save(state, state_h)
    pump(2)

    rden[...] = jnp.zeros_like(rden)
    @pl.loop(0, heads_here)
    def _(h):
        own = lanes((tall, 128)) == h
        dens = jnp.sum(jnp.where(own, state[heads_here].astype(jnp.float32), 0.0), 1, keepdims=True)
        dens = jnp.broadcast_to(dens, (tall, 128)).astype(jnp.bfloat16)
        table = jnp.concatenate([state[h], dens], axis=1)
        table = jnp.concatenate(
            [table, jnp.zeros((maps.shape[2] - tall, 256), jnp.bfloat16)], axis=0
        )
        for j in range(rows // tile):
            here = slice(j * tile, (j + 1) * tile)
            query = of_head(heads[here, 0:q_wide], h)
            one = dot(query, maps[0]) + plus[0, 0:1, :]
            two = dot(query, maps[1]) + plus[1, 0:1, :]
            carried = jnp.where(starts_col[here] < first, 1.0, 0.0)
            phi = (one * two * plus[2, 0:1, :] * carried).astype(jnp.bfloat16)
            total = numer[h, here, :] + dot(phi, table)
            inverse = 1.0 / total[:, 128:]
            rden[here, :] = jnp.where(lanes((1, 128)) == h, inverse, rden[here, :])
            mixed[here, pl.ds(pl.multiple_of(h * 128, 128), 128)] = (
                total[:, :128] * inverse
            ).astype(jnp.bfloat16)

    save(mixed, mixed_h)
    save(rden, rden_h)
    pump.until(g_out.extra)
    g_out.arrive()
    load(out_h, w_out).wait()
    for copy in copies:
        copy.wait()
    copies.clear()

    part_sum = Sum(team, h_one, *near_sum[:2], near_sum[2:])
    for j in range(Sum.pieces):
        columns = slice(j * part_sum.wide, (j + 1) * part_sum.wide)

        @pl.loop(0, rows // 256)
        def _(r):
            here = pl.ds(pl.multiple_of(r * 256, 256), 256)
            h_one[here, columns] = dot(mixed[here, :], w_out[columns, :], COLS).astype(jnp.bfloat16)

        part_sum.near(j).start()
        if j:
            part_sum.fold(j - 1)
            pump(1)
    part_sum.fold(Sum.pieces - 1)
    part_sum.arrive()
    spread = Spread(team, h_two, spread_sems)
    for j in range(Spread.pieces):
        for k in range(spread.tall // 32):
            down = j * spread.tall + k * 32
            here = pl.ds(pl.multiple_of(team.quarter_at + down, 32), 32)
            x = part_sum.rows(down, 32) + stream[here, :].astype(jnp.float32)
            mid[down : down + 32, :] = x
            scale = lax.rsqrt(jnp.mean(x * x, axis=1, keepdims=True) + EPSILON)
            h_two[here, :] = (x * scale * gain[1, 0:1, :]).astype(jnp.bfloat16)
        spread.send(j)
    save(mid, mid_h)
    for j in range(Spread.pieces):
        pump((2, 1, 1, 1)[j])
        spread.pass_on(j)
    get_cot = load(cot_h, stream)
    spread.arrive()
    part_sum.drain()
    spread.drain()
    save(h_two, h_two_h)
    pump.until(feed_forward_here)
    g_gate.arrive()
    get_gate = load(gate_h, w_ff.at[0])
    g_up.arrive()
    load(up_h, w_ff.at[1]).wait()
    get_gate.wait()
    stages = 4
    for stage in range(stages):

        @pl.loop(0, rows // 128 // stages)
        def _(r):
            start = pl.multiple_of((stage * (rows // 128 // stages) + r) * 128, 128)
            here = pl.ds(start, 128)
            gate = dot(h_two[here, :], w_ff[0])
            up = dot(h_two[here, :], w_ff[1])
            hidden = gate * jax.nn.sigmoid(gate) * up
            gate_v[here, :] = gate.astype(jnp.bfloat16)
            up_v[here, :] = up.astype(jnp.bfloat16)
            hid[here, :] = hidden.astype(jnp.bfloat16)

        pump(1)
    save(gate_v, gate_v_h)
    save(up_v, up_v_h)
    save(hid, hid_h)
    get_cot.wait()
    def to_hbm(s, slot):
        here = pl.ds(pl.multiple_of(s * 256, 256), 256)
        return fetch(part.at[slot], part_h.at[here], part_sem.at[slot])

    count = width // 256
    for half in range(2):

        @pl.loop(half * (count // 2), (half + 1) * (count // 2))
        def _(s):
            slot = lax.rem(s, 2)
            pl.when(s > 1)(lambda: to_hbm(s - 2, slot).wait())
            columns = pl.ds(pl.multiple_of(s * 256, 256), 256)
            part[slot] = dot(stream[:, columns], hid[...], BOTH).astype(jnp.bfloat16)
            to_hbm(s, slot).start()

        pump(1)
    for s in range(count - 2, count):
        to_hbm(s, s % 2).wait()
    pump.rest()
    g_down.arrive()
    for group in groups:
        group.drain()
    to_pair.wait_send()
    pl.when(at.has_right)(lambda: to_right.wait_send())
    for copy in copies:
        copy.wait()


def forward(n, lengths, stream, cot, maps, shards):
    rows, width = stream.shape
    gains, query, key, value, out, gate, up, down = shards
    hidden, deep = gate.shape
    values = out.shape[0]
    qkv_wide = 2 * query.shape[0] + values
    heads_here = values // 128
    tall = maps[1].shape[1]
    bf, f32 = jnp.bfloat16, jnp.float32
    shape = jax.ShapeDtypeStruct
    wholes = [
        shape((n,) + gains.shape, f32),
        shape((width, qkv_wide), bf),
        shape((width, values), bf),
        shape((width, hidden), bf),
        shape((width, hidden), bf),
        shape((width, hidden), bf),
    ]
    kept = [
        shape((rows, width), bf),
        shape((rows, qkv_wide), bf),
        shape((rows, values), bf),
        shape((rows, 128), f32),
        shape((heads_here + 1, tall, 128), bf),
        shape((rows // 4, width), f32),
        shape((rows, width), bf),
        shape((rows, hidden), bf),
        shape((rows, hidden), bf),
        shape((rows, hidden), bf),
        shape((width, hidden), bf),
    ]
    state = (heads_here + 1, tall, 128)
    scratch = [pltpu.VMEM(a.shape, bf) for a in shards[1:]]
    scratch += [pltpu.VMEM((deep, wide), bf) for wide in (qkv_wide, values, hidden, hidden, hidden)]
    scratch += [
        pltpu.VMEM((rows, width), bf),
        pltpu.VMEM((rows, width), bf),
        pltpu.VMEM((rows, qkv_wide), bf),
        pltpu.VMEM((width, qkv_wide), bf),
        pltpu.VMEM((width, values), bf),
        pltpu.VMEM((rows, values), bf),
        pltpu.VMEM((rows, 128), f32),
        pltpu.VMEM((heads_here, rows, 256), f32),
        pltpu.VMEM((rows // 4, width), f32),
        pltpu.VMEM((rows, width), bf),
        pltpu.VMEM((2, width, hidden), bf),
        pltpu.VMEM((rows, hidden), bf),
        pltpu.VMEM((rows, hidden), bf),
        pltpu.VMEM((rows, hidden), bf),
        pltpu.VMEM((2, 256, hidden), bf),
        pltpu.VMEM((n,) + gains.shape, f32),
        pltpu.VMEM((2, 8, width), f32),
        pltpu.VMEM(state, bf),
        pltpu.VMEM(state, bf),
        pltpu.VMEM(state, bf),
        pltpu.VMEM(state, bf),
        pltpu.VMEM(state, bf),
        pltpu.SemaphoreType.DMA((2,)),
        pltpu.SemaphoreType.DMA((2,)),
        pltpu.SemaphoreType.DMA((32,)),
        pltpu.SemaphoreType.DMA((2,)),
    ]
    scratch += Sum.scratch(rows, width) + Spread.scratch() + Gather.scratch(n) * len(wholes)
    anywhere, inside = pl.BlockSpec(memory_space=pl.ANY), pl.BlockSpec(memory_space=pltpu.VMEM)
    result = pl.pallas_call(
        functools.partial(forward_kernel, n, None),
        out_shape=wholes + kept,
        in_specs=[pl.BlockSpec(memory_space=pltpu.SMEM), anywhere, anywhere]
        + [inside] * 4
        + [anywhere] * len(shards),
        out_specs=[anywhere] * (len(wholes) + len(kept)),
        scratch_shapes=scratch,
        compiler_params=pltpu.CompilerParams(
            collective_id=0, has_side_effects=True, vmem_limit_bytes=62 * MIB
        ),
    )(lengths, stream, cot, *maps, *shards)
    return result[: len(wholes)], result[len(wholes) :]


class SpreadOut(Spread):
    def __init__(self, team, quarter, whole, sems):
        super().__init__(team, whole, sems[:-1])
        self.own, self.kept = quarter, sems[-1]

    @staticmethod
    def scratch():
        return Spread.scratch() + [pltpu.SemaphoreType.DMA((1,))]

    def own_copy(self, j, send, recv, device):
        start = self.team.quarter_at + j * self.tall
        rows = self.whole.at[pl.ds(pl.multiple_of(start, self.tall), self.tall)]
        src = self.own.at[pl.ds(j * self.tall, self.tall)]
        return remote(src, rows, send.at[j], recv.at[j], device)

    def far(self, j):
        return self.own_copy(j, self.far_send, self.far_recv, self.team.far)

    def near(self, j):
        return self.own_copy(j, self.near_send, self.near_recv, self.team.near)

    def keep(self):
        team = self.team
        rows = self.whole.at[pl.ds(pl.multiple_of(team.quarter_at, team.quarter), team.quarter)]
        return pltpu.make_async_copy(self.own, rows, self.kept.at[0])


def backward_kernel(n, *refs):
    (
        lengths, maps, maps_t, plus, plus_t,
        stream_h, cot_h, gains_h, qkv_h, out_h, gate_h, up_h, down_h,
        h_one_h, heads_h, mixed_h, rden_h, state_h, mid_h, h_two_h, gate_v_h, up_v_h, hid_h, part_h,
        *refs,
    ) = refs
    act_h, ig_h, *refs = refs
    outs, refs = refs[:6], refs[6:]
    parts, refs = [part_h] + refs[:5], refs[5:]
    landings, refs = refs[:18], refs[18:]
    (
        part, arena, d_mid, dm, gains, gain, gain_sum, gain_near, gain_far, gain_parts,
        t_own, t_pair, t_line, t_next, state, back, t_send, t_recv, gain_send, gain_recv, local,
        stage_g, stage_o, stage_q, stage_n,
        *sems,
    ) = refs
    rows, width = arena.shape
    hidden = gate_v_h.shape[1]
    values_wide = mixed_h.shape[1]
    heads_here = values_wide // 128
    q_wide = heads_here * FEAT
    at = Place(n)
    team = Team(at, rows)

    def take(count):
        nonlocal sems
        taken, sems = sems[:count], sems[count:]
        return taken

    sums = [take(6) for _ in range(2)]
    first_sems = take(4)
    dm_sems, act_sems, ig_sems = take(6), take(7), take(7)
    stages = (stage_g, stage_g, stage_g, stage_o, stage_q, stage_n)
    groups = []
    for g in range(6):
        mine, aside, *own_sems = take(9)
        groups.append(
            Scatter(
                at,
                parts[g],
                outs[g],
                landings[3 * g : 3 * g + 3],
                (mine, aside, stages[g]),
                own_sems,
                g < 3,
            )
        )
    s_down, s_gate, s_up, s_out, s_qkv, s_gains = groups
    at.greet((team.near, team.far))
    cell = iter(range(local.shape[0]))

    def load(src, dst):
        copy = fetch(src, dst, local.at[next(cell)])
        copy.start()
        return copy

    pump = Pump([])

    def begin(group):
        group.start()
        for d in range(at.m - 1, 0, -1):
            pump.events.append(functools.partial(group.step, d))
            if d == max(1, at.m - 2) and group.balanced:
                pump.events.append(group.extra)

    begin(s_down)
    get_gains = load(gains_h, gains)
    get_mid = load(mid_h, d_mid)
    part_sum = Sum(team, part, *sums[0][:2], sums[0][2:])
    feed_sum = Sum(team, part, *sums[1][:2], sums[1][2:])
    first_sum = Sum(team, part, *sums[0][:2], first_sems)
    spread = Spread(team, dm, dm_sems)
    ig_rows = team.quarter
    ig_spread = SpreadOut(team, arena.at[pl.ds(ig_rows, team.quarter)], ig_h, ig_sems)
    act_spread = SpreadOut(team, feed_sum.from_far, act_h, act_sems)
    piece = part_sum.wide

    def staged(sem, tile, parts_h, compute):
        count = width // 256

        def to_hbm(s, slot):
            here = pl.ds(pl.multiple_of(s * 256, 256), 256)
            return fetch(tile.at[slot], parts_h.at[here], sem.at[slot])

        @pl.loop(0, count)
        def _(s):
            slot = lax.rem(s, 2)
            pl.when(s > 1)(lambda: to_hbm(s - 2, slot).wait())
            columns = pl.ds(pl.multiple_of(s * 256, 256), 256)
            tile[slot] = compute(columns).astype(jnp.bfloat16)
            to_hbm(s, slot).start()

        for s in range(count - 2, count):
            to_hbm(s, s % 2).wait()

    def norm_back(x, grad, gain_ref, which):
        scale = lax.rsqrt(jnp.mean(x * x, axis=1, keepdims=True) + EPSILON)
        unit = x * scale
        total = jnp.sum((grad * unit).reshape(-1, 8, width), axis=0)
        gain_sum[8 * which : 8 * which + 8, :] += total
        scaled = grad * gain_ref[0:1, :]
        return scale * (scaled - unit * jnp.mean(scaled * unit, axis=1, keepdims=True))

    gain_sum[...] = jnp.zeros_like(gain_sum)

    def feed_forward(w_down, w_ff, ff, w_sem, tile_sem):
        get_cot, get_down = load(cot_h, arena), load(down_h, w_down)
        get_gate, get_up = load(gate_v_h, ff.at[0]), load(up_v_h, ff.at[1])
        tall = w_ff.shape[2]

        def weights(j, which):
            here = pl.ds(j * tall, tall)
            return fetch(
                (gate_h, up_h)[which].at[here], w_ff.at[j % 2, which], w_sem.at[j % 2, which]
            )

        for which in (0, 1):
            weights(0, which).start()
        get_cot.wait()
        get_down.wait()
        get_gate.wait()
        get_up.wait()
        block = 256
        for low in range(0, hidden, 512):
            high = min(hidden, low + 512)

            @pl.loop(0, rows // block)
            def _(r):
                here = pl.ds(pl.multiple_of(r * block, block), block)
                grad = dot(arena[here, :], w_down[:, low:high])
                gate = ff[0, here, low:high].astype(jnp.float32)
                sigma = jax.nn.sigmoid(gate)
                silu = gate * sigma
                up = ff[1, here, low:high].astype(jnp.float32)
                ff[0, here, low:high] = (grad * up * (sigma + silu * (1.0 - sigma))).astype(
                    jnp.bfloat16
                )
                ff[1, here, low:high] = (grad * silu).astype(jnp.bfloat16)

        pump(1)
        get_two = load(h_two_h, arena)
        count = width // tall
        for j in range(count):
            for which in (0, 1):
                if j + 1 < count:
                    weights(j + 1, which).start()
                weights(j, which).wait()

            @pl.loop(0, rows // 512)
            def _(r):
                here = pl.ds(pl.multiple_of(r * 512, 512), 512)
                grad = dot(ff[0, here, :], w_ff[j % 2, 0], COLS)
                grad += dot(ff[1, here, :], w_ff[j % 2, 1], COLS)
                part[here, j * tall : (j + 1) * tall] = grad.astype(jnp.bfloat16)

            if (j + 1) * tall % piece == 0:
                p = (j + 1) * tall // piece - 1
                part_sum.near(p).start()
                if p:
                    part_sum.fold(p - 1)
        part_sum.fold(Sum.pieces - 1)
        get_two.wait()
        pump(2)
        tile = w_ff.at[0]

        def grads(which):
            return lambda columns: dot(arena[:, columns], ff[which], BOTH)

        staged(tile_sem, tile, parts[1], grads(0))
        begin(s_gate)
        get_gains.wait()
        gain_row(gains, 0, gain.at[0])
        gain_row(gains, 1, gain.at[1])
        get_mid.wait()
        part_sum.arrive()
        quarter = pl.ds(pl.multiple_of(team.quarter_at, team.quarter), team.quarter)
        load(cot_h.at[quarter], dm.at[quarter]).wait()
        for j in range(Spread.pieces):

            @pl.loop(0, spread.tall // 32)
            def _(r):
                start = pl.multiple_of(j * spread.tall + r * 32, 32)
                here = pl.ds(pl.multiple_of(team.quarter_at + start, 32), 32)
                x = d_mid[pl.ds(start, 32), :]
                grad = norm_back(x, part_sum.rows(start, 32), gain.at[1], 1)
                grad = grad + dm[here, :].astype(jnp.float32)
                d_mid[pl.ds(start, 32), :] = grad
                dm[here, :] = grad.astype(jnp.bfloat16)

            spread.send(j)
        part_sum.drain()
        pump(1)
        staged(tile_sem, tile, parts[2], grads(1))
        get_hid = load(hid_h, ff.at[0])
        get_hid.wait()
        for j in range(Sum.pieces):
            columns = slice(j * piece, (j + 1) * piece)

            @pl.loop(0, rows // 512)
            def _(r):
                here = pl.ds(pl.multiple_of(r * 512, 512), 512)
                feed = dot(ff[0, here, :], w_down[columns, :], COLS)
                part[here, columns] = feed.astype(jnp.bfloat16)

            feed_sum.near(j).start()
            spread.pass_on(j)
            if j == Sum.pieces - 2:
                pump(1)


    pl.run_scoped(
        feed_forward,
        pltpu.VMEM(down_h.shape, jnp.bfloat16),
        pltpu.VMEM((2, 2, 256, hidden), jnp.bfloat16),
        pltpu.VMEM((2, rows, hidden), jnp.bfloat16),
        pltpu.SemaphoreType.DMA((2, 2)),
        pltpu.SemaphoreType.DMA((2,)),
    )

    def attention(
        heads, d_heads, mixed, w_out, w_qkv, delta, g, delta_row, d_query, d_key,
        dens, tile_o, tile_q, tile_sem, d_values, mid_part, mid_sem, qkv_sem,
    ):
        gets = [
            load(heads_h, heads),
            load(mixed_h, mixed),
            load(out_h, w_out),
            load(rden_h, delta),
            load(state_h, state),
        ]
        get_one = load(h_one_h, arena)

        def mid_rows(j):
            here = pl.ds(j * act_spread.tall, act_spread.tall)
            return fetch(mid_h.at[here], mid_part.at[j % 2], mid_sem.at[j % 2])

        def qkv_rows(j):
            here = pl.ds(j * piece, piece)
            return fetch(qkv_h.at[here], w_qkv.at[j % 2], qkv_sem.at[j % 2])

        for j in range(2):
            mid_rows(j).start()
            qkv_rows(j).start()
        for get in gets:
            get.wait()
        spread.arrive()

        @pl.loop(0, rows // 256)
        def _(r):
            here = pl.ds(pl.multiple_of(r * 256, 256), 256)
            d_values[here, :] = dot(dm[here, :], w_out[...])

        for j in range(Sum.pieces):
            feed_sum.fold(j)

        @pl.loop(0, heads_here)
        def _(h):
            across = pl.ds(pl.multiple_of(h * 128, 128), 128)
            grad = d_values[:, across] * column(delta[...], h)
            g[h] = grad.astype(jnp.bfloat16)
            sums_of = jnp.sum(grad * mixed[:, across].astype(jnp.float32), axis=1, keepdims=True)
            wide = jnp.broadcast_to(sums_of, (rows, 128))
            delta[...] = jnp.where(lanes((1, 128)) == h, wide, delta[...])
            delta_row[h] = wide.T[0:8]

        first = at.s * rows
        starts_col = row_start(lengths, first + lax.broadcasted_iota(jnp.int32, (rows, 1), 0))
        starts_row = row_start(lengths, first + lax.broadcasted_iota(jnp.int32, (1, rows), 1))
        last = row_start(lengths, first + rows - 1)
        tall = t_own.shape[1]
        wide = maps.shape[2]
        carried_row = jnp.where(starts_row < first, 1.0, 0.0)
        dens[1, 0:tall, 0:128] = jnp.zeros((tall, 128), jnp.float32)

        def values_of(h):
            return pl.ds(pl.multiple_of(2 * q_wide + h * 128, 128), 128)

        def head_at(h):
            return pl.ds(pl.multiple_of(h * 128, 128), 128)

        @pl.loop(0, heads_here)
        def _(h):
            query = of_head(heads[:, 0:q_wide], h)
            one = dot(maps_t[0], query, COLS) + plus_t[0][:, 0:1]
            two = dot(maps_t[1], query, COLS) + plus_t[1][:, 0:1]
            phi = one * two * plus_t[2][:, 0:1] * carried_row
            t_own[h] = dot(phi.astype(jnp.bfloat16), g[h]).astype(jnp.bfloat16)
            below = -jnp.sum(phi * delta_row[h][0:1, :], axis=1, keepdims=True)
            dens[1, 0:tall, 0:128] += jnp.where(lanes((tall, 128)) == h, below, 0.0)

        t_own[heads_here] = dens[1, 0:tall, 0:128].astype(jnp.bfloat16)
        to_pair = remote(t_own, t_pair, t_send.at[0], t_recv.at[0], at.pair)
        to_left = remote(t_next, t_line, t_send.at[1], t_recv.at[1], at.left)
        to_pair.start()
        begin(s_up)

        @pl.when(at.o == at.m - 1)
        def _():
            t_line[...] = jnp.zeros_like(t_line)

        def closed(s):
            return jnp.where(row_start(lengths, (s + 1) * rows - 1) >= s * rows, 0.0, 1.0)

        on_one, on_two = closed(at.o * 2), closed(at.o * 2 + 1)

        def relay():
            to_pair.wait_recv()
            pl.when(at.has_right)(lambda: to_left.wait_recv())

            @pl.loop(0, heads_here + 1)
            def _(h):
                mine, other = t_own[h].astype(jnp.float32), t_pair[h].astype(jnp.float32)
                t_one, t_two = jnp.where(at.i == 0, mine, other), jnp.where(at.i == 0, other, mine)
                come = t_line[h].astype(jnp.float32)
                middle = t_two + on_two * come
                t_next[h] = (t_one + on_one * middle).astype(jnp.bfloat16)
                back[h] = jnp.where(at.i == 0, middle, come).astype(jnp.bfloat16)

            pl.when(at.has_left)(lambda: to_left.start())

        turns = min(4, at.m)

        def turn(p):
            mine = at.o == at.m - 1 - p if p < turns - 1 else at.o <= at.m - turns
            pl.when(mine)(relay)

        d_query[...] = jnp.zeros_like(d_query)
        d_key[...] = jnp.zeros_like(d_key)
        tile = 128

        def intra(h):
            key, query = of_head(heads[:, q_wide : 2 * q_wide], h), of_head(heads[:, 0:q_wide], h)
            across = values_of(h)
            for j in range(rows // tile):
                here, upto = slice(j * tile, (j + 1) * tile), (j + 1) * tile
                mask = pair_mask(starts_col[here], starts_row[:, :upto], j * tile, 0)
                more, _ = scores(query[here], key[:upto], mask)
                d_weight = dot(g[h, here, :], heads[0:upto, across], COLS) - column(delta[here, :], h)
                d_score = jnp.where(mask, d_weight * more, 0.0).astype(jnp.bfloat16)
                d_query[here, :] += dot(d_score, key[:upto]) * 0.25
            for j in range(rows // tile):
                here, after = slice(j * tile, (j + 1) * tile), j * tile
                shape = (tile, rows - after)
                key_at = lax.broadcasted_iota(jnp.int32, shape, 0)
                query_at = lax.broadcasted_iota(jnp.int32, shape, 1)
                mask = (starts_col[here] == starts_row[:, after:]) & (key_at <= query_at)
                more, weight = scores(key[here], query[after:], mask)
                d_weight = dot(heads[here, across], g[h, after:, :], COLS)
                d_weight = d_weight - delta_row[h, 0:1, after:]
                d_score = jnp.where(mask, d_weight * more, 0.0).astype(jnp.bfloat16)
                d_values[here, head_at(h)] = dot(weight.astype(jnp.bfloat16), g[h, after:, :])
                grad = dot(d_score, query[after:]) * 0.25
                d_key[here, :] = jnp.where(h == 0, grad, d_key[here, :] + grad)

        for half in range(2):
            @pl.loop(half * heads_here // 2, (half + 1) * heads_here // 2)
            def _(h):
                intra(h)

            if half == 0:
                pump(1)
        turn(0)
        pump(1)

        def through(u, h, grad):
            one = dot(u, maps[0]) + plus[0, 0:1, :]
            two = dot(u, maps[1]) + plus[1, 0:1, :]
            grad = grad()
            left = dot((grad * two).astype(jnp.bfloat16), maps[0], COLS)
            left += dot((grad * one).astype(jnp.bfloat16), maps[1], COLS)
            return one * two, of_head(left, h)

        wider = 256

        def each_tile(body):
            @pl.loop(0, heads_here)
            def _(h):
                @pl.loop(0, rows // wider)
                def _(j):
                    here = pl.ds(pl.multiple_of(j * wider, wider), wider)
                    at_row = first + j * wider + lax.broadcasted_iota(jnp.int32, (wider, 1), 0)
                    body(h, here, row_start(lengths, at_row))

        filler = jnp.zeros((wide - tall, 128), jnp.bfloat16)
        dens[0] = jnp.zeros_like(dens[0])
        dens[0, 0:128, 0:tall] = state[heads_here].astype(jnp.float32).T

        def through_in(h, here, starts):
            carried = jnp.where(starts < first, 1.0, 0.0)

            def grad_phi():
                table = jnp.concatenate([state[h], filler], axis=0)
                grad = dot(g[h, here, :], table, COLS)
                grad = grad - column(delta[here, :], h) * dens[0, pl.ds(h, 1), :]
                return grad * plus[2, 0:1, :] * carried

            _, grad = through(of_head(heads[here, 0:q_wide], h), h, grad_phi)
            d_query[here, :] += grad

        each_tile(through_in)
        turn(1)
        pump(1)

        def grad_out(columns):
            return dot(dm[:, columns], mixed[...], BOTH)

        staged(tile_sem, tile_o, parts[3], grad_out)
        begin(s_out)
        turn(2)
        pump(1)
        feed_sum.arrive()
        for j in range(Spread.pieces):
            mid_rows(j).wait()

            @pl.loop(0, act_spread.tall // 32)
            def _(r):
                start = pl.multiple_of(j * act_spread.tall + r * 32, 32)
                x = mid_part[j % 2, pl.ds(pl.multiple_of(r * 32, 32), 32), :]
                x = x + feed_sum.rows(start, 32)
                feed_sum.from_far[pl.ds(start, 32), :] = x.astype(bf)

            if j + 2 < Spread.pieces:
                mid_rows(j + 2).start()
            act_spread.send(j)
        act_spread.keep().start()
        feed_sum.drain()
        for p in range(3, turns):
            turn(p)

        dens[1] = jnp.zeros_like(dens[1])
        dens[1, 0:128, 0:tall] = back[heads_here].astype(jnp.float32).T

        def through_out(h, here, starts):
            keep = jnp.where(starts == last, 1.0, 0.0)
            table = jnp.concatenate([back[h], filler], axis=0)

            def grad_phi():
                grad = dot(heads[here, values_of(h)], table, COLS)
                return (grad + dens[1, pl.ds(h, 1), :]) * keep

            phi, grad = through(of_head(heads[here, q_wide : 2 * q_wide], h), h, grad_phi)
            d_key[here, :] += grad
            far = dot((phi * keep).astype(jnp.bfloat16), table)
            d_heads[here, values_of(h)] = (d_values[here, head_at(h)] + far).astype(jnp.bfloat16)

        each_tile(through_out)
        d_heads[:, 0:q_wide] = d_query[...].astype(jnp.bfloat16)
        d_heads[:, q_wide : 2 * q_wide] = d_key[...].astype(jnp.bfloat16)
        pump(2)
        for j in range(Sum.pieces):
            columns = slice(j * piece, (j + 1) * piece)
            qkv_rows(j).wait()

            @pl.loop(0, rows // 256)
            def _(r):
                here = pl.ds(pl.multiple_of(r * 256, 256), 256)
                grad = dot(d_heads[here, :], w_qkv[j % 2], COLS)
                part[here, columns] = grad.astype(jnp.bfloat16)

            first_sum.near(j).start()
            if j + 2 < Sum.pieces:
                qkv_rows(j + 2).start()
            if j:
                first_sum.fold(j - 1)
        first_sum.fold(Sum.pieces - 1)

        pump(1)
        get_one.wait()

        def grad_qkv(columns):
            return dot(arena[:, columns], d_heads[...], BOTH)

        staged(tile_sem, tile_q, parts[4], grad_qkv)
        pump(1)
        begin(s_qkv)
        s_down.final()
        for j in range(Spread.pieces):
            act_spread.pass_on(j)
        to_pair.wait_send()
        pl.when(at.has_left)(lambda: to_left.wait_send())

    bf, f32 = jnp.bfloat16, jnp.float32
    pl.run_scoped(
        attention,
        pltpu.VMEM((rows, heads_h.shape[1]), bf),
        pltpu.VMEM((rows, heads_h.shape[1]), bf),
        pltpu.VMEM((rows, values_wide), bf),
        pltpu.VMEM(out_h.shape, bf),
        pltpu.VMEM((2, piece, qkv_h.shape[1]), bf),
        pltpu.VMEM((rows, 128), f32),
        pltpu.VMEM((heads_here, rows, 128), bf),
        pltpu.VMEM((heads_here, 8, rows), f32),
        pltpu.VMEM((rows, q_wide), f32),
        pltpu.VMEM((rows, q_wide), f32),
        pltpu.VMEM((2, maps.shape[2], maps.shape[2]), f32),
        pltpu.VMEM((2, 256, values_wide), bf),
        pltpu.VMEM((2, 256, heads_h.shape[1]), bf),
        pltpu.SemaphoreType.DMA((2,)),
        pltpu.VMEM((rows, values_wide), f32),
        pltpu.VMEM((2, act_spread.tall, width), f32),
        pltpu.SemaphoreType.DMA((2,)),
        pltpu.SemaphoreType.DMA((2,)),
    )

    quarter = pl.ds(pl.multiple_of(team.quarter_at, team.quarter), team.quarter)
    load(stream_h.at[quarter], arena.at[0 : team.quarter]).wait()
    first_sum.arrive()
    @pl.loop(0, team.quarter // 32)
    def _(r):
        start = pl.multiple_of(r * 32, 32)
        here = pl.ds(start, 32)
        x = arena[here, :].astype(f32)
        grad = norm_back(x, first_sum.rows(start, 32), gain.at[0], 0)
        arena[pl.ds(ig_rows + start, 32), :] = (d_mid[here, :] + grad).astype(bf)

    pump(1)
    gain_to_near = remote(gain_sum, gain_near, gain_send.at[0], gain_recv.at[0], team.near)
    gain_to_near.start()
    gain_to_near.wait()
    gain_sum[...] += gain_near[...]
    gain_to_far = remote(gain_sum, gain_far, gain_send.at[1], gain_recv.at[1], team.far)
    gain_to_far.start()
    for j in range(Spread.pieces):
        ig_spread.send(j)
    ig_spread.keep().start()
    pump(1)
    gain_to_far.wait()
    gain_near[...] = gain_sum[...] + gain_far[...]
    deep = width // n
    for s in range(n):
        gain_parts[s] = gain_near[:, s * deep : (s + 1) * deep]
    load(gain_parts, parts[5]).wait()
    begin(s_gains)
    pump(1)
    s_gate.final()
    pump(1)
    s_up.final()
    pump.rest()
    for group in groups[3:]:
        group.final()
    for j in range(Spread.pieces):
        ig_spread.pass_on(j)
    for spread_of in (ig_spread, act_spread):
        spread_of.arrive()
        spread_of.drain()
        spread_of.keep().wait()
    spread.drain()
    first_sum.drain()
    for group in groups:
        group.drain()


def backward(n, lengths, maps, stream, cot, wholes, kept):
    rows, width = stream.shape
    gains, qkv, out, gate, up, down = wholes
    heads_here = out.shape[1] // 128
    hidden = gate.shape[1]
    tall = maps[1].shape[1]
    bf, f32 = jnp.bfloat16, jnp.float32
    shape = jax.ShapeDtypeStruct
    deep = width // n
    kinds = [
        ((deep, hidden), bf),
        ((deep, hidden), bf),
        ((deep, hidden), bf),
        ((deep, out.shape[1]), bf),
        ((deep, qkv.shape[1]), bf),
        ((16, deep), f32),
    ]
    results = [shape((rows, width), bf)] * 2 + [shape(*kind) for kind in kinds]
    work = [shape((width, size[1]), kind) for size, kind in kinds[1:-1]]
    work += [shape((n,) + kinds[-1][0], f32)]
    work += sum((Scatter.landing(n, *kind) for kind in kinds), [])
    state = (heads_here + 1, tall, 128)
    scratch = [
        pltpu.VMEM((rows, width), bf),
        pltpu.VMEM((rows, width), bf),
        pltpu.VMEM((rows // 4, width), f32),
        pltpu.VMEM((rows, width), bf),
        pltpu.VMEM(gains.shape, f32),
        pltpu.VMEM((2, 8, width), f32),
        pltpu.VMEM((16, width), f32),
        pltpu.VMEM((16, width), f32),
        pltpu.VMEM((16, width), f32),
        pltpu.VMEM((n, 16, deep), f32),
    ]
    scratch += [pltpu.VMEM(state, bf)] * 6
    scratch += [pltpu.SemaphoreType.DMA((2,))] * 4
    scratch += [pltpu.SemaphoreType.DMA((24,))]
    scratch += [pltpu.VMEM((2,) + kinds[k][0], kinds[k][1]) for k in (0, 3, 4, 5)]
    scratch += Sum.scratch(rows, width) * 2 + Sum.scratch(rows, width)[2:] + Spread.scratch() + SpreadOut.scratch() * 2
    scratch += sum((Scatter.scratch(n, *kind) for kind in kinds), [])
    anywhere, inside = pl.BlockSpec(memory_space=pl.ANY), pl.BlockSpec(memory_space=pltpu.VMEM)
    given = [stream, cot, *wholes, *kept]
    result = pl.pallas_call(
        functools.partial(backward_kernel, n),
        out_shape=results + work,
        in_specs=[pl.BlockSpec(memory_space=pltpu.SMEM)] + [inside] * 4 + [anywhere] * len(given),
        out_specs=[anywhere] * (len(results) + len(work)),
        scratch_shapes=scratch,
        compiler_params=pltpu.CompilerParams(
            collective_id=1, has_side_effects=True, vmem_limit_bytes=63 * MIB
        ),
    )(lengths, *maps, *given)
    return result[: len(results)]


def finish_kernel(q_wide, *refs):
    act_h, ig_h, down_h, gate_h, up_h, out_h, qkv_h, *refs = refs
    act_o, ig_o, query_o, key_o, value_o, out_o, gate_o, up_o, down_o, *refs = refs
    act, ig, down, gate, up, out, qkv, *refs = refs
    ig_f, down_f, gate_f, up_f, out_f, query_f, key_f, value_f, get_sem, put_sem = refs
    parts = 8
    rows = ig.shape[0] // parts

    def get_rows(j):
        here = pl.ds(j * rows, rows)
        return fetch(ig_h.at[here], ig.at[here], get_sem.at[j])

    def put_rows(j):
        here = pl.ds(j * rows, rows)
        return fetch(ig_f.at[here], ig_o.at[here], put_sem.at[j])

    get_act, put_act = fetch(act_h, act, get_sem.at[parts]), fetch(act, act_o, get_sem.at[parts])
    gets = [
        fetch(src, dst, get_sem.at[parts + 1 + k])
        for k, (src, dst) in enumerate(
            ((down_h, down), (gate_h, gate), (up_h, up), (out_h, out), (qkv_h, qkv))
        )
    ]
    for j in range(parts):
        get_rows(j).start()
    for get in gets:
        get.start()
    get_act.start()
    for j in range(parts):
        get_rows(j).wait()

        @pl.loop(0, rows // 32)
        def _(r):
            here = pl.ds(pl.multiple_of(j * rows + r * 32, 32), 32)
            ig_f[here, :] = ig[here, :].astype(jnp.float32)

        put_rows(j).start()
    get_act.wait()
    put_act.start()
    puts = []

    def put(src, dst):
        puts.append(fetch(src, dst, put_sem.at[parts + len(puts)]))
        puts[-1].start()

    for get, src, mid, dst in zip(
        gets, (down, gate, up, out), (down_f, gate_f, up_f, out_f), (down_o, gate_o, up_o, out_o)
    ):
        get.wait()
        mid[...] = src[...].astype(jnp.float32).T
        put(mid, dst)
    gets[4].wait()
    query_f[...] = qkv[:, 0:q_wide].astype(jnp.float32).T
    key_f[...] = qkv[:, q_wide : 2 * q_wide].astype(jnp.float32).T
    value_f[...] = qkv[:, 2 * q_wide :].astype(jnp.float32)
    put(query_f, query_o)
    put(key_f, key_o)
    put(value_f, value_o)
    for j in range(parts):
        put_rows(j).wait()
    for copy in puts:
        copy.wait()
    put_act.wait()


def finish(q_wide, act, ig, down, gate, up, out, qkv):
    f32 = jnp.float32
    deep, hidden = gate.shape
    values = out.shape[1]
    shapes = [
        ig.shape,
        (q_wide, deep),
        (q_wide, deep),
        (deep, values),
        (values, deep),
        (hidden, deep),
        (hidden, deep),
        (hidden, deep),
    ]
    anywhere = pl.BlockSpec(memory_space=pl.ANY)
    given = (act, ig, down, gate, up, out, qkv)
    order = (0, 7, 5, 6, 4, 1, 2, 3)
    return pl.pallas_call(
        functools.partial(finish_kernel, q_wide),
        out_shape=[jax.ShapeDtypeStruct(act.shape, act.dtype)]
        + [jax.ShapeDtypeStruct(a, f32) for a in shapes],
        in_specs=[anywhere] * len(given),
        out_specs=[anywhere] * 9,
        scratch_shapes=[pltpu.VMEM(a.shape, a.dtype) for a in given]
        + [pltpu.VMEM(shapes[k], f32) for k in order]
        + [pltpu.SemaphoreType.DMA((16,)), pltpu.SemaphoreType.DMA((16,))],
        compiler_params=pltpu.CompilerParams(vmem_limit_bytes=56 * MIB),
    )(*given)


def on_device(
    stream_in,
    doc_lengths,
    first_gain,
    w_query,
    w_key,
    w_value,
    w_out,
    second_gain,
    w_gate,
    w_up,
    w_down,
    cotangent,
):
    n = lax.axis_size("seq")
    f32 = jnp.float32
    q_wide = w_query.shape[1]
    gains_own = jnp.concatenate([first_gain, second_gain]).astype(f32)
    gains_own = jnp.broadcast_to(gains_own[None], (16, gains_own.shape[0]))
    maps = feature_maps(q_wide)
    shards = (gains_own, w_query.T, w_key.T, w_value, w_out, w_gate.T, w_up.T, w_down)
    wholes, kept = forward(n, doc_lengths, stream_in, cotangent, maps, shards)
    *results, g_gains = backward(n, doc_lengths, maps, stream_in, cotangent, wholes, kept)
    activations, input_grad, query, key, value, out, gate, up, down = finish(q_wide, *results)
    return (
        activations,
        input_grad,
        jnp.sum(g_gains[:8], axis=0),
        query.T,
        key.T,
        value,
        out,
        jnp.sum(g_gains[8:], axis=0),
        gate.T,
        up.T,
        down,
    )


def solution(mesh):
    placed = (
        P("seq", None),
        P(),
        P("seq"),
        P("seq", "tp"),
        P("seq", "tp"),
        P("seq", "tp"),
        P("tp", "seq"),
        P("seq"),
        P("seq", "tp"),
        P("seq", "tp"),
        P("tp", "seq"),
        P("seq", None),
    )
    return jax.shard_map(
        on_device,
        mesh=mesh,
        in_specs=placed,
        out_specs=(
            P("seq", None),
            P("seq", None),
            P("seq"),
            P("seq", "tp"),
            P("seq", "tp"),
            P("seq", "tp"),
            P("tp", "seq"),
            P("seq"),
            P("seq", "tp"),
            P("seq", "tp"),
            P("tp", "seq"),
        ),
        check_vma=False,
    )
```

```python
import functools

import jax
import jax.numpy as jnp
import numpy as np
from jax import lax
from jax.experimental import pallas as pl
from jax.experimental.pallas import tpu as pltpu
from jax.sharding import PartitionSpec as P

FEAT = 16
EPSILON = 1e-06
MESH = pl.DeviceIdType.MESH
MIB = 2**20
GATHER_CUT, SCATTER_CUT = 4, 4


def remote(src, dst, send, recv, device):
    return pltpu.make_async_remote_copy(
        src_ref=src,
        dst_ref=dst,
        send_sem=send,
        recv_sem=recv,
        device_id=device,
        device_id_type=MESH,
    )


class Place:
    def __init__(self, n):
        self.n, self.m = n, n // 2
        self.s, self.t = lax.axis_index("seq"), lax.axis_index("tp")
        self.o, self.i = self.s // 2, lax.rem(self.s, 2)
        self.right, self.left = (self.s + 2, self.t), (self.s - 2, self.t)
        self.pair = (self.o * 2 + 1 - self.i, self.t)
        self.has_right, self.has_left = self.o < self.m - 1, self.o > 0
        self.balanced = self.m >= 4
        m, o = self.m, self.o
        self.end = (o == 0) | (o == m - 1)
        self.next = (o == 1) | (o == m - 2)
        self.partner = jnp.where(
            o == 0, 1, jnp.where(o == m - 1, m - 2, jnp.where(o == 1, 0, m - 1))
        )

    def greet(self, others=()):
        barrier = pltpu.get_barrier_semaphore()

        def signal(device):
            pl.semaphore_signal(barrier, inc=1, device_id=device, device_id_type=MESH)

        pl.when(self.has_right)(lambda: signal(self.right))
        pl.when(self.has_left)(lambda: signal(self.left))
        signal(self.pair)
        for other in others:
            signal(other)
        beside = self.has_right.astype(jnp.int32) + self.has_left.astype(jnp.int32)
        pl.semaphore_wait(barrier, beside + (1 + len(others)))


class Gather:
    def __init__(self, at, own, held, sems, balanced, part=(0, 1)):
        self.at, self.own_ref, self.held, self.part = at, own, held, part
        self.balanced = at.balanced and balanced
        self.send, self.recv, self.half_recv, self.local = sems

    @staticmethod
    def scratch(n):
        return [
            pltpu.SemaphoreType.DMA((3, n)),
            pltpu.SemaphoreType.DMA((n,)),
            pltpu.SemaphoreType.DMA((1,)),
            pltpu.SemaphoreType.DMA((1,)),
        ]

    def slot(self, slot, start=0, rows=None):
        if self.held.ndim == 3:
            return self.held.at[slot] if rows is None else self.held.at[slot, pl.ds(start, rows)]
        tall = self.own_ref.shape[0]
        which, of = self.part
        first = pl.multiple_of((slot * of + which) * tall, 16) + start
        return self.held.at[pl.ds(first, tall if rows is None else rows)]

    def copy(self, slot, way, own=False):
        at = self.at
        return remote(
            self.own_ref if own else self.slot(slot),
            self.slot(slot),
            self.send.at[way, slot],
            self.recv.at[slot],
            (at.right, at.left, at.pair)[way],
        )

    def half(self, slot, way, which):
        at, rows = self.at, self.own_ref.shape[0]
        cut = rows * GATHER_CUT // 8
        part = self.slot(slot, which * cut, (cut, rows - cut)[which])
        return remote(
            part,
            part,
            self.send.at[way, slot],
            self.recv.at[slot] if which == 0 else self.half_recv.at[0],
            (at.right, at.left, at.pair)[way],
        )

    def local_copy(self):
        return pltpu.make_async_copy(self.own_ref, self.slot(self.at.s), self.local.at[0])

    def own(self):
        at = self.at
        self.local_copy().start()
        pl.when(at.has_right)(lambda: self.copy(at.s, 0, True).start())
        pl.when(at.has_left)(lambda: self.copy(at.s, 1, True).start())
        self.copy(at.s, 2, True).start()

    def to_pair(self, slot, act):
        at = self.at
        if not self.balanced:
            act(self.copy(slot, 2))
            return
        partner = slot // 2 == at.partner
        pl.when(jnp.logical_not(partner & (at.end | at.next)))(lambda: act(self.copy(slot, 2)))
        pl.when(partner & at.end)(lambda: act(self.half(slot, 2, 0)))

    def step(self, k):
        at = self.at
        for way in (0, 1):
            slot = at.s - 2 * k if way == 0 else at.s + 2 * k
            there = at.o - k >= 0 if way == 0 else at.o + k < at.m
            on = at.has_right if way == 0 else at.has_left

            @pl.when(there)
            def _(slot=slot, on=on, way=way):
                self.copy(slot, 2).wait_recv()
                pl.when(on)(lambda: self.copy(slot, way).start())
                self.to_pair(slot, lambda c: c.start())

    def extra_copies(self, act):
        at = self.at
        slot = at.o * 2 + 1 - at.i
        pl.when(at.o == 0)(lambda: act(self.copy(slot, 0)))
        pl.when(at.o == at.m - 1)(lambda: act(self.copy(slot, 1)))
        pl.when(at.o == 1)(lambda: act(self.half(slot, 1, 1)))
        pl.when(at.o == at.m - 2)(lambda: act(self.half(slot, 0, 1)))

    def extra(self):
        at = self.at
        if self.balanced:
            slot = at.o * 2 + 1 - at.i
            pl.when(at.end | at.next)(lambda: self.copy(slot, 2).wait_recv())
            self.extra_copies(lambda c: c.start())

    def arrive(self):
        at = self.at
        self.local_copy().wait()
        for layer in range(at.m):
            slot = layer * 2 + 1 - at.i
            if not self.balanced:
                self.copy(slot, 2).wait_recv()
                continue
            met = (at.o == layer) & (at.end | at.next)
            halved = at.end & (at.partner == layer)
            pl.when(jnp.logical_not(met | halved))(lambda: self.copy(slot, 2).wait_recv())

            @pl.when(halved)
            def _():
                self.half(slot, 2, 0).wait_recv()
                self.half(slot, 2, 1).wait_recv()

    def drain(self):
        at = self.at
        pl.when(at.has_right)(lambda: self.copy(at.s, 0, True).wait_send())
        pl.when(at.has_left)(lambda: self.copy(at.s, 1, True).wait_send())
        self.copy(at.s, 2, True).wait_send()
        for k in range(1, at.m):
            for way in (0, 1):
                slot = at.s - 2 * k if way == 0 else at.s + 2 * k
                there = at.o - k >= 0 if way == 0 else at.o + k < at.m
                on = at.has_right if way == 0 else at.has_left

                @pl.when(there)
                def _(slot=slot, on=on, way=way):
                    pl.when(on)(lambda: self.copy(slot, way).wait_send())
                    self.to_pair(slot, lambda c: c.wait_send())

        if self.balanced:
            self.extra_copies(lambda c: c.wait_send())


def add_rows(total, part, start, rows):
    step = next(size for size in (64, 32, 16, 8) if rows % size == 0)

    @pl.loop(0, rows // step)
    def _(j):
        at = pl.ds(pl.multiple_of(start + j * step, 8), step)
        both = total[at, :].astype(jnp.float32) + part[at, :].astype(jnp.float32)
        total[at, :] = both.astype(total.dtype)


class Scatter:
    def __init__(self, at, parts, out, landing, bufs, sems, balanced):
        self.at, self.parts, self.out = at, parts, out
        self.balanced = at.balanced and balanced
        self.from_pair, self.from_line, self.shifted_in = landing
        self.mine, self.aside, self.stage = bufs
        (
            self.pair_send,
            self.pair_recv,
            self.line_send,
            self.line_recv,
            self.extra_send,
            self.extra_recv,
            self.local,
        ) = sems
        self.rows = self.mine.shape[1]
        self.cut = self.rows * SCATTER_CUT // 8

    @staticmethod
    def landing(n, shape, dtype):
        m = n // 2
        return [jax.ShapeDtypeStruct((size,) + shape, dtype) for size in (m, m + 1, 1)]

    @staticmethod
    def scratch(n, shape, dtype):
        m = n // 2
        return [pltpu.VMEM((size,) + shape, dtype) for size in (m, 1)] + [
            pltpu.SemaphoreType.DMA((m,)),
            pltpu.SemaphoreType.DMA((m,)),
            pltpu.SemaphoreType.DMA((m,)),
            pltpu.SemaphoreType.DMA((m + 1,)),
            pltpu.SemaphoreType.DMA((2,)),
            pltpu.SemaphoreType.DMA((2,)),
            pltpu.SemaphoreType.DMA((m + 4,)),
        ]

    def slot(self, slot):
        if self.parts.ndim == 3:
            return self.parts.at[slot]
        return self.parts.at[pl.ds(pl.multiple_of(slot * self.rows, 16), self.rows)]

    def load(self, layer):
        return pltpu.make_async_copy(
            self.slot(layer * 2 + self.at.i), self.mine.at[layer], self.local.at[layer]
        )

    def load_aside(self):
        at = self.at
        return pltpu.make_async_copy(
            self.slot(at.o * 2 + 1 - at.i), self.aside.at[0], self.local.at[at.m]
        )

    def store(self):
        at = self.at
        return pltpu.make_async_copy(self.mine.at[at.o], self.out, self.local.at[at.m + 1])

    def to_stage(self, src, which, start=0, rows=None):
        part = pl.ds(start, self.rows if rows is None else rows)
        return pltpu.make_async_copy(
            src.at[part], self.stage.at[which, part], self.local.at[self.at.m + 2 + which]
        )

    def to_pair(self, layer):
        return remote(
            self.slot(layer * 2 + 1 - self.at.i),
            self.from_pair.at[layer],
            self.pair_send.at[layer],
            self.pair_recv.at[layer],
            self.at.pair,
        )

    def half_to_pair(self, layer, which, src):
        cut = self.cut
        part = pl.ds(which * cut, (cut, self.rows - cut)[which])
        return remote(
            src.at[part],
            self.from_pair.at[layer, part],
            self.pair_send.at[layer] if which == 0 else self.extra_send.at[1],
            self.pair_recv.at[layer] if which == 0 else self.extra_recv.at[1],
            self.at.pair,
        )

    def sum_to_pair(self):
        return remote(
            self.aside.at[0],
            self.from_pair.at[self.at.o],
            self.pair_send.at[self.at.o],
            self.pair_recv.at[self.at.o],
            self.at.pair,
        )

    def along(self, layer, way):
        at = self.at
        there = layer if way == 0 else jnp.where(layer == at.o - 1, at.m, layer)
        return remote(
            self.mine.at[layer],
            self.from_line.at[there],
            self.line_send.at[layer],
            self.line_recv.at[there],
            (at.right, at.left)[way],
        )

    def wait_line(self, place):
        remote(
            self.mine.at[0],
            self.from_line.at[place],
            self.line_send.at[0],
            self.line_recv.at[place],
            self.at.right,
        ).wait_recv()

    def shifted(self, way, which=None):
        at, cut = self.at, self.cut
        src, dst = self.slot(at.partner * 2 + 1 - at.i), self.shifted_in.at[0]
        if which is not None:
            part = pl.ds(cut, self.rows - cut)
            src, dst = src.at[part], dst.at[part]
        return remote(
            src, dst, self.extra_send.at[0], self.extra_recv.at[0], (at.right, at.left)[way]
        )

    def far_first(self):
        at = self.at
        for d in range(at.m - 1, 0, -1):
            yield at.o + d, at.o + d < at.m
            yield at.o - d, at.o - d >= 0

    def pair_copies(self, act):
        at = self.at
        for layer, there in self.far_first():
            if not self.balanced:
                pl.when(there)(lambda: act(self.to_pair(layer)))
                continue
            partner = layer == at.partner
            pl.when(there & jnp.logical_not(partner & (at.end | at.next)))(
                lambda: act(self.to_pair(layer))
            )
            pl.when(there & partner & at.end)(
                lambda: act(self.half_to_pair(layer, 0, self.slot(layer * 2 + 1 - at.i)))
            )
        if not self.balanced:
            act(self.to_pair(at.o))
            return
        pl.when(jnp.logical_not(at.end | at.next))(lambda: act(self.to_pair(at.o)))
        pl.when(at.next)(
            lambda: act(self.half_to_pair(at.o, 0, self.slot(at.o * 2 + 1 - at.i)))
        )

    def shift_copies(self, act):
        at = self.at
        if self.balanced:
            pl.when(at.o == 0)(lambda: act(self.shifted(0, 1)))
            pl.when(at.o == at.m - 1)(lambda: act(self.shifted(1, 1)))
            pl.when(at.o == 1)(lambda: act(self.shifted(1)))
            pl.when(at.o == at.m - 2)(lambda: act(self.shifted(0)))

    def start(self):
        at = self.at
        self.shift_copies(lambda c: c.start())
        self.pair_copies(lambda c: c.start())
        for layer in range(at.m):
            self.load(layer).start()
        if self.balanced:
            self.load_aside().start()

    def extra(self):
        at = self.at
        if not self.balanced:
            return
        self.load_aside().wait()
        cut, landed = self.cut, self.shifted_in.at[0]
        left = self.rows - cut

        @pl.when(at.end)
        def _():
            self.shifted(0).wait_recv()
            self.to_stage(landed, 0).start()
            self.to_stage(landed, 0).wait()
            add_rows(self.aside.at[0], self.stage.at[0], 0, self.rows)
            self.sum_to_pair().start()

        @pl.when(at.next)
        def _():
            self.shifted(0, 1).wait_recv()
            self.to_stage(landed, 0, cut, left).start()
            self.to_stage(landed, 0, cut, left).wait()
            add_rows(self.aside.at[0], self.stage.at[0], cut, left)
            self.half_to_pair(at.o, 1, self.aside.at[0]).start()

    def wait_pair(self, layer):
        at = self.at
        if not self.balanced:
            self.to_pair(layer).wait_recv()
            return
        partner, own = layer == at.partner, layer == at.o
        parted = (partner & at.end) | (own & at.next)
        pl.when(jnp.logical_not((partner & (at.end | at.next)) | (own & at.next)))(
            lambda: self.to_pair(layer).wait_recv()
        )
        pl.when(parted)(lambda: self.half_to_pair(layer, 0, self.aside.at[0]).wait_recv())
        pl.when(own & at.next)(lambda: self.half_to_pair(layer, 1, self.aside.at[0]).wait_recv())

    def step(self, d):
        at = self.at
        for way in (0, 1):
            layer = at.o + d if way == 0 else at.o - d
            there = layer < at.m if way == 0 else layer >= 0
            behind = at.has_left if way == 0 else at.has_right

            @pl.when(there)
            def _(layer=layer, behind=behind, way=way):
                mine, paired, half = self.mine.at[layer], self.from_pair.at[layer], self.cut
                self.load(layer).wait()
                self.wait_pair(layer)
                partner = (layer == at.partner) & self.balanced
                whole = jnp.logical_not(partner & (at.end | at.next))
                halved = partner & at.end
                pl.when(whole)(lambda: self.to_stage(paired, 0).start())
                pl.when(halved)(lambda: self.to_stage(paired, 0, 0, half).start())

                @pl.when(behind)
                def _():
                    self.wait_line(layer)
                    self.to_stage(self.from_line.at[layer], 1).start()

                @pl.when(whole)
                def _():
                    self.to_stage(paired, 0).wait()
                    add_rows(mine, self.stage.at[0], 0, self.rows)

                @pl.when(halved)
                def _():
                    self.to_stage(paired, 0, 0, half).wait()
                    add_rows(mine, self.stage.at[0], 0, half)

                @pl.when(behind)
                def _():
                    self.to_stage(self.from_line.at[layer], 1).wait()
                    add_rows(mine, self.stage.at[1], 0, self.rows)

                self.along(layer, way).start()

    def final(self):
        at = self.at
        mine = self.mine.at[at.o]
        self.load(at.o).wait()
        self.wait_pair(at.o)
        self.to_stage(self.from_pair.at[at.o], 0).start()

        @pl.when(at.has_left)
        def _():
            self.wait_line(at.o)
            self.to_stage(self.from_line.at[at.o], 1).start()

        self.to_stage(self.from_pair.at[at.o], 0).wait()
        add_rows(mine, self.stage.at[0], 0, self.rows)

        @pl.when(at.has_right)
        def _():
            self.wait_line(at.m)
            self.to_stage(self.from_line.at[at.m], 0).start()

        @pl.when(at.has_left)
        def _():
            self.to_stage(self.from_line.at[at.o], 1).wait()
            add_rows(mine, self.stage.at[1], 0, self.rows)

        @pl.when(at.has_right)
        def _():
            self.to_stage(self.from_line.at[at.m], 0).wait()
            add_rows(mine, self.stage.at[0], 0, self.rows)

        self.store().start()

    def drain(self):
        at = self.at
        self.pair_copies(lambda c: c.wait_send())
        if self.balanced:
            pl.when(at.end)(lambda: self.sum_to_pair().wait_send())
            pl.when(at.next)(lambda: self.half_to_pair(at.o, 1, self.aside.at[0]).wait_send())
        self.shift_copies(lambda c: c.wait_send())
        for d in range(1, at.m):
            pl.when(at.o + d < at.m)(lambda: self.along(at.o + d, 0).wait_send())
            pl.when(at.o - d >= 0)(lambda: self.along(at.o - d, 1).wait_send())
        self.store().wait()


def fetch(src, dst, sem):
    return pltpu.make_async_copy(src, dst, sem)


def dot(a, b, dims=((1,), (0,))):
    return lax.dot_general(a, b, (dims, ((), ())), preferred_element_type=jnp.float32)


ROWS, COLS, BOTH = ((1,), (0,)), ((1,), (1,)), ((0,), (0,))


def row_start(lengths, position):
    at, start = jnp.int32(0), jnp.zeros_like(position)
    for k in range(lengths.shape[0]):
        start = jnp.maximum(start, jnp.where(at <= position, at, 0))
        at = at + lengths[k]
    return start


def lanes(shape):
    return lax.broadcasted_iota(jnp.int32, shape, len(shape) - 1)


def feature_maps(width):
    count = FEAT + 1 + FEAT * (FEAT + 1) // 2
    wide = -(-count // 128) * 128
    first, second = np.zeros((width, wide), np.float32), np.zeros((width, wide), np.float32)
    plus = np.zeros((3, wide), np.float32)
    plus[:, 0] = 1.0
    heads = np.arange(width // FEAT) * FEAT
    for i in range(FEAT):
        first[heads + i, 1 + i] = 1.0
        plus[1:, 1 + i] = 1.0, 0.25
    at = 1 + FEAT
    for i in range(FEAT):
        for j in range(i, FEAT):
            first[heads + i, at] = 1.0
            second[heads + j, at] = 1.0
            plus[2, at] = 1 / 32 if i == j else 1 / 16
            at += 1
    tall = -(-count // 16) * 16
    return (
        jnp.asarray(np.stack([first, second]), jnp.bfloat16),
        jnp.asarray(np.stack([first.T, second.T])[:, :tall], jnp.bfloat16),
        jnp.asarray(np.repeat(plus[:, None], 8, 1)),
        jnp.asarray(np.repeat(plus[:, :tall, None], 128, 2)),
    )


class Team:
    def __init__(self, at, rows):
        self.at, self.half, self.quarter = at, rows // 2, rows // 4
        t = at.t
        low, high = lax.rem(t, 2), t // 2
        self.near, self.far = (at.s, t + 1 - 2 * low), (at.s, lax.rem(t + 2, 4))
        self.half_at, self.other_half_at = low * self.half, (1 - low) * self.half
        self.quarter_at = self.half_at + high * self.quarter
        self.other_quarter_at = self.half_at + (1 - high) * self.quarter
        self.in_half, self.other_in_half = high * self.quarter, (1 - high) * self.quarter
        self.near_quarter_at = self.other_half_at + high * self.quarter
        self.near_other_at = self.other_half_at + (1 - high) * self.quarter


class Sum:
    pieces = 4

    def __init__(self, team, part, from_near, from_far, sems):
        self.team, self.part, self.from_near, self.from_far = team, part, from_near, from_far
        self.near_send, self.near_recv, self.far_send, self.far_recv = sems
        self.wide = part.shape[1] // self.pieces

    @staticmethod
    def scratch(rows, columns):
        return [
            pltpu.VMEM((rows // 2, columns), jnp.bfloat16),
            pltpu.VMEM((rows // 4, columns), jnp.bfloat16),
        ] + [pltpu.SemaphoreType.DMA((Sum.pieces,))] * 4

    def near(self, j):
        team, columns = self.team, pl.ds(j * self.wide, self.wide)
        return remote(
            self.part.at[pl.ds(pl.multiple_of(team.other_half_at, team.half), team.half), columns],
            self.from_near.at[:, columns],
            self.near_send.at[j],
            self.near_recv.at[j],
            team.near,
        )

    def far(self, j):
        team, columns = self.team, pl.ds(j * self.wide, self.wide)
        at = pl.multiple_of(team.other_quarter_at, team.quarter)
        return remote(
            self.part.at[pl.ds(at, team.quarter), columns],
            self.from_far.at[:, columns],
            self.far_send.at[j],
            self.far_recv.at[j],
            team.far,
        )

    def fold(self, j):
        team, columns = self.team, pl.ds(j * self.wide, self.wide)
        self.near(j).wait_recv()
        step = 64

        @pl.loop(0, team.quarter // step)
        def _(r):
            to = pl.ds(pl.multiple_of(team.other_quarter_at + r * step, step), step)
            of = pl.ds(pl.multiple_of(team.other_in_half + r * step, step), step)
            both = self.part[to, columns].astype(jnp.float32)
            both = both + self.from_near[of, columns].astype(jnp.float32)
            self.part[to, columns] = both.astype(jnp.bfloat16)

        self.far(j).start()

    def arrive(self):
        for j in range(self.pieces):
            self.far(j).wait_recv()

    def rows(self, start, count):
        team = self.team
        a = self.part[pl.ds(pl.multiple_of(team.quarter_at + start, 16), count), :]
        b = self.from_near[pl.ds(pl.multiple_of(team.in_half + start, 16), count), :]
        c = self.from_far[pl.ds(pl.multiple_of(start, 16), count), :]
        return a.astype(jnp.float32) + b.astype(jnp.float32) + c.astype(jnp.float32)

    def drain(self):
        for j in range(self.pieces):
            self.near(j).wait_send()
            self.far(j).wait_send()


class Spread:
    pieces = 4

    def __init__(self, team, whole, sems):
        self.team, self.whole = team, whole
        self.far_send, self.far_recv, self.near_send, self.near_recv, self.on_send, self.on_recv = (
            sems
        )
        self.tall = team.quarter // self.pieces

    @staticmethod
    def scratch():
        return [pltpu.SemaphoreType.DMA((Spread.pieces,))] * 6

    def copy(self, start, j, send, recv, device):
        rows = self.whole.at[pl.ds(pl.multiple_of(start + j * self.tall, self.tall), self.tall)]
        return remote(rows, rows, send.at[j], recv.at[j], device)

    def far(self, j):
        team = self.team
        return self.copy(team.quarter_at, j, self.far_send, self.far_recv, team.far)

    def near(self, j):
        team = self.team
        return self.copy(team.quarter_at, j, self.near_send, self.near_recv, team.near)

    def on(self, j):
        team = self.team
        return self.copy(team.other_quarter_at, j, self.on_send, self.on_recv, team.near)

    def send(self, j):
        self.far(j).start()
        self.near(j).start()

    def pass_on(self, j):
        self.far(j).wait_recv()
        self.on(j).start()

    def arrive(self):
        for j in range(self.pieces):
            self.near(j).wait_recv()
            self.on(j).wait_recv()

    def drain(self):
        for j in range(self.pieces):
            self.far(j).wait_send()
            self.near(j).wait_send()
            self.on(j).wait_send()


class Pump:
    def __init__(self, events):
        self.events = list(events)

    def __call__(self, count):
        for _ in range(min(count, len(self.events))):
            self.events.pop(0)()

    def until(self, event):
        while event in self.events:
            self.events.pop(0)()

    def rest(self):
        self(len(self.events))


def gain_row(gains, which, row):
    n, depth = gains.shape[0], gains.shape[2] // 2
    for s in range(n):
        part = gains[s, 0:8, which * depth : (which + 1) * depth]
        row[:, s * depth : (s + 1) * depth] = part


def scores(query, key, mask):
    s = dot(query, key, COLS) * 0.25
    return 1.0 + s, jnp.where(mask, 1.0 + s + 0.5 * s * s, 0.0)


def pair_mask(row_starts, column_starts, first_row, first_column):
    shape = (row_starts.shape[0], column_starts.shape[1])
    rows = lax.broadcasted_iota(jnp.int32, shape, 0) + first_row
    columns = lax.broadcasted_iota(jnp.int32, shape, 1) + first_column
    return (row_starts == column_starts) & (columns <= rows)


def of_head(values, h):
    lane = lanes((1, values.shape[1]))
    mine = (lane >= h * FEAT) & (lane < (h + 1) * FEAT)
    return jnp.where(mine, values, jnp.zeros_like(values))


def column(values, h):
    return jnp.sum(jnp.where(lanes((1, 128)) == h, values, 0.0), axis=1, keepdims=True)


def with_ones(values):
    return jnp.concatenate([values, jnp.ones_like(values)], axis=1)


def forward_kernel(n, sizes, *refs):
    (
        lengths, stream_h, cot_h, maps, maps_t, plus, plus_t,
        gains_own, query_h, key_h, value_h, out_raw_h, gate_raw_h, up_raw_h, down_raw_h,
        gains_h, qkv_h, out_h, gate_h, up_h, down_h,
        h_one_h, heads_h, mixed_h, rden_h, state_h, mid_h, h_two_h, gate_v_h, up_v_h, hid_h, part_h,
        query_own, key_own, value_own, out_raw, gate_raw, up_raw, down_raw,
        qkv_own, out_own, gate_own, up_own, down_own,
        stream, h_one, heads, w_qkv, w_out, mixed, rden, numer, mid, h_two, w_ff,
        gate_v, up_v, hid, part, gains, gain,
        t_own, t_pair, t_line, t_next, state, t_send, t_recv, local, part_sem,
        *sems,
    ) = refs
    rows, width = stream.shape
    heads_here = mixed.shape[1] // 128
    q_wide = heads_here * FEAT
    at = Place(n)
    team = Team(at, rows)
    near_sum, sems = sems[:6], sems[6:]
    spread_sems, sems = sems[:6], sems[6:]
    tall_half = down_own.shape[0] // 2
    down_halves = [(down_own.at[pl.ds(k * tall_half, tall_half)], down_h, (k, 2)) for k in range(2)]
    arrays = [
        (gains_own, gains_h, (0, 1)),
        (qkv_own, qkv_h, (0, 1)),
        (out_own, out_h, (0, 1)),
        (gate_own, gate_h, (0, 1)),
        (up_own, up_h, (0, 1)),
        *down_halves,
    ]
    groups = [
        Gather(at, own, whole, sems[4 * g : 4 * g + 4], g > 0, part)
        for g, (own, whole, part) in enumerate(arrays)
    ]
    g_gains, g_qkv, g_out, g_gate, g_up, g_down, g_rest = groups
    cell = iter(range(local.shape[0]))
    copies = []

    def load(src, dst):
        copy = fetch(src, dst, local.at[next(cell)])
        copy.start()
        return copy

    def save(src, dst):
        copies.append(load(src, dst))

    raw = [
        load(query_h, query_own),
        load(key_h, key_own),
        load(value_h, value_own),
        load(out_raw_h, out_raw),
        load(gate_raw_h, gate_raw),
        load(up_raw_h, up_raw),
        load(down_raw_h, down_raw),
    ]
    get_stream = load(stream_h, stream)
    at.greet((team.near, team.far))
    pump = Pump([])

    def queue(group, *steps):
        for k in steps:
            pump.events.append(functools.partial(group.step, k) if isinstance(k, int) else k)

    last = at.m - 1
    def values_here():
        pass

    queue(g_gains, 1)
    for k in range(2, last + 1):
        queue(g_gains, k)
        queue(g_qkv, k - 1)
        if k == 2:
            queue(g_qkv, g_qkv.extra)
    queue(g_gains, g_gains.extra, g_out.own)
    queue(g_qkv, last, values_here)
    queue(g_out, 1, *range(2, last), g_out.extra, last)

    def feed_forward_here():
        pass

    queue(g_gate, 1, g_gate.extra)
    for k in range(2, last + 1):
        queue(g_gate, k)
        queue(g_up, k - 1)
        if k == 2:
            queue(g_up, g_up.extra)
    queue(g_down, g_down.own, g_rest.own)
    queue(g_up, last, feed_forward_here)
    for k in range(1, last + 1):
        for group in (g_down, g_rest):
            queue(group, k)
            if k == 1:
                queue(group, group.extra)
    g_gains.own()
    for copy in raw[:3]:
        copy.wait()
    qkv_own[:, 0:q_wide] = query_own[...].T
    qkv_own[:, q_wide : 2 * q_wide] = key_own[...].T
    qkv_own[:, 2 * q_wide :] = value_own[...]
    g_qkv.own()
    for copy, turned, own in zip(
        raw[3:], (out_raw, gate_raw, up_raw, down_raw), (out_own, gate_own, up_own, down_own)
    ):
        copy.wait()
        own[...] = turned[...].T
    pump.until(g_gains.extra)
    g_gains.arrive()
    load(gains_h, gains).wait()
    gain_row(gains, 0, gain.at[0])
    gain_row(gains, 1, gain.at[1])
    get_stream.wait()

    @pl.loop(0, rows // 64)
    def _(j):
        here = pl.ds(pl.multiple_of(j * 64, 64), 64)
        x = stream[here, :].astype(jnp.float32)
        scale = lax.rsqrt(jnp.mean(x * x, axis=1, keepdims=True) + EPSILON)
        h_one[here, :] = (x * scale * gain[0, 0:1, :]).astype(jnp.bfloat16)

    save(h_one, h_one_h)
    pump.until(values_here)
    pump(1)
    g_gate.own()
    g_qkv.arrive()
    load(qkv_h, w_qkv).wait()

    @pl.loop(0, rows // 256)
    def _(j):
        here = pl.ds(pl.multiple_of(j * 256, 256), 256)
        heads[here, :] = dot(h_one[here, :], w_qkv[...]).astype(jnp.bfloat16)

    save(heads, heads_h)
    pump(1)
    first = at.s * rows
    starts_col = row_start(lengths, first + lax.broadcasted_iota(jnp.int32, (rows, 1), 0))
    starts_row = row_start(lengths, first + lax.broadcasted_iota(jnp.int32, (1, rows), 1))
    last = row_start(lengths, first + rows - 1)
    keep = jnp.where(starts_row == last, 1.0, 0.0)
    tall = t_own.shape[1]

    def values_of(h):
        return pl.ds(pl.multiple_of(2 * q_wide + h * 128, 128), 128)

    t_sum = numer.at[0, 0:tall, 0:128]
    t_sum[...] = jnp.zeros((tall, 128), jnp.float32)

    @pl.loop(0, heads_here)
    def _(h):
        key = of_head(heads[:, q_wide : 2 * q_wide], h)
        one = dot(maps_t[0], key, COLS) + plus_t[0][:, 0:1]
        two = dot(maps_t[1], key, COLS) + plus_t[1][:, 0:1]
        phi = (one * two * keep).astype(jnp.bfloat16)
        total = dot(phi, with_ones(heads[:, values_of(h)]))
        t_own[h] = total[:, :128].astype(jnp.bfloat16)
        t_sum[...] += jnp.where(lanes((tall, 128)) == h, total[:, 128:], 0.0)

    t_own[heads_here] = t_sum[...].astype(jnp.bfloat16)
    to_pair = remote(t_own, t_pair, t_send.at[0], t_recv.at[0], at.pair)
    to_right = remote(t_next, t_line, t_send.at[1], t_recv.at[1], at.right)
    to_pair.start()
    pump(1)
    tile = 256

    @pl.loop(0, heads_here)
    def _(h):
        key = heads[:, q_wide : 2 * q_wide]
        for j in range(rows // tile):
            upto = (j + 1) * tile
            query = of_head(heads[j * tile : upto, 0:q_wide], h)
            mask = pair_mask(starts_col[j * tile : upto], starts_row[:, :upto], j * tile, 0)
            _, weights = scores(query, key[:upto], mask)
            values = with_ones(heads[0:upto, values_of(h)])
            numer[h, j * tile : upto, :] = dot(weights.astype(jnp.bfloat16), values)

    pump(2)

    def closed(s):
        return jnp.where(row_start(lengths, (s + 1) * rows - 1) >= s * rows, 0.0, 1.0)

    on_one, on_two = closed(at.o * 2), closed(at.o * 2 + 1)

    @pl.when(at.o == 0)
    def _():
        t_line[...] = jnp.zeros_like(t_line)

    to_pair.wait_recv()
    pl.when(at.has_left)(lambda: to_right.wait_recv())
    for h in range(heads_here + 1):
        mine, other = t_own[h].astype(jnp.float32), t_pair[h].astype(jnp.float32)
        t_one, t_two = jnp.where(at.i == 0, mine, other), jnp.where(at.i == 0, other, mine)
        come = t_line[h].astype(jnp.float32)
        middle = t_one + on_one * come
        t_next[h] = (t_two + on_two * middle).astype(jnp.bfloat16)
        state[h] = jnp.where(at.i == 0, come, middle).astype(jnp.bfloat16)
    pl.when(at.has_right)(lambda: to_right.start())
    g_up.own()
    save(state, state_h)
    pump(2)

    rden[...] = jnp.zeros_like(rden)
    @pl.loop(0, heads_here)
    def _(h):
        own = lanes((tall, 128)) == h
        dens = jnp.sum(jnp.where(own, state[heads_here].astype(jnp.float32), 0.0), 1, keepdims=True)
        dens = jnp.broadcast_to(dens, (tall, 128)).astype(jnp.bfloat16)
        table = jnp.concatenate([state[h], dens], axis=1)
        table = jnp.concatenate(
            [table, jnp.zeros((maps.shape[2] - tall, 256), jnp.bfloat16)], axis=0
        )
        for j in range(rows // tile):
            here = slice(j * tile, (j + 1) * tile)
            query = of_head(heads[here, 0:q_wide], h)
            one = dot(query, maps[0]) + plus[0, 0:1, :]
            two = dot(query, maps[1]) + plus[1, 0:1, :]
            carried = jnp.where(starts_col[here] < first, 1.0, 0.0)
            phi = (one * two * plus[2, 0:1, :] * carried).astype(jnp.bfloat16)
            total = numer[h, here, :] + dot(phi, table)
            inverse = 1.0 / total[:, 128:]
            rden[here, :] = jnp.where(lanes((1, 128)) == h, inverse, rden[here, :])
            mixed[here, pl.ds(pl.multiple_of(h * 128, 128), 128)] = (
                total[:, :128] * inverse
            ).astype(jnp.bfloat16)

    save(mixed, mixed_h)
    save(rden, rden_h)
    pump.until(g_out.extra)
    g_out.arrive()
    load(out_h, w_out).wait()
    for copy in copies:
        copy.wait()
    copies.clear()

    part_sum = Sum(team, h_one, *near_sum[:2], near_sum[2:])
    for j in range(Sum.pieces):
        columns = slice(j * part_sum.wide, (j + 1) * part_sum.wide)

        @pl.loop(0, rows // 256)
        def _(r):
            here = pl.ds(pl.multiple_of(r * 256, 256), 256)
            h_one[here, columns] = dot(mixed[here, :], w_out[columns, :], COLS).astype(jnp.bfloat16)

        part_sum.near(j).start()
        if j:
            part_sum.fold(j - 1)
            pump(1)
    part_sum.fold(Sum.pieces - 1)
    part_sum.arrive()
    spread = Spread(team, h_two, spread_sems)
    for j in range(Spread.pieces):
        for k in range(spread.tall // 32):
            down = j * spread.tall + k * 32
            here = pl.ds(pl.multiple_of(team.quarter_at + down, 32), 32)
            x = part_sum.rows(down, 32) + stream[here, :].astype(jnp.float32)
            mid[down : down + 32, :] = x
            scale = lax.rsqrt(jnp.mean(x * x, axis=1, keepdims=True) + EPSILON)
            h_two[here, :] = (x * scale * gain[1, 0:1, :]).astype(jnp.bfloat16)
        spread.send(j)
    save(mid, mid_h)
    for j in range(Spread.pieces):
        pump((3, 1, 1, 1)[j])
        spread.pass_on(j)
    get_cot = load(cot_h, stream)
    spread.arrive()
    part_sum.drain()
    spread.drain()
    save(h_two, h_two_h)
    pump.until(feed_forward_here)
    g_gate.arrive()
    get_gate = load(gate_h, w_ff.at[0])
    g_up.arrive()
    load(up_h, w_ff.at[1]).wait()
    get_gate.wait()
    stages = 4
    for stage in range(stages):

        @pl.loop(0, rows // 128 // stages)
        def _(r):
            start = pl.multiple_of((stage * (rows // 128 // stages) + r) * 128, 128)
            here = pl.ds(start, 128)
            gate = dot(h_two[here, :], w_ff[0])
            up = dot(h_two[here, :], w_ff[1])
            hidden = gate * jax.nn.sigmoid(gate) * up
            gate_v[here, :] = gate.astype(jnp.bfloat16)
            up_v[here, :] = up.astype(jnp.bfloat16)
            hid[here, :] = hidden.astype(jnp.bfloat16)

        pump(1 if stage else 3)
    save(gate_v, gate_v_h)
    save(up_v, up_v_h)
    save(hid, hid_h)
    get_cot.wait()
    def to_hbm(s, slot):
        here = pl.ds(pl.multiple_of(s * 256, 256), 256)
        return fetch(part.at[slot], part_h.at[here], part_sem.at[slot])

    count = width // 256
    for half in range(2):

        @pl.loop(half * (count // 2), (half + 1) * (count // 2))
        def _(s):
            slot = lax.rem(s, 2)
            pl.when(s > 1)(lambda: to_hbm(s - 2, slot).wait())
            columns = pl.ds(pl.multiple_of(s * 256, 256), 256)
            part[slot] = dot(stream[:, columns], hid[...], BOTH).astype(jnp.bfloat16)
            to_hbm(s, slot).start()

        pump(1)
    for s in range(count - 2, count):
        to_hbm(s, s % 2).wait()
    pump.rest()
    g_down.arrive()
    g_rest.arrive()
    for group in groups:
        group.drain()
    to_pair.wait_send()
    pl.when(at.has_right)(lambda: to_right.wait_send())
    for copy in copies:
        copy.wait()


def forward(n, lengths, stream, cot, maps, shards):
    rows, width = stream.shape
    gains, query, key, value, out, gate, up, down = shards
    hidden, deep = gate.shape
    values = out.shape[0]
    qkv_wide = 2 * query.shape[0] + values
    heads_here = values // 128
    tall = maps[1].shape[1]
    bf, f32 = jnp.bfloat16, jnp.float32
    shape = jax.ShapeDtypeStruct
    wholes = [
        shape((n,) + gains.shape, f32),
        shape((width, qkv_wide), bf),
        shape((width, values), bf),
        shape((width, hidden), bf),
        shape((width, hidden), bf),
        shape((width, hidden), bf),
    ]
    kept = [
        shape((rows, width), bf),
        shape((rows, qkv_wide), bf),
        shape((rows, values), bf),
        shape((rows, 128), f32),
        shape((heads_here + 1, tall, 128), bf),
        shape((rows // 4, width), f32),
        shape((rows, width), bf),
        shape((rows, hidden), bf),
        shape((rows, hidden), bf),
        shape((rows, hidden), bf),
        shape((width, hidden), bf),
    ]
    state = (heads_here + 1, tall, 128)
    scratch = [pltpu.VMEM(a.shape, bf) for a in shards[1:]]
    scratch += [pltpu.VMEM((deep, wide), bf) for wide in (qkv_wide, values, hidden, hidden, hidden)]
    scratch += [
        pltpu.VMEM((rows, width), bf),
        pltpu.VMEM((rows, width), bf),
        pltpu.VMEM((rows, qkv_wide), bf),
        pltpu.VMEM((width, qkv_wide), bf),
        pltpu.VMEM((width, values), bf),
        pltpu.VMEM((rows, values), bf),
        pltpu.VMEM((rows, 128), f32),
        pltpu.VMEM((heads_here, rows, 256), f32),
        pltpu.VMEM((rows // 4, width), f32),
        pltpu.VMEM((rows, width), bf),
        pltpu.VMEM((2, width, hidden), bf),
        pltpu.VMEM((rows, hidden), bf),
        pltpu.VMEM((rows, hidden), bf),
        pltpu.VMEM((rows, hidden), bf),
        pltpu.VMEM((2, 256, hidden), bf),
        pltpu.VMEM((n,) + gains.shape, f32),
        pltpu.VMEM((2, 8, width), f32),
        pltpu.VMEM(state, bf),
        pltpu.VMEM(state, bf),
        pltpu.VMEM(state, bf),
        pltpu.VMEM(state, bf),
        pltpu.VMEM(state, bf),
        pltpu.SemaphoreType.DMA((2,)),
        pltpu.SemaphoreType.DMA((2,)),
        pltpu.SemaphoreType.DMA((32,)),
        pltpu.SemaphoreType.DMA((2,)),
    ]
    scratch += Sum.scratch(rows, width) + Spread.scratch() + Gather.scratch(n) * (len(wholes) + 1)
    anywhere, inside = pl.BlockSpec(memory_space=pl.ANY), pl.BlockSpec(memory_space=pltpu.VMEM)
    result = pl.pallas_call(
        functools.partial(forward_kernel, n, None),
        out_shape=wholes + kept,
        in_specs=[pl.BlockSpec(memory_space=pltpu.SMEM), anywhere, anywhere]
        + [inside] * 4
        + [anywhere] * len(shards),
        out_specs=[anywhere] * (len(wholes) + len(kept)),
        scratch_shapes=scratch,
        compiler_params=pltpu.CompilerParams(
            collective_id=0, has_side_effects=True, vmem_limit_bytes=62 * MIB
        ),
    )(lengths, stream, cot, *maps, *shards)
    return result[: len(wholes)], result[len(wholes) :]


class SpreadOut(Spread):
    def __init__(self, team, quarter, whole, sems):
        super().__init__(team, whole, sems[:-1])
        self.own, self.kept = quarter, sems[-1]

    @staticmethod
    def scratch():
        return Spread.scratch() + [pltpu.SemaphoreType.DMA((1,))]

    def own_copy(self, j, send, recv, device):
        start = self.team.quarter_at + j * self.tall
        rows = self.whole.at[pl.ds(pl.multiple_of(start, self.tall), self.tall)]
        src = self.own.at[pl.ds(j * self.tall, self.tall)]
        return remote(src, rows, send.at[j], recv.at[j], device)

    def far(self, j):
        return self.own_copy(j, self.far_send, self.far_recv, self.team.far)

    def near(self, j):
        return self.own_copy(j, self.near_send, self.near_recv, self.team.near)

    def keep(self):
        team = self.team
        rows = self.whole.at[pl.ds(pl.multiple_of(team.quarter_at, team.quarter), team.quarter)]
        return pltpu.make_async_copy(self.own, rows, self.kept.at[0])


def backward_kernel(n, *refs):
    (
        lengths, maps, maps_t, plus, plus_t,
        stream_h, cot_h, gains_h, qkv_h, out_h, gate_h, up_h, down_h,
        h_one_h, heads_h, mixed_h, rden_h, state_h, mid_h, h_two_h, gate_v_h, up_v_h, hid_h, part_h,
        *refs,
    ) = refs
    act_h, ig_h, *refs = refs
    outs, refs = refs[:6], refs[6:]
    parts, refs = [part_h] + refs[:5], refs[5:]
    landings, refs = refs[:18], refs[18:]
    (
        part, arena, d_mid, dm, gains, gain, gain_sum, gain_near, gain_far, gain_parts,
        t_own, t_pair, t_line, t_next, state, back, t_send, t_recv, gain_send, gain_recv, local,
        stage_g, stage_o, stage_q, stage_n,
        *sems,
    ) = refs
    rows, width = arena.shape
    hidden = gate_v_h.shape[1]
    values_wide = mixed_h.shape[1]
    heads_here = values_wide // 128
    q_wide = heads_here * FEAT
    at = Place(n)
    team = Team(at, rows)

    def take(count):
        nonlocal sems
        taken, sems = sems[:count], sems[count:]
        return taken

    sums = [take(6) for _ in range(2)]
    first_sems = take(4)
    dm_sems, act_sems, ig_sems = take(6), take(7), take(7)
    stages = (stage_g, stage_g, stage_g, stage_o, stage_q, stage_n)
    groups = []
    for g in range(6):
        mine, aside, *own_sems = take(9)
        groups.append(
            Scatter(
                at,
                parts[g],
                outs[g],
                landings[3 * g : 3 * g + 3],
                (mine, aside, stages[g]),
                own_sems,
                g < 3,
            )
        )
    s_down, s_gate, s_up, s_out, s_qkv, s_gains = groups
    at.greet((team.near, team.far))
    cell = iter(range(local.shape[0]))

    def load(src, dst):
        copy = fetch(src, dst, local.at[next(cell)])
        copy.start()
        return copy

    pump = Pump([])

    def begin(group):
        group.start()
        for d in range(at.m - 1, 0, -1):
            pump.events.append(functools.partial(group.step, d))
            if d == max(1, at.m - 2) and group.balanced:
                pump.events.append(group.extra)

    begin(s_down)
    get_gains = load(gains_h, gains)
    get_mid = load(mid_h, d_mid)
    part_sum = Sum(team, part, *sums[0][:2], sums[0][2:])
    feed_sum = Sum(team, part, *sums[1][:2], sums[1][2:])
    first_sum = Sum(team, part, *sums[0][:2], first_sems)
    spread = Spread(team, dm, dm_sems)
    ig_rows = team.quarter
    ig_spread = SpreadOut(team, arena.at[pl.ds(ig_rows, team.quarter)], ig_h, ig_sems)
    act_spread = SpreadOut(team, feed_sum.from_far, act_h, act_sems)
    piece = part_sum.wide

    def staged(sem, tile, parts_h, compute):
        count = width // 256

        def to_hbm(s, slot):
            here = pl.ds(pl.multiple_of(s * 256, 256), 256)
            return fetch(tile.at[slot], parts_h.at[here], sem.at[slot])

        @pl.loop(0, count)
        def _(s):
            slot = lax.rem(s, 2)
            pl.when(s > 1)(lambda: to_hbm(s - 2, slot).wait())
            columns = pl.ds(pl.multiple_of(s * 256, 256), 256)
            tile[slot] = compute(columns).astype(jnp.bfloat16)
            to_hbm(s, slot).start()

        for s in range(count - 2, count):
            to_hbm(s, s % 2).wait()

    def norm_back(x, grad, gain_ref, which):
        scale = lax.rsqrt(jnp.mean(x * x, axis=1, keepdims=True) + EPSILON)
        unit = x * scale
        total = jnp.sum((grad * unit).reshape(-1, 8, width), axis=0)
        gain_sum[8 * which : 8 * which + 8, :] += total
        scaled = grad * gain_ref[0:1, :]
        return scale * (scaled - unit * jnp.mean(scaled * unit, axis=1, keepdims=True))

    gain_sum[...] = jnp.zeros_like(gain_sum)

    def feed_forward(w_down, w_ff, ff, w_sem, tile_sem):
        get_cot, get_down = load(cot_h, arena), load(down_h, w_down)
        get_gate, get_up = load(gate_v_h, ff.at[0]), load(up_v_h, ff.at[1])
        tall = w_ff.shape[2]

        def weights(j, which):
            here = pl.ds(j * tall, tall)
            return fetch(
                (gate_h, up_h)[which].at[here], w_ff.at[j % 2, which], w_sem.at[j % 2, which]
            )

        for which in (0, 1):
            weights(0, which).start()
        get_cot.wait()
        get_down.wait()
        get_gate.wait()
        get_up.wait()
        block = 256
        for low in range(0, hidden, 512):
            high = min(hidden, low + 512)

            @pl.loop(0, rows // block)
            def _(r):
                here = pl.ds(pl.multiple_of(r * block, block), block)
                grad = dot(arena[here, :], w_down[:, low:high])
                gate = ff[0, here, low:high].astype(jnp.float32)
                sigma = jax.nn.sigmoid(gate)
                silu = gate * sigma
                up = ff[1, here, low:high].astype(jnp.float32)
                ff[0, here, low:high] = (grad * up * (sigma + silu * (1.0 - sigma))).astype(
                    jnp.bfloat16
                )
                ff[1, here, low:high] = (grad * silu).astype(jnp.bfloat16)

        pump(1)
        get_two = load(h_two_h, arena)
        count = width // tall
        for j in range(count):
            for which in (0, 1):
                if j + 1 < count:
                    weights(j + 1, which).start()
                weights(j, which).wait()

            @pl.loop(0, rows // 512)
            def _(r):
                here = pl.ds(pl.multiple_of(r * 512, 512), 512)
                grad = dot(ff[0, here, :], w_ff[j % 2, 0], COLS)
                grad += dot(ff[1, here, :], w_ff[j % 2, 1], COLS)
                part[here, j * tall : (j + 1) * tall] = grad.astype(jnp.bfloat16)

            if (j + 1) * tall % piece == 0:
                p = (j + 1) * tall // piece - 1
                part_sum.near(p).start()
                if p:
                    part_sum.fold(p - 1)
        part_sum.fold(Sum.pieces - 1)
        get_two.wait()
        pump(2)
        tile = w_ff.at[0]

        def grads(which):
            return lambda columns: dot(arena[:, columns], ff[which], BOTH)

        staged(tile_sem, tile, parts[1], grads(0))
        begin(s_gate)
        get_gains.wait()
        gain_row(gains, 0, gain.at[0])
        gain_row(gains, 1, gain.at[1])
        get_mid.wait()
        part_sum.arrive()
        quarter = pl.ds(pl.multiple_of(team.quarter_at, team.quarter), team.quarter)
        load(cot_h.at[quarter], dm.at[quarter]).wait()
        for j in range(Spread.pieces):

            @pl.loop(0, spread.tall // 32)
            def _(r):
                start = pl.multiple_of(j * spread.tall + r * 32, 32)
                here = pl.ds(pl.multiple_of(team.quarter_at + start, 32), 32)
                x = d_mid[pl.ds(start, 32), :]
                grad = norm_back(x, part_sum.rows(start, 32), gain.at[1], 1)
                grad = grad + dm[here, :].astype(jnp.float32)
                d_mid[pl.ds(start, 32), :] = grad
                dm[here, :] = grad.astype(jnp.bfloat16)

            spread.send(j)
        part_sum.drain()
        pump(1)
        staged(tile_sem, tile, parts[2], grads(1))
        get_hid = load(hid_h, ff.at[0])
        get_hid.wait()
        for j in range(Sum.pieces):
            columns = slice(j * piece, (j + 1) * piece)

            @pl.loop(0, rows // 512)
            def _(r):
                here = pl.ds(pl.multiple_of(r * 512, 512), 512)
                feed = dot(ff[0, here, :], w_down[columns, :], COLS)
                part[here, columns] = feed.astype(jnp.bfloat16)

            feed_sum.near(j).start()
            spread.pass_on(j)
            if j == Sum.pieces - 2:
                pump(1)


    pl.run_scoped(
        feed_forward,
        pltpu.VMEM(down_h.shape, jnp.bfloat16),
        pltpu.VMEM((2, 2, 256, hidden), jnp.bfloat16),
        pltpu.VMEM((2, rows, hidden), jnp.bfloat16),
        pltpu.SemaphoreType.DMA((2, 2)),
        pltpu.SemaphoreType.DMA((2,)),
    )

    def attention(
        heads, d_heads, mixed, w_out, w_qkv, delta, g, delta_row, d_query, d_key,
        dens, tile_o, tile_q, tile_sem, d_values, mid_part, mid_sem, qkv_sem,
    ):
        gets = [
            load(heads_h, heads),
            load(mixed_h, mixed),
            load(out_h, w_out),
            load(rden_h, delta),
            load(state_h, state),
        ]
        get_one = load(h_one_h, arena)

        def mid_rows(j):
            here = pl.ds(j * act_spread.tall, act_spread.tall)
            return fetch(mid_h.at[here], mid_part.at[j % 2], mid_sem.at[j % 2])

        def qkv_rows(j):
            here = pl.ds(j * piece, piece)
            return fetch(qkv_h.at[here], w_qkv.at[j % 2], qkv_sem.at[j % 2])

        for j in range(2):
            mid_rows(j).start()
            qkv_rows(j).start()
        for get in gets:
            get.wait()
        spread.arrive()

        @pl.loop(0, rows // 256)
        def _(r):
            here = pl.ds(pl.multiple_of(r * 256, 256), 256)
            d_values[here, :] = dot(dm[here, :], w_out[...])

        for j in range(Sum.pieces):
            feed_sum.fold(j)

        @pl.loop(0, heads_here)
        def _(h):
            across = pl.ds(pl.multiple_of(h * 128, 128), 128)
            grad = d_values[:, across] * column(delta[...], h)
            g[h] = grad.astype(jnp.bfloat16)
            sums_of = jnp.sum(grad * mixed[:, across].astype(jnp.float32), axis=1, keepdims=True)
            wide = jnp.broadcast_to(sums_of, (rows, 128))
            delta[...] = jnp.where(lanes((1, 128)) == h, wide, delta[...])
            delta_row[h] = wide.T[0:8]

        first = at.s * rows
        starts_col = row_start(lengths, first + lax.broadcasted_iota(jnp.int32, (rows, 1), 0))
        starts_row = row_start(lengths, first + lax.broadcasted_iota(jnp.int32, (1, rows), 1))
        last = row_start(lengths, first + rows - 1)
        tall = t_own.shape[1]
        wide = maps.shape[2]
        carried_row = jnp.where(starts_row < first, 1.0, 0.0)
        dens[1, 0:tall, 0:128] = jnp.zeros((tall, 128), jnp.float32)

        def values_of(h):
            return pl.ds(pl.multiple_of(2 * q_wide + h * 128, 128), 128)

        def head_at(h):
            return pl.ds(pl.multiple_of(h * 128, 128), 128)

        @pl.loop(0, heads_here)
        def _(h):
            query = of_head(heads[:, 0:q_wide], h)
            one = dot(maps_t[0], query, COLS) + plus_t[0][:, 0:1]
            two = dot(maps_t[1], query, COLS) + plus_t[1][:, 0:1]
            phi = one * two * plus_t[2][:, 0:1] * carried_row
            t_own[h] = dot(phi.astype(jnp.bfloat16), g[h]).astype(jnp.bfloat16)
            below = -jnp.sum(phi * delta_row[h][0:1, :], axis=1, keepdims=True)
            dens[1, 0:tall, 0:128] += jnp.where(lanes((tall, 128)) == h, below, 0.0)

        t_own[heads_here] = dens[1, 0:tall, 0:128].astype(jnp.bfloat16)
        to_pair = remote(t_own, t_pair, t_send.at[0], t_recv.at[0], at.pair)
        to_left = remote(t_next, t_line, t_send.at[1], t_recv.at[1], at.left)
        to_pair.start()
        begin(s_up)

        @pl.when(at.o == at.m - 1)
        def _():
            t_line[...] = jnp.zeros_like(t_line)

        def closed(s):
            return jnp.where(row_start(lengths, (s + 1) * rows - 1) >= s * rows, 0.0, 1.0)

        on_one, on_two = closed(at.o * 2), closed(at.o * 2 + 1)

        def relay():
            to_pair.wait_recv()
            pl.when(at.has_right)(lambda: to_left.wait_recv())

            @pl.loop(0, heads_here + 1)
            def _(h):
                mine, other = t_own[h].astype(jnp.float32), t_pair[h].astype(jnp.float32)
                t_one, t_two = jnp.where(at.i == 0, mine, other), jnp.where(at.i == 0, other, mine)
                come = t_line[h].astype(jnp.float32)
                middle = t_two + on_two * come
                t_next[h] = (t_one + on_one * middle).astype(jnp.bfloat16)
                back[h] = jnp.where(at.i == 0, middle, come).astype(jnp.bfloat16)

            pl.when(at.has_left)(lambda: to_left.start())

        turns = min(4, at.m)

        def turn(p):
            mine = at.o == at.m - 1 - p if p < turns - 1 else at.o <= at.m - turns
            pl.when(mine)(relay)

        d_query[...] = jnp.zeros_like(d_query)
        d_key[...] = jnp.zeros_like(d_key)
        tile = 128

        def intra(h):
            key, query = of_head(heads[:, q_wide : 2 * q_wide], h), of_head(heads[:, 0:q_wide], h)
            across = values_of(h)
            for j in range(rows // tile):
                here, upto = slice(j * tile, (j + 1) * tile), (j + 1) * tile
                mask = pair_mask(starts_col[here], starts_row[:, :upto], j * tile, 0)
                more, _ = scores(query[here], key[:upto], mask)
                d_weight = dot(g[h, here, :], heads[0:upto, across], COLS) - column(delta[here, :], h)
                d_score = jnp.where(mask, d_weight * more, 0.0).astype(jnp.bfloat16)
                d_query[here, :] += dot(d_score, key[:upto]) * 0.25
            for j in range(rows // tile):
                here, after = slice(j * tile, (j + 1) * tile), j * tile
                shape = (tile, rows - after)
                key_at = lax.broadcasted_iota(jnp.int32, shape, 0)
                query_at = lax.broadcasted_iota(jnp.int32, shape, 1)
                mask = (starts_col[here] == starts_row[:, after:]) & (key_at <= query_at)
                more, weight = scores(key[here], query[after:], mask)
                d_weight = dot(heads[here, across], g[h, after:, :], COLS)
                d_weight = d_weight - delta_row[h, 0:1, after:]
                d_score = jnp.where(mask, d_weight * more, 0.0).astype(jnp.bfloat16)
                d_values[here, head_at(h)] = dot(weight.astype(jnp.bfloat16), g[h, after:, :])
                grad = dot(d_score, query[after:]) * 0.25
                d_key[here, :] = jnp.where(h == 0, grad, d_key[here, :] + grad)

        for half in range(2):
            @pl.loop(half * heads_here // 2, (half + 1) * heads_here // 2)
            def _(h):
                intra(h)

            if half == 0:
                pump(1)
        turn(0)
        pump(1)

        def through(u, h, grad):
            one = dot(u, maps[0]) + plus[0, 0:1, :]
            two = dot(u, maps[1]) + plus[1, 0:1, :]
            grad = grad()
            left = dot((grad * two).astype(jnp.bfloat16), maps[0], COLS)
            left += dot((grad * one).astype(jnp.bfloat16), maps[1], COLS)
            return one * two, of_head(left, h)

        wider = 256

        def each_tile(body):
            @pl.loop(0, heads_here)
            def _(h):
                @pl.loop(0, rows // wider)
                def _(j):
                    here = pl.ds(pl.multiple_of(j * wider, wider), wider)
                    at_row = first + j * wider + lax.broadcasted_iota(jnp.int32, (wider, 1), 0)
                    body(h, here, row_start(lengths, at_row))

        filler = jnp.zeros((wide - tall, 128), jnp.bfloat16)
        dens[0] = jnp.zeros_like(dens[0])
        dens[0, 0:128, 0:tall] = state[heads_here].astype(jnp.float32).T

        def through_in(h, here, starts):
            carried = jnp.where(starts < first, 1.0, 0.0)

            def grad_phi():
                table = jnp.concatenate([state[h], filler], axis=0)
                grad = dot(g[h, here, :], table, COLS)
                grad = grad - column(delta[here, :], h) * dens[0, pl.ds(h, 1), :]
                return grad * plus[2, 0:1, :] * carried

            _, grad = through(of_head(heads[here, 0:q_wide], h), h, grad_phi)
            d_query[here, :] += grad

        each_tile(through_in)
        turn(1)
        pump(1)

        def grad_out(columns):
            return dot(dm[:, columns], mixed[...], BOTH)

        staged(tile_sem, tile_o, parts[3], grad_out)
        begin(s_out)
        turn(2)
        pump(1)
        feed_sum.arrive()
        for j in range(Spread.pieces):
            mid_rows(j).wait()

            @pl.loop(0, act_spread.tall // 32)
            def _(r):
                start = pl.multiple_of(j * act_spread.tall + r * 32, 32)
                x = mid_part[j % 2, pl.ds(pl.multiple_of(r * 32, 32), 32), :]
                x = x + feed_sum.rows(start, 32)
                feed_sum.from_far[pl.ds(start, 32), :] = x.astype(bf)

            if j + 2 < Spread.pieces:
                mid_rows(j + 2).start()
            act_spread.send(j)
        act_spread.keep().start()
        feed_sum.drain()
        for p in range(3, turns):
            turn(p)

        dens[1] = jnp.zeros_like(dens[1])
        dens[1, 0:128, 0:tall] = back[heads_here].astype(jnp.float32).T

        def through_out(h, here, starts):
            keep = jnp.where(starts == last, 1.0, 0.0)
            table = jnp.concatenate([back[h], filler], axis=0)

            def grad_phi():
                grad = dot(heads[here, values_of(h)], table, COLS)
                return (grad + dens[1, pl.ds(h, 1), :]) * keep

            phi, grad = through(of_head(heads[here, q_wide : 2 * q_wide], h), h, grad_phi)
            d_key[here, :] += grad
            far = dot((phi * keep).astype(jnp.bfloat16), table)
            d_heads[here, values_of(h)] = (d_values[here, head_at(h)] + far).astype(jnp.bfloat16)

        each_tile(through_out)
        d_heads[:, 0:q_wide] = d_query[...].astype(jnp.bfloat16)
        d_heads[:, q_wide : 2 * q_wide] = d_key[...].astype(jnp.bfloat16)
        pump(2)
        for j in range(Sum.pieces):
            columns = slice(j * piece, (j + 1) * piece)
            qkv_rows(j).wait()

            @pl.loop(0, rows // 256)
            def _(r):
                here = pl.ds(pl.multiple_of(r * 256, 256), 256)
                grad = dot(d_heads[here, :], w_qkv[j % 2], COLS)
                part[here, columns] = grad.astype(jnp.bfloat16)

            first_sum.near(j).start()
            if j + 2 < Sum.pieces:
                qkv_rows(j + 2).start()
            if j:
                first_sum.fold(j - 1)
        first_sum.fold(Sum.pieces - 1)

        pump(1)
        get_one.wait()

        def grad_qkv(columns):
            return dot(arena[:, columns], d_heads[...], BOTH)

        staged(tile_sem, tile_q, parts[4], grad_qkv)
        pump(1)
        begin(s_qkv)
        s_down.final()
        for j in range(Spread.pieces):
            act_spread.pass_on(j)
        to_pair.wait_send()
        pl.when(at.has_left)(lambda: to_left.wait_send())

    bf, f32 = jnp.bfloat16, jnp.float32
    pl.run_scoped(
        attention,
        pltpu.VMEM((rows, heads_h.shape[1]), bf),
        pltpu.VMEM((rows, heads_h.shape[1]), bf),
        pltpu.VMEM((rows, values_wide), bf),
        pltpu.VMEM(out_h.shape, bf),
        pltpu.VMEM((2, piece, qkv_h.shape[1]), bf),
        pltpu.VMEM((rows, 128), f32),
        pltpu.VMEM((heads_here, rows, 128), bf),
        pltpu.VMEM((heads_here, 8, rows), f32),
        pltpu.VMEM((rows, q_wide), f32),
        pltpu.VMEM((rows, q_wide), f32),
        pltpu.VMEM((2, maps.shape[2], maps.shape[2]), f32),
        pltpu.VMEM((2, 256, values_wide), bf),
        pltpu.VMEM((2, 256, heads_h.shape[1]), bf),
        pltpu.SemaphoreType.DMA((2,)),
        pltpu.VMEM((rows, values_wide), f32),
        pltpu.VMEM((2, act_spread.tall, width), f32),
        pltpu.SemaphoreType.DMA((2,)),
        pltpu.SemaphoreType.DMA((2,)),
    )

    quarter = pl.ds(pl.multiple_of(team.quarter_at, team.quarter), team.quarter)
    load(stream_h.at[quarter], arena.at[0 : team.quarter]).wait()
    first_sum.arrive()
    @pl.loop(0, team.quarter // 32)
    def _(r):
        start = pl.multiple_of(r * 32, 32)
        here = pl.ds(start, 32)
        x = arena[here, :].astype(f32)
        grad = norm_back(x, first_sum.rows(start, 32), gain.at[0], 0)
        arena[pl.ds(ig_rows + start, 32), :] = (d_mid[here, :] + grad).astype(bf)

    pump(1)
    gain_to_near = remote(gain_sum, gain_near, gain_send.at[0], gain_recv.at[0], team.near)
    gain_to_near.start()
    gain_to_near.wait()
    gain_sum[...] += gain_near[...]
    gain_to_far = remote(gain_sum, gain_far, gain_send.at[1], gain_recv.at[1], team.far)
    gain_to_far.start()
    for j in range(Spread.pieces):
        ig_spread.send(j)
    ig_spread.keep().start()
    pump(1)
    gain_to_far.wait()
    gain_near[...] = gain_sum[...] + gain_far[...]
    deep = width // n
    for s in range(n):
        gain_parts[s] = gain_near[:, s * deep : (s + 1) * deep]
    load(gain_parts, parts[5]).wait()
    begin(s_gains)
    pump(1)
    s_gate.final()
    pump(1)
    s_up.final()
    pump.rest()
    for group in groups[3:]:
        group.final()
    for j in range(Spread.pieces):
        ig_spread.pass_on(j)
    for spread_of in (ig_spread, act_spread):
        spread_of.arrive()
        spread_of.drain()
        spread_of.keep().wait()
    spread.drain()
    first_sum.drain()
    for group in groups:
        group.drain()


def backward(n, lengths, maps, stream, cot, wholes, kept):
    rows, width = stream.shape
    gains, qkv, out, gate, up, down = wholes
    heads_here = out.shape[1] // 128
    hidden = gate.shape[1]
    tall = maps[1].shape[1]
    bf, f32 = jnp.bfloat16, jnp.float32
    shape = jax.ShapeDtypeStruct
    deep = width // n
    kinds = [
        ((deep, hidden), bf),
        ((deep, hidden), bf),
        ((deep, hidden), bf),
        ((deep, out.shape[1]), bf),
        ((deep, qkv.shape[1]), bf),
        ((16, deep), f32),
    ]
    results = [shape((rows, width), bf)] * 2 + [shape(*kind) for kind in kinds]
    work = [shape((width, size[1]), kind) for size, kind in kinds[1:-1]]
    work += [shape((n,) + kinds[-1][0], f32)]
    work += sum((Scatter.landing(n, *kind) for kind in kinds), [])
    state = (heads_here + 1, tall, 128)
    scratch = [
        pltpu.VMEM((rows, width), bf),
        pltpu.VMEM((rows, width), bf),
        pltpu.VMEM((rows // 4, width), f32),
        pltpu.VMEM((rows, width), bf),
        pltpu.VMEM(gains.shape, f32),
        pltpu.VMEM((2, 8, width), f32),
        pltpu.VMEM((16, width), f32),
        pltpu.VMEM((16, width), f32),
        pltpu.VMEM((16, width), f32),
        pltpu.VMEM((n, 16, deep), f32),
    ]
    scratch += [pltpu.VMEM(state, bf)] * 6
    scratch += [pltpu.SemaphoreType.DMA((2,))] * 4
    scratch += [pltpu.SemaphoreType.DMA((24,))]
    scratch += [pltpu.VMEM((2,) + kinds[k][0], kinds[k][1]) for k in (0, 3, 4, 5)]
    scratch += Sum.scratch(rows, width) * 2 + Sum.scratch(rows, width)[2:] + Spread.scratch() + SpreadOut.scratch() * 2
    scratch += sum((Scatter.scratch(n, *kind) for kind in kinds), [])
    anywhere, inside = pl.BlockSpec(memory_space=pl.ANY), pl.BlockSpec(memory_space=pltpu.VMEM)
    given = [stream, cot, *wholes, *kept]
    result = pl.pallas_call(
        functools.partial(backward_kernel, n),
        out_shape=results + work,
        in_specs=[pl.BlockSpec(memory_space=pltpu.SMEM)] + [inside] * 4 + [anywhere] * len(given),
        out_specs=[anywhere] * (len(results) + len(work)),
        scratch_shapes=scratch,
        compiler_params=pltpu.CompilerParams(
            collective_id=1, has_side_effects=True, vmem_limit_bytes=63 * MIB
        ),
    )(lengths, *maps, *given)
    return result[: len(results)]


def finish_kernel(q_wide, *refs):
    act_h, ig_h, down_h, gate_h, up_h, out_h, qkv_h, *refs = refs
    act_o, ig_o, query_o, key_o, value_o, out_o, gate_o, up_o, down_o, *refs = refs
    act, ig, down, gate, up, out, qkv, *refs = refs
    ig_f, down_f, gate_f, up_f, out_f, query_f, key_f, value_f, get_sem, put_sem = refs
    parts = 8
    rows = ig.shape[0] // parts

    def get_rows(j):
        here = pl.ds(j * rows, rows)
        return fetch(ig_h.at[here], ig.at[here], get_sem.at[j])

    def put_rows(j):
        here = pl.ds(j * rows, rows)
        return fetch(ig_f.at[here], ig_o.at[here], put_sem.at[j])

    get_act, put_act = fetch(act_h, act, get_sem.at[parts]), fetch(act, act_o, get_sem.at[parts])
    gets = [
        fetch(src, dst, get_sem.at[parts + 1 + k])
        for k, (src, dst) in enumerate(
            ((down_h, down), (gate_h, gate), (up_h, up), (out_h, out), (qkv_h, qkv))
        )
    ]
    for j in range(parts):
        get_rows(j).start()
    for get in gets:
        get.start()
    get_act.start()
    for j in range(parts):
        get_rows(j).wait()

        @pl.loop(0, rows // 32)
        def _(r):
            here = pl.ds(pl.multiple_of(j * rows + r * 32, 32), 32)
            ig_f[here, :] = ig[here, :].astype(jnp.float32)

        put_rows(j).start()
    get_act.wait()
    put_act.start()
    puts = []

    def put(src, dst):
        puts.append(fetch(src, dst, put_sem.at[parts + len(puts)]))
        puts[-1].start()

    for get, src, mid, dst in zip(
        gets, (down, gate, up, out), (down_f, gate_f, up_f, out_f), (down_o, gate_o, up_o, out_o)
    ):
        get.wait()
        mid[...] = src[...].astype(jnp.float32).T
        put(mid, dst)
    gets[4].wait()
    query_f[...] = qkv[:, 0:q_wide].astype(jnp.float32).T
    key_f[...] = qkv[:, q_wide : 2 * q_wide].astype(jnp.float32).T
    value_f[...] = qkv[:, 2 * q_wide :].astype(jnp.float32)
    put(query_f, query_o)
    put(key_f, key_o)
    put(value_f, value_o)
    for j in range(parts):
        put_rows(j).wait()
    for copy in puts:
        copy.wait()
    put_act.wait()


def finish(q_wide, act, ig, down, gate, up, out, qkv):
    f32 = jnp.float32
    deep, hidden = gate.shape
    values = out.shape[1]
    shapes = [
        ig.shape,
        (q_wide, deep),
        (q_wide, deep),
        (deep, values),
        (values, deep),
        (hidden, deep),
        (hidden, deep),
        (hidden, deep),
    ]
    anywhere = pl.BlockSpec(memory_space=pl.ANY)
    given = (act, ig, down, gate, up, out, qkv)
    order = (0, 7, 5, 6, 4, 1, 2, 3)
    return pl.pallas_call(
        functools.partial(finish_kernel, q_wide),
        out_shape=[jax.ShapeDtypeStruct(act.shape, act.dtype)]
        + [jax.ShapeDtypeStruct(a, f32) for a in shapes],
        in_specs=[anywhere] * len(given),
        out_specs=[anywhere] * 9,
        scratch_shapes=[pltpu.VMEM(a.shape, a.dtype) for a in given]
        + [pltpu.VMEM(shapes[k], f32) for k in order]
        + [pltpu.SemaphoreType.DMA((16,)), pltpu.SemaphoreType.DMA((16,))],
        compiler_params=pltpu.CompilerParams(vmem_limit_bytes=56 * MIB),
    )(*given)


def on_device(
    stream_in,
    doc_lengths,
    first_gain,
    w_query,
    w_key,
    w_value,
    w_out,
    second_gain,
    w_gate,
    w_up,
    w_down,
    cotangent,
):
    n = lax.axis_size("seq")
    f32 = jnp.float32
    q_wide = w_query.shape[1]
    gains_own = jnp.concatenate([first_gain, second_gain]).astype(f32)
    gains_own = jnp.broadcast_to(gains_own[None], (16, gains_own.shape[0]))
    maps = feature_maps(q_wide)
    shards = (gains_own, w_query.T, w_key.T, w_value, w_out, w_gate.T, w_up.T, w_down)
    wholes, kept = forward(n, doc_lengths, stream_in, cotangent, maps, shards)
    *results, g_gains = backward(n, doc_lengths, maps, stream_in, cotangent, wholes, kept)
    activations, input_grad, query, key, value, out, gate, up, down = finish(q_wide, *results)
    return (
        activations,
        input_grad,
        jnp.sum(g_gains[:8], axis=0),
        query.T,
        key.T,
        value,
        out,
        jnp.sum(g_gains[8:], axis=0),
        gate.T,
        up.T,
        down,
    )


def solution(mesh):
    placed = (
        P("seq", None),
        P(),
        P("seq"),
        P("seq", "tp"),
        P("seq", "tp"),
        P("seq", "tp"),
        P("tp", "seq"),
        P("seq"),
        P("seq", "tp"),
        P("seq", "tp"),
        P("tp", "seq"),
        P("seq", None),
    )
    return jax.shard_map(
        on_device,
        mesh=mesh,
        in_specs=placed,
        out_specs=(
            P("seq", None),
            P("seq", None),
            P("seq"),
            P("seq", "tp"),
            P("seq", "tp"),
            P("seq", "tp"),
            P("tp", "seq"),
            P("seq"),
            P("seq", "tp"),
            P("seq", "tp"),
            P("tp", "seq"),
        ),
        check_vma=False,
    )
```

```python
import functools

import jax
import jax.numpy as jnp
import numpy as np
from jax import lax
from jax.experimental import pallas as pl
from jax.experimental.pallas import tpu as pltpu
from jax.sharding import PartitionSpec as P

FEAT = 16
EPSILON = 1e-06
MESH = pl.DeviceIdType.MESH
MIB = 2**20
GATHER_CUT, SCATTER_CUT = 4, 4


def remote(src, dst, send, recv, device):
    return pltpu.make_async_remote_copy(
        src_ref=src,
        dst_ref=dst,
        send_sem=send,
        recv_sem=recv,
        device_id=device,
        device_id_type=MESH,
    )


class Place:
    def __init__(self, n):
        self.n, self.m = n, n // 2
        self.s, self.t = lax.axis_index("seq"), lax.axis_index("tp")
        self.o, self.i = self.s // 2, lax.rem(self.s, 2)
        self.right, self.left = (self.s + 2, self.t), (self.s - 2, self.t)
        self.pair = (self.o * 2 + 1 - self.i, self.t)
        self.has_right, self.has_left = self.o < self.m - 1, self.o > 0
        self.balanced = self.m >= 4
        m, o = self.m, self.o
        self.end = (o == 0) | (o == m - 1)
        self.next = (o == 1) | (o == m - 2)
        self.partner = jnp.where(
            o == 0, 1, jnp.where(o == m - 1, m - 2, jnp.where(o == 1, 0, m - 1))
        )

    def greet(self, others=()):
        barrier = pltpu.get_barrier_semaphore()

        def signal(device):
            pl.semaphore_signal(barrier, inc=1, device_id=device, device_id_type=MESH)

        pl.when(self.has_right)(lambda: signal(self.right))
        pl.when(self.has_left)(lambda: signal(self.left))
        signal(self.pair)
        for other in others:
            signal(other)
        beside = self.has_right.astype(jnp.int32) + self.has_left.astype(jnp.int32)
        pl.semaphore_wait(barrier, beside + (1 + len(others)))


class Gather:
    def __init__(self, at, own, held, sems, balanced, part=(0, 1)):
        self.at, self.own_ref, self.held, self.part = at, own, held, part
        self.balanced = at.balanced and balanced
        self.send, self.recv, self.half_recv, self.local = sems

    @staticmethod
    def scratch(n):
        return [
            pltpu.SemaphoreType.DMA((3, n)),
            pltpu.SemaphoreType.DMA((n,)),
            pltpu.SemaphoreType.DMA((1,)),
            pltpu.SemaphoreType.DMA((1,)),
        ]

    def slot(self, slot, start=0, rows=None):
        if self.held.ndim == 3:
            return self.held.at[slot] if rows is None else self.held.at[slot, pl.ds(start, rows)]
        tall = self.own_ref.shape[0]
        which, of = self.part
        first = pl.multiple_of((slot * of + which) * tall, 16) + start
        return self.held.at[pl.ds(first, tall if rows is None else rows)]

    def copy(self, slot, way, own=False):
        at = self.at
        return remote(
            self.own_ref if own else self.slot(slot),
            self.slot(slot),
            self.send.at[way, slot],
            self.recv.at[slot],
            (at.right, at.left, at.pair)[way],
        )

    def half(self, slot, way, which):
        at, rows = self.at, self.own_ref.shape[0]
        cut = rows * GATHER_CUT // 8
        part = self.slot(slot, which * cut, (cut, rows - cut)[which])
        return remote(
            part,
            part,
            self.send.at[way, slot],
            self.recv.at[slot] if which == 0 else self.half_recv.at[0],
            (at.right, at.left, at.pair)[way],
        )

    def local_copy(self):
        return pltpu.make_async_copy(self.own_ref, self.slot(self.at.s), self.local.at[0])

    def own(self):
        at = self.at
        self.local_copy().start()
        pl.when(at.has_right)(lambda: self.copy(at.s, 0, True).start())
        pl.when(at.has_left)(lambda: self.copy(at.s, 1, True).start())
        self.copy(at.s, 2, True).start()

    def to_pair(self, slot, act):
        at = self.at
        if not self.balanced:
            act(self.copy(slot, 2))
            return
        partner = slot // 2 == at.partner
        pl.when(jnp.logical_not(partner & (at.end | at.next)))(lambda: act(self.copy(slot, 2)))
        pl.when(partner & at.end)(lambda: act(self.half(slot, 2, 0)))

    def step(self, k):
        at = self.at
        for way in (0, 1):
            slot = at.s - 2 * k if way == 0 else at.s + 2 * k
            there = at.o - k >= 0 if way == 0 else at.o + k < at.m
            on = at.has_right if way == 0 else at.has_left

            @pl.when(there)
            def _(slot=slot, on=on, way=way):
                self.copy(slot, 2).wait_recv()
                pl.when(on)(lambda: self.copy(slot, way).start())
                self.to_pair(slot, lambda c: c.start())

    def extra_copies(self, act):
        at = self.at
        slot = at.o * 2 + 1 - at.i
        pl.when(at.o == 0)(lambda: act(self.copy(slot, 0)))
        pl.when(at.o == at.m - 1)(lambda: act(self.copy(slot, 1)))
        pl.when(at.o == 1)(lambda: act(self.half(slot, 1, 1)))
        pl.when(at.o == at.m - 2)(lambda: act(self.half(slot, 0, 1)))

    def extra(self):
        at = self.at
        if self.balanced:
            slot = at.o * 2 + 1 - at.i
            pl.when(at.end | at.next)(lambda: self.copy(slot, 2).wait_recv())
            self.extra_copies(lambda c: c.start())

    def arrive(self):
        at = self.at
        self.local_copy().wait()
        for layer in range(at.m):
            slot = layer * 2 + 1 - at.i
            if not self.balanced:
                self.copy(slot, 2).wait_recv()
                continue
            met = (at.o == layer) & (at.end | at.next)
            halved = at.end & (at.partner == layer)
            pl.when(jnp.logical_not(met | halved))(lambda: self.copy(slot, 2).wait_recv())

            @pl.when(halved)
            def _():
                self.half(slot, 2, 0).wait_recv()
                self.half(slot, 2, 1).wait_recv()

    def drain(self):
        at = self.at
        pl.when(at.has_right)(lambda: self.copy(at.s, 0, True).wait_send())
        pl.when(at.has_left)(lambda: self.copy(at.s, 1, True).wait_send())
        self.copy(at.s, 2, True).wait_send()
        for k in range(1, at.m):
            for way in (0, 1):
                slot = at.s - 2 * k if way == 0 else at.s + 2 * k
                there = at.o - k >= 0 if way == 0 else at.o + k < at.m
                on = at.has_right if way == 0 else at.has_left

                @pl.when(there)
                def _(slot=slot, on=on, way=way):
                    pl.when(on)(lambda: self.copy(slot, way).wait_send())
                    self.to_pair(slot, lambda c: c.wait_send())

        if self.balanced:
            self.extra_copies(lambda c: c.wait_send())


def add_rows(total, part, start, rows):
    step = next(size for size in (64, 32, 16, 8) if rows % size == 0)

    @pl.loop(0, rows // step)
    def _(j):
        at = pl.ds(pl.multiple_of(start + j * step, 8), step)
        both = total[at, :].astype(jnp.float32) + part[at, :].astype(jnp.float32)
        total[at, :] = both.astype(total.dtype)


class Scatter:
    def __init__(self, at, parts, out, landing, bufs, sems, balanced):
        self.at, self.parts, self.out = at, parts, out
        self.balanced = at.balanced and balanced
        self.from_pair, self.from_line, self.shifted_in = landing
        self.mine, self.aside, self.stage = bufs
        (
            self.pair_send,
            self.pair_recv,
            self.line_send,
            self.line_recv,
            self.extra_send,
            self.extra_recv,
            self.local,
        ) = sems
        self.rows = self.mine.shape[1]
        self.cut = self.rows * SCATTER_CUT // 8

    @staticmethod
    def landing(n, shape, dtype):
        m = n // 2
        return [jax.ShapeDtypeStruct((size,) + shape, dtype) for size in (m, m + 1, 1)]

    @staticmethod
    def scratch(n, shape, dtype):
        m = n // 2
        return [pltpu.VMEM((size,) + shape, dtype) for size in (m, 1)] + [
            pltpu.SemaphoreType.DMA((m,)),
            pltpu.SemaphoreType.DMA((m,)),
            pltpu.SemaphoreType.DMA((m,)),
            pltpu.SemaphoreType.DMA((m + 1,)),
            pltpu.SemaphoreType.DMA((2,)),
            pltpu.SemaphoreType.DMA((2,)),
            pltpu.SemaphoreType.DMA((m + 4,)),
        ]

    def slot(self, slot):
        if self.parts.ndim == 3:
            return self.parts.at[slot]
        return self.parts.at[pl.ds(pl.multiple_of(slot * self.rows, 16), self.rows)]

    def load(self, layer):
        return pltpu.make_async_copy(
            self.slot(layer * 2 + self.at.i), self.mine.at[layer], self.local.at[layer]
        )

    def load_aside(self):
        at = self.at
        return pltpu.make_async_copy(
            self.slot(at.o * 2 + 1 - at.i), self.aside.at[0], self.local.at[at.m]
        )

    def store(self):
        at = self.at
        return pltpu.make_async_copy(self.mine.at[at.o], self.out, self.local.at[at.m + 1])

    def to_stage(self, src, which, start=0, rows=None):
        part = pl.ds(start, self.rows if rows is None else rows)
        return pltpu.make_async_copy(
            src.at[part], self.stage.at[which, part], self.local.at[self.at.m + 2 + which]
        )

    def to_pair(self, layer):
        return remote(
            self.slot(layer * 2 + 1 - self.at.i),
            self.from_pair.at[layer],
            self.pair_send.at[layer],
            self.pair_recv.at[layer],
            self.at.pair,
        )

    def half_to_pair(self, layer, which, src):
        cut = self.cut
        part = pl.ds(which * cut, (cut, self.rows - cut)[which])
        return remote(
            src.at[part],
            self.from_pair.at[layer, part],
            self.pair_send.at[layer] if which == 0 else self.extra_send.at[1],
            self.pair_recv.at[layer] if which == 0 else self.extra_recv.at[1],
            self.at.pair,
        )

    def sum_to_pair(self):
        return remote(
            self.aside.at[0],
            self.from_pair.at[self.at.o],
            self.pair_send.at[self.at.o],
            self.pair_recv.at[self.at.o],
            self.at.pair,
        )

    def along(self, layer, way):
        at = self.at
        there = layer if way == 0 else jnp.where(layer == at.o - 1, at.m, layer)
        return remote(
            self.mine.at[layer],
            self.from_line.at[there],
            self.line_send.at[layer],
            self.line_recv.at[there],
            (at.right, at.left)[way],
        )

    def wait_line(self, place):
        remote(
            self.mine.at[0],
            self.from_line.at[place],
            self.line_send.at[0],
            self.line_recv.at[place],
            self.at.right,
        ).wait_recv()

    def shifted(self, way, which=None):
        at, cut = self.at, self.cut
        src, dst = self.slot(at.partner * 2 + 1 - at.i), self.shifted_in.at[0]
        if which is not None:
            part = pl.ds(cut, self.rows - cut)
            src, dst = src.at[part], dst.at[part]
        return remote(
            src, dst, self.extra_send.at[0], self.extra_recv.at[0], (at.right, at.left)[way]
        )

    def far_first(self):
        at = self.at
        for d in range(at.m - 1, 0, -1):
            yield at.o + d, at.o + d < at.m
            yield at.o - d, at.o - d >= 0

    def pair_copies(self, act):
        at = self.at
        for layer, there in self.far_first():
            if not self.balanced:
                pl.when(there)(lambda: act(self.to_pair(layer)))
                continue
            partner = layer == at.partner
            pl.when(there & jnp.logical_not(partner & (at.end | at.next)))(
                lambda: act(self.to_pair(layer))
            )
            pl.when(there & partner & at.end)(
                lambda: act(self.half_to_pair(layer, 0, self.slot(layer * 2 + 1 - at.i)))
            )
        if not self.balanced:
            act(self.to_pair(at.o))
            return
        pl.when(jnp.logical_not(at.end | at.next))(lambda: act(self.to_pair(at.o)))
        pl.when(at.next)(
            lambda: act(self.half_to_pair(at.o, 0, self.slot(at.o * 2 + 1 - at.i)))
        )

    def shift_copies(self, act):
        at = self.at
        if self.balanced:
            pl.when(at.o == 0)(lambda: act(self.shifted(0, 1)))
            pl.when(at.o == at.m - 1)(lambda: act(self.shifted(1, 1)))
            pl.when(at.o == 1)(lambda: act(self.shifted(1)))
            pl.when(at.o == at.m - 2)(lambda: act(self.shifted(0)))

    def start(self):
        at = self.at
        self.shift_copies(lambda c: c.start())
        self.pair_copies(lambda c: c.start())
        for layer in range(at.m):
            self.load(layer).start()
        if self.balanced:
            self.load_aside().start()

    def extra(self):
        at = self.at
        if not self.balanced:
            return
        self.load_aside().wait()
        cut, landed = self.cut, self.shifted_in.at[0]
        left = self.rows - cut

        @pl.when(at.end)
        def _():
            self.shifted(0).wait_recv()
            self.to_stage(landed, 0).start()
            self.to_stage(landed, 0).wait()
            add_rows(self.aside.at[0], self.stage.at[0], 0, self.rows)
            self.sum_to_pair().start()

        @pl.when(at.next)
        def _():
            self.shifted(0, 1).wait_recv()
            self.to_stage(landed, 0, cut, left).start()
            self.to_stage(landed, 0, cut, left).wait()
            add_rows(self.aside.at[0], self.stage.at[0], cut, left)
            self.half_to_pair(at.o, 1, self.aside.at[0]).start()

    def wait_pair(self, layer):
        at = self.at
        if not self.balanced:
            self.to_pair(layer).wait_recv()
            return
        partner, own = layer == at.partner, layer == at.o
        parted = (partner & at.end) | (own & at.next)
        pl.when(jnp.logical_not((partner & (at.end | at.next)) | (own & at.next)))(
            lambda: self.to_pair(layer).wait_recv()
        )
        pl.when(parted)(lambda: self.half_to_pair(layer, 0, self.aside.at[0]).wait_recv())
        pl.when(own & at.next)(lambda: self.half_to_pair(layer, 1, self.aside.at[0]).wait_recv())

    def step(self, d):
        at = self.at
        for way in (0, 1):
            layer = at.o + d if way == 0 else at.o - d
            there = layer < at.m if way == 0 else layer >= 0
            behind = at.has_left if way == 0 else at.has_right

            @pl.when(there)
            def _(layer=layer, behind=behind, way=way):
                mine, paired, half = self.mine.at[layer], self.from_pair.at[layer], self.cut
                self.load(layer).wait()
                self.wait_pair(layer)
                partner = (layer == at.partner) & self.balanced
                whole = jnp.logical_not(partner & (at.end | at.next))
                halved = partner & at.end
                pl.when(whole)(lambda: self.to_stage(paired, 0).start())
                pl.when(halved)(lambda: self.to_stage(paired, 0, 0, half).start())

                @pl.when(behind)
                def _():
                    self.wait_line(layer)
                    self.to_stage(self.from_line.at[layer], 1).start()

                @pl.when(whole)
                def _():
                    self.to_stage(paired, 0).wait()
                    add_rows(mine, self.stage.at[0], 0, self.rows)

                @pl.when(halved)
                def _():
                    self.to_stage(paired, 0, 0, half).wait()
                    add_rows(mine, self.stage.at[0], 0, half)

                @pl.when(behind)
                def _():
                    self.to_stage(self.from_line.at[layer], 1).wait()
                    add_rows(mine, self.stage.at[1], 0, self.rows)

                self.along(layer, way).start()

    def final(self):
        at = self.at
        mine = self.mine.at[at.o]
        self.load(at.o).wait()
        self.wait_pair(at.o)
        self.to_stage(self.from_pair.at[at.o], 0).start()

        @pl.when(at.has_left)
        def _():
            self.wait_line(at.o)
            self.to_stage(self.from_line.at[at.o], 1).start()

        self.to_stage(self.from_pair.at[at.o], 0).wait()
        add_rows(mine, self.stage.at[0], 0, self.rows)

        @pl.when(at.has_right)
        def _():
            self.wait_line(at.m)
            self.to_stage(self.from_line.at[at.m], 0).start()

        @pl.when(at.has_left)
        def _():
            self.to_stage(self.from_line.at[at.o], 1).wait()
            add_rows(mine, self.stage.at[1], 0, self.rows)

        @pl.when(at.has_right)
        def _():
            self.to_stage(self.from_line.at[at.m], 0).wait()
            add_rows(mine, self.stage.at[0], 0, self.rows)

        self.store().start()

    def drain(self):
        at = self.at
        self.pair_copies(lambda c: c.wait_send())
        if self.balanced:
            pl.when(at.end)(lambda: self.sum_to_pair().wait_send())
            pl.when(at.next)(lambda: self.half_to_pair(at.o, 1, self.aside.at[0]).wait_send())
        self.shift_copies(lambda c: c.wait_send())
        for d in range(1, at.m):
            pl.when(at.o + d < at.m)(lambda: self.along(at.o + d, 0).wait_send())
            pl.when(at.o - d >= 0)(lambda: self.along(at.o - d, 1).wait_send())
        self.store().wait()


def fetch(src, dst, sem):
    return pltpu.make_async_copy(src, dst, sem)


def dot(a, b, dims=((1,), (0,))):
    return lax.dot_general(a, b, (dims, ((), ())), preferred_element_type=jnp.float32)


ROWS, COLS, BOTH = ((1,), (0,)), ((1,), (1,)), ((0,), (0,))


def row_start(lengths, position):
    at, start = jnp.int32(0), jnp.zeros_like(position)
    for k in range(lengths.shape[0]):
        start = jnp.maximum(start, jnp.where(at <= position, at, 0))
        at = at + lengths[k]
    return start


def lanes(shape):
    return lax.broadcasted_iota(jnp.int32, shape, len(shape) - 1)


def feature_maps(width):
    count = FEAT + 1 + FEAT * (FEAT + 1) // 2
    wide = -(-count // 128) * 128
    first, second = np.zeros((width, wide), np.float32), np.zeros((width, wide), np.float32)
    plus = np.zeros((3, wide), np.float32)
    plus[:, 0] = 1.0
    heads = np.arange(width // FEAT) * FEAT
    for i in range(FEAT):
        first[heads + i, 1 + i] = 1.0
        plus[1:, 1 + i] = 1.0, 0.25
    at = 1 + FEAT
    for i in range(FEAT):
        for j in range(i, FEAT):
            first[heads + i, at] = 1.0
            second[heads + j, at] = 1.0
            plus[2, at] = 1 / 32 if i == j else 1 / 16
            at += 1
    tall = -(-count // 16) * 16
    return (
        jnp.asarray(np.stack([first, second]), jnp.bfloat16),
        jnp.asarray(np.stack([first.T, second.T])[:, :tall], jnp.bfloat16),
        jnp.asarray(np.repeat(plus[:, None], 8, 1)),
        jnp.asarray(np.repeat(plus[:, :tall, None], 128, 2)),
    )


class Team:
    def __init__(self, at, rows):
        self.at, self.half, self.quarter = at, rows // 2, rows // 4
        t = at.t
        low, high = lax.rem(t, 2), t // 2
        self.near, self.far = (at.s, t + 1 - 2 * low), (at.s, lax.rem(t + 2, 4))
        self.half_at, self.other_half_at = low * self.half, (1 - low) * self.half
        self.quarter_at = self.half_at + high * self.quarter
        self.other_quarter_at = self.half_at + (1 - high) * self.quarter
        self.in_half, self.other_in_half = high * self.quarter, (1 - high) * self.quarter
        self.near_quarter_at = self.other_half_at + high * self.quarter
        self.near_other_at = self.other_half_at + (1 - high) * self.quarter


class Sum:
    pieces = 4

    def __init__(self, team, part, from_near, from_far, sems):
        self.team, self.part, self.from_near, self.from_far = team, part, from_near, from_far
        self.near_send, self.near_recv, self.far_send, self.far_recv = sems
        self.wide = part.shape[1] // self.pieces

    @staticmethod
    def scratch(rows, columns):
        return [
            pltpu.VMEM((rows // 2, columns), jnp.bfloat16),
            pltpu.VMEM((rows // 4, columns), jnp.bfloat16),
        ] + [pltpu.SemaphoreType.DMA((Sum.pieces,))] * 4

    def near(self, j):
        team, columns = self.team, pl.ds(j * self.wide, self.wide)
        return remote(
            self.part.at[pl.ds(pl.multiple_of(team.other_half_at, team.half), team.half), columns],
            self.from_near.at[:, columns],
            self.near_send.at[j],
            self.near_recv.at[j],
            team.near,
        )

    def far(self, j):
        team, columns = self.team, pl.ds(j * self.wide, self.wide)
        at = pl.multiple_of(team.other_quarter_at, team.quarter)
        return remote(
            self.part.at[pl.ds(at, team.quarter), columns],
            self.from_far.at[:, columns],
            self.far_send.at[j],
            self.far_recv.at[j],
            team.far,
        )

    def fold(self, j):
        team, columns = self.team, pl.ds(j * self.wide, self.wide)
        self.near(j).wait_recv()
        step = 64

        @pl.loop(0, team.quarter // step)
        def _(r):
            to = pl.ds(pl.multiple_of(team.other_quarter_at + r * step, step), step)
            of = pl.ds(pl.multiple_of(team.other_in_half + r * step, step), step)
            both = self.part[to, columns].astype(jnp.float32)
            both = both + self.from_near[of, columns].astype(jnp.float32)
            self.part[to, columns] = both.astype(jnp.bfloat16)

        self.far(j).start()

    def arrive(self):
        for j in range(self.pieces):
            self.far(j).wait_recv()

    def rows(self, start, count):
        team = self.team
        a = self.part[pl.ds(pl.multiple_of(team.quarter_at + start, 16), count), :]
        b = self.from_near[pl.ds(pl.multiple_of(team.in_half + start, 16), count), :]
        c = self.from_far[pl.ds(pl.multiple_of(start, 16), count), :]
        return a.astype(jnp.float32) + b.astype(jnp.float32) + c.astype(jnp.float32)

    def drain(self):
        for j in range(self.pieces):
            self.near(j).wait_send()
            self.far(j).wait_send()


class Spread:
    pieces = 4

    def __init__(self, team, whole, sems):
        self.team, self.whole = team, whole
        self.far_send, self.far_recv, self.near_send, self.near_recv, self.on_send, self.on_recv = (
            sems
        )
        self.tall = team.quarter // self.pieces

    @staticmethod
    def scratch():
        return [pltpu.SemaphoreType.DMA((Spread.pieces,))] * 6

    def copy(self, start, j, send, recv, device):
        rows = self.whole.at[pl.ds(pl.multiple_of(start + j * self.tall, self.tall), self.tall)]
        return remote(rows, rows, send.at[j], recv.at[j], device)

    def far(self, j):
        team = self.team
        return self.copy(team.quarter_at, j, self.far_send, self.far_recv, team.far)

    def near(self, j):
        team = self.team
        return self.copy(team.quarter_at, j, self.near_send, self.near_recv, team.near)

    def on(self, j):
        team = self.team
        return self.copy(team.other_quarter_at, j, self.on_send, self.on_recv, team.near)

    def send(self, j):
        self.far(j).start()
        self.near(j).start()

    def pass_on(self, j):
        self.far(j).wait_recv()
        self.on(j).start()

    def arrive(self):
        for j in range(self.pieces):
            self.near(j).wait_recv()
            self.on(j).wait_recv()

    def drain(self):
        for j in range(self.pieces):
            self.far(j).wait_send()
            self.near(j).wait_send()
            self.on(j).wait_send()


class Pump:
    def __init__(self, events):
        self.events = list(events)

    def __call__(self, count):
        for _ in range(min(count, len(self.events))):
            self.events.pop(0)()

    def until(self, event):
        while event in self.events:
            self.events.pop(0)()

    def rest(self):
        self(len(self.events))


def gain_row(gains, which, row):
    n, depth = gains.shape[0], gains.shape[2] // 2
    for s in range(n):
        part = gains[s, 0:8, which * depth : (which + 1) * depth]
        row[:, s * depth : (s + 1) * depth] = part


def scores(query, key, mask):
    s = dot(query, key, COLS) * 0.25
    return 1.0 + s, jnp.where(mask, 1.0 + s + 0.5 * s * s, 0.0)


def pair_mask(row_starts, column_starts, first_row, first_column):
    shape = (row_starts.shape[0], column_starts.shape[1])
    rows = lax.broadcasted_iota(jnp.int32, shape, 0) + first_row
    columns = lax.broadcasted_iota(jnp.int32, shape, 1) + first_column
    return (row_starts == column_starts) & (columns <= rows)


def of_head(values, h):
    lane = lanes((1, values.shape[1]))
    mine = (lane >= h * FEAT) & (lane < (h + 1) * FEAT)
    return jnp.where(mine, values, jnp.zeros_like(values))


def column(values, h):
    return jnp.sum(jnp.where(lanes((1, 128)) == h, values, 0.0), axis=1, keepdims=True)


def with_ones(values):
    return jnp.concatenate([values, jnp.ones_like(values)], axis=1)


def forward_kernel(n, sizes, *refs):
    (
        lengths, stream_h, cot_h, maps, maps_t, plus, plus_t,
        gains_own, query_h, key_h, value_h, out_raw_h, gate_raw_h, up_raw_h, down_raw_h,
        gains_h, qkv_h, out_h, gate_h, up_h, down_h,
        h_one_h, heads_h, mixed_h, rden_h, state_h, mid_h, h_two_h, gate_v_h, up_v_h, hid_h, part_h,
        query_own, key_own, value_own, out_raw, gate_raw, up_raw, down_raw,
        qkv_own, out_own, gate_own, up_own, down_own,
        stream, h_one, heads, w_qkv, w_out, mixed, rden, numer, mid, h_two, w_ff,
        gate_v, up_v, hid, part, gains, gain,
        t_own, t_pair, t_line, t_next, state, t_send, t_recv, local, part_sem,
        *sems,
    ) = refs
    rows, width = stream.shape
    heads_here = mixed.shape[1] // 128
    q_wide = heads_here * FEAT
    at = Place(n)
    team = Team(at, rows)
    near_sum, sems = sems[:6], sems[6:]
    spread_sems, sems = sems[:6], sems[6:]
    tall_half = down_own.shape[0] // 2
    down_halves = [(down_own.at[pl.ds(k * tall_half, tall_half)], down_h, (k, 2)) for k in range(2)]
    arrays = [
        (gains_own, gains_h, (0, 1)),
        (qkv_own, qkv_h, (0, 1)),
        (out_own, out_h, (0, 1)),
        (gate_own, gate_h, (0, 1)),
        (up_own, up_h, (0, 1)),
        *down_halves,
    ]
    groups = [
        Gather(at, own, whole, sems[4 * g : 4 * g + 4], g > 0, part)
        for g, (own, whole, part) in enumerate(arrays)
    ]
    g_gains, g_qkv, g_out, g_gate, g_up, g_down, g_rest = groups
    cell = iter(range(local.shape[0]))
    copies = []

    def load(src, dst):
        copy = fetch(src, dst, local.at[next(cell)])
        copy.start()
        return copy

    def save(src, dst):
        copies.append(load(src, dst))

    raw = [
        load(query_h, query_own),
        load(key_h, key_own),
        load(value_h, value_own),
        load(out_raw_h, out_raw),
        load(gate_raw_h, gate_raw),
        load(up_raw_h, up_raw),
        load(down_raw_h, down_raw),
    ]
    get_stream = load(stream_h, stream)
    at.greet((team.near, team.far))
    pump = Pump([])

    def queue(group, *steps):
        for k in steps:
            pump.events.append(functools.partial(group.step, k) if isinstance(k, int) else k)

    last = at.m - 1
    def values_here():
        pass

    queue(g_gains, 1)
    for k in range(2, last + 1):
        queue(g_gains, k)
        queue(g_qkv, k - 1)
        if k == 2:
            queue(g_qkv, g_qkv.extra)
    queue(g_gains, g_gains.extra, g_out.own)
    queue(g_qkv, last, values_here)
    queue(g_out, 1, *range(2, last), g_out.extra, last)

    def feed_forward_here():
        pass

    queue(g_gate, 1, g_gate.extra)
    for k in range(2, last + 1):
        queue(g_gate, k)
        queue(g_up, k - 1)
        if k == 2:
            queue(g_up, g_up.extra)
    queue(g_down, g_down.own, g_rest.own)
    queue(g_up, last, feed_forward_here)
    for k in range(1, last + 1):
        for group in (g_down, g_rest):
            queue(group, k)
            if k == 1:
                queue(group, group.extra)
    g_gains.own()
    for copy in raw[:3]:
        copy.wait()
    qkv_own[:, 0:q_wide] = query_own[...].T
    qkv_own[:, q_wide : 2 * q_wide] = key_own[...].T
    qkv_own[:, 2 * q_wide :] = value_own[...]
    g_qkv.own()
    for copy, turned, own in zip(
        raw[3:], (out_raw, gate_raw, up_raw, down_raw), (out_own, gate_own, up_own, down_own)
    ):
        copy.wait()
        own[...] = turned[...].T
    pump.until(g_gains.extra)
    g_gains.arrive()
    load(gains_h, gains).wait()
    gain_row(gains, 0, gain.at[0])
    gain_row(gains, 1, gain.at[1])
    get_stream.wait()

    @pl.loop(0, rows // 64)
    def _(j):
        here = pl.ds(pl.multiple_of(j * 64, 64), 64)
        x = stream[here, :].astype(jnp.float32)
        scale = lax.rsqrt(jnp.mean(x * x, axis=1, keepdims=True) + EPSILON)
        h_one[here, :] = (x * scale * gain[0, 0:1, :]).astype(jnp.bfloat16)

    save(h_one, h_one_h)
    pump.until(values_here)
    pump(1)
    g_gate.own()
    g_qkv.arrive()
    load(qkv_h, w_qkv).wait()

    @pl.loop(0, rows // 256)
    def _(j):
        here = pl.ds(pl.multiple_of(j * 256, 256), 256)
        heads[here, :] = dot(h_one[here, :], w_qkv[...]).astype(jnp.bfloat16)

    save(heads, heads_h)
    pump(1)
    first = at.s * rows
    starts_col = row_start(lengths, first + lax.broadcasted_iota(jnp.int32, (rows, 1), 0))
    starts_row = row_start(lengths, first + lax.broadcasted_iota(jnp.int32, (1, rows), 1))
    last = row_start(lengths, first + rows - 1)
    keep = jnp.where(starts_row == last, 1.0, 0.0)
    tall = t_own.shape[1]

    def values_of(h):
        return pl.ds(pl.multiple_of(2 * q_wide + h * 128, 128), 128)

    t_sum = numer.at[0, 0:tall, 0:128]
    t_sum[...] = jnp.zeros((tall, 128), jnp.float32)

    @pl.loop(0, heads_here)
    def _(h):
        key = of_head(heads[:, q_wide : 2 * q_wide], h)
        one = dot(maps_t[0], key, COLS) + plus_t[0][:, 0:1]
        two = dot(maps_t[1], key, COLS) + plus_t[1][:, 0:1]
        phi = (one * two * keep).astype(jnp.bfloat16)
        total = dot(phi, with_ones(heads[:, values_of(h)]))
        t_own[h] = total[:, :128].astype(jnp.bfloat16)
        t_sum[...] += jnp.where(lanes((tall, 128)) == h, total[:, 128:], 0.0)

    t_own[heads_here] = t_sum[...].astype(jnp.bfloat16)
    to_pair = remote(t_own, t_pair, t_send.at[0], t_recv.at[0], at.pair)
    to_right = remote(t_next, t_line, t_send.at[1], t_recv.at[1], at.right)
    to_pair.start()
    pump(1)
    tile = 256

    @pl.loop(0, heads_here)
    def _(h):
        key = heads[:, q_wide : 2 * q_wide]
        for j in range(rows // tile):
            upto = (j + 1) * tile
            query = of_head(heads[j * tile : upto, 0:q_wide], h)
            mask = pair_mask(starts_col[j * tile : upto], starts_row[:, :upto], j * tile, 0)
            _, weights = scores(query, key[:upto], mask)
            values = with_ones(heads[0:upto, values_of(h)])
            numer[h, j * tile : upto, :] = dot(weights.astype(jnp.bfloat16), values)

    pump(2)

    def closed(s):
        return jnp.where(row_start(lengths, (s + 1) * rows - 1) >= s * rows, 0.0, 1.0)

    on_one, on_two = closed(at.o * 2), closed(at.o * 2 + 1)

    @pl.when(at.o == 0)
    def _():
        t_line[...] = jnp.zeros_like(t_line)

    to_pair.wait_recv()
    pl.when(at.has_left)(lambda: to_right.wait_recv())
    for h in range(heads_here + 1):
        mine, other = t_own[h].astype(jnp.float32), t_pair[h].astype(jnp.float32)
        t_one, t_two = jnp.where(at.i == 0, mine, other), jnp.where(at.i == 0, other, mine)
        come = t_line[h].astype(jnp.float32)
        middle = t_one + on_one * come
        t_next[h] = (t_two + on_two * middle).astype(jnp.bfloat16)
        state[h] = jnp.where(at.i == 0, come, middle).astype(jnp.bfloat16)
    pl.when(at.has_right)(lambda: to_right.start())
    g_up.own()
    save(state, state_h)
    pump(2)

    rden[...] = jnp.zeros_like(rden)
    @pl.loop(0, heads_here)
    def _(h):
        own = lanes((tall, 128)) == h
        dens = jnp.sum(jnp.where(own, state[heads_here].astype(jnp.float32), 0.0), 1, keepdims=True)
        dens = jnp.broadcast_to(dens, (tall, 128)).astype(jnp.bfloat16)
        table = jnp.concatenate([state[h], dens], axis=1)
        table = jnp.concatenate(
            [table, jnp.zeros((maps.shape[2] - tall, 256), jnp.bfloat16)], axis=0
        )
        for j in range(rows // tile):
            here = slice(j * tile, (j + 1) * tile)
            query = of_head(heads[here, 0:q_wide], h)
            one = dot(query, maps[0]) + plus[0, 0:1, :]
            two = dot(query, maps[1]) + plus[1, 0:1, :]
            carried = jnp.where(starts_col[here] < first, 1.0, 0.0)
            phi = (one * two * plus[2, 0:1, :] * carried).astype(jnp.bfloat16)
            total = numer[h, here, :] + dot(phi, table)
            inverse = 1.0 / total[:, 128:]
            rden[here, :] = jnp.where(lanes((1, 128)) == h, inverse, rden[here, :])
            mixed[here, pl.ds(pl.multiple_of(h * 128, 128), 128)] = (
                total[:, :128] * inverse
            ).astype(jnp.bfloat16)

    save(mixed, mixed_h)
    save(rden, rden_h)
    pump.until(g_out.extra)
    g_out.arrive()
    load(out_h, w_out).wait()
    for copy in copies:
        copy.wait()
    copies.clear()

    part_sum = Sum(team, h_one, *near_sum[:2], near_sum[2:])
    for j in range(Sum.pieces):
        columns = slice(j * part_sum.wide, (j + 1) * part_sum.wide)

        @pl.loop(0, rows // 256)
        def _(r):
            here = pl.ds(pl.multiple_of(r * 256, 256), 256)
            h_one[here, columns] = dot(mixed[here, :], w_out[columns, :], COLS).astype(jnp.bfloat16)

        part_sum.near(j).start()
        if j:
            part_sum.fold(j - 1)
            pump(1)
    part_sum.fold(Sum.pieces - 1)
    part_sum.arrive()
    spread = Spread(team, h_two, spread_sems)
    for j in range(Spread.pieces):
        for k in range(spread.tall // 32):
            down = j * spread.tall + k * 32
            here = pl.ds(pl.multiple_of(team.quarter_at + down, 32), 32)
            x = part_sum.rows(down, 32) + stream[here, :].astype(jnp.float32)
            mid[down : down + 32, :] = x
            scale = lax.rsqrt(jnp.mean(x * x, axis=1, keepdims=True) + EPSILON)
            h_two[here, :] = (x * scale * gain[1, 0:1, :]).astype(jnp.bfloat16)
        spread.send(j)
    save(mid, mid_h)
    for j in range(Spread.pieces):
        pump((3, 1, 1, 1)[j])
        spread.pass_on(j)
    get_cot = load(cot_h, stream)
    spread.arrive()
    part_sum.drain()
    spread.drain()
    save(h_two, h_two_h)
    pump.until(feed_forward_here)
    g_gate.arrive()
    get_gate = load(gate_h, w_ff.at[0])
    g_up.arrive()
    load(up_h, w_ff.at[1]).wait()
    get_gate.wait()
    stages = 4
    for stage in range(stages):

        @pl.loop(0, rows // 128 // stages)
        def _(r):
            start = pl.multiple_of((stage * (rows // 128 // stages) + r) * 128, 128)
            here = pl.ds(start, 128)
            gate = dot(h_two[here, :], w_ff[0])
            up = dot(h_two[here, :], w_ff[1])
            hidden = gate * jax.nn.sigmoid(gate) * up
            gate_v[here, :] = gate.astype(jnp.bfloat16)
            up_v[here, :] = up.astype(jnp.bfloat16)
            hid[here, :] = hidden.astype(jnp.bfloat16)

        pump(1 if stage else 3)
    save(gate_v, gate_v_h)
    save(up_v, up_v_h)
    save(hid, hid_h)
    get_cot.wait()
    def to_hbm(s, slot):
        here = pl.ds(pl.multiple_of(s * 256, 256), 256)
        return fetch(part.at[slot], part_h.at[here], part_sem.at[slot])

    count = width // 256
    for half in range(2):

        @pl.loop(half * (count // 2), (half + 1) * (count // 2))
        def _(s):
            slot = lax.rem(s, 2)
            pl.when(s > 1)(lambda: to_hbm(s - 2, slot).wait())
            columns = pl.ds(pl.multiple_of(s * 256, 256), 256)
            part[slot] = dot(stream[:, columns], hid[...], BOTH).astype(jnp.bfloat16)
            to_hbm(s, slot).start()

        pump(1)
    for s in range(count - 2, count):
        to_hbm(s, s % 2).wait()
    pump.rest()
    g_down.arrive()
    g_rest.arrive()
    for group in groups:
        group.drain()
    to_pair.wait_send()
    pl.when(at.has_right)(lambda: to_right.wait_send())
    for copy in copies:
        copy.wait()


def forward(n, lengths, stream, cot, maps, shards):
    rows, width = stream.shape
    gains, query, key, value, out, gate, up, down = shards
    hidden, deep = gate.shape
    values = out.shape[0]
    qkv_wide = 2 * query.shape[0] + values
    heads_here = values // 128
    tall = maps[1].shape[1]
    bf, f32 = jnp.bfloat16, jnp.float32
    shape = jax.ShapeDtypeStruct
    wholes = [
        shape((n,) + gains.shape, f32),
        shape((width, qkv_wide), bf),
        shape((width, values), bf),
        shape((width, hidden), bf),
        shape((width, hidden), bf),
        shape((width, hidden), bf),
    ]
    kept = [
        shape((rows, width), bf),
        shape((rows, qkv_wide), bf),
        shape((rows, values), bf),
        shape((rows, 128), f32),
        shape((heads_here + 1, tall, 128), bf),
        shape((rows // 4, width), f32),
        shape((rows, width), bf),
        shape((rows, hidden), bf),
        shape((rows, hidden), bf),
        shape((rows, hidden), bf),
        shape((width, hidden), bf),
    ]
    state = (heads_here + 1, tall, 128)
    scratch = [pltpu.VMEM(a.shape, bf) for a in shards[1:]]
    scratch += [pltpu.VMEM((deep, wide), bf) for wide in (qkv_wide, values, hidden, hidden, hidden)]
    scratch += [
        pltpu.VMEM((rows, width), bf),
        pltpu.VMEM((rows, width), bf),
        pltpu.VMEM((rows, qkv_wide), bf),
        pltpu.VMEM((width, qkv_wide), bf),
        pltpu.VMEM((width, values), bf),
        pltpu.VMEM((rows, values), bf),
        pltpu.VMEM((rows, 128), f32),
        pltpu.VMEM((heads_here, rows, 256), f32),
        pltpu.VMEM((rows // 4, width), f32),
        pltpu.VMEM((rows, width), bf),
        pltpu.VMEM((2, width, hidden), bf),
        pltpu.VMEM((rows, hidden), bf),
        pltpu.VMEM((rows, hidden), bf),
        pltpu.VMEM((rows, hidden), bf),
        pltpu.VMEM((2, 256, hidden), bf),
        pltpu.VMEM((n,) + gains.shape, f32),
        pltpu.VMEM((2, 8, width), f32),
        pltpu.VMEM(state, bf),
        pltpu.VMEM(state, bf),
        pltpu.VMEM(state, bf),
        pltpu.VMEM(state, bf),
        pltpu.VMEM(state, bf),
        pltpu.SemaphoreType.DMA((2,)),
        pltpu.SemaphoreType.DMA((2,)),
        pltpu.SemaphoreType.DMA((32,)),
        pltpu.SemaphoreType.DMA((2,)),
    ]
    scratch += Sum.scratch(rows, width) + Spread.scratch() + Gather.scratch(n) * (len(wholes) + 1)
    anywhere, inside = pl.BlockSpec(memory_space=pl.ANY), pl.BlockSpec(memory_space=pltpu.VMEM)
    result = pl.pallas_call(
        functools.partial(forward_kernel, n, None),
        out_shape=wholes + kept,
        in_specs=[pl.BlockSpec(memory_space=pltpu.SMEM), anywhere, anywhere]
        + [inside] * 4
        + [anywhere] * len(shards),
        out_specs=[anywhere] * (len(wholes) + len(kept)),
        scratch_shapes=scratch,
        compiler_params=pltpu.CompilerParams(
            collective_id=0, has_side_effects=True, vmem_limit_bytes=62 * MIB
        ),
    )(lengths, stream, cot, *maps, *shards)
    return result[: len(wholes)], result[len(wholes) :]


class SpreadOut(Spread):
    def __init__(self, team, quarter, whole, sems):
        super().__init__(team, whole, sems[:-1])
        self.own, self.kept = quarter, sems[-1]

    @staticmethod
    def scratch():
        return Spread.scratch() + [pltpu.SemaphoreType.DMA((1,))]

    def own_copy(self, j, send, recv, device):
        start = self.team.quarter_at + j * self.tall
        rows = self.whole.at[pl.ds(pl.multiple_of(start, self.tall), self.tall)]
        src = self.own.at[pl.ds(j * self.tall, self.tall)]
        return remote(src, rows, send.at[j], recv.at[j], device)

    def far(self, j):
        return self.own_copy(j, self.far_send, self.far_recv, self.team.far)

    def near(self, j):
        return self.own_copy(j, self.near_send, self.near_recv, self.team.near)

    def keep(self):
        team = self.team
        rows = self.whole.at[pl.ds(pl.multiple_of(team.quarter_at, team.quarter), team.quarter)]
        return pltpu.make_async_copy(self.own, rows, self.kept.at[0])


def backward_kernel(n, *refs):
    (
        lengths, maps, maps_t, plus, plus_t,
        stream_h, cot_h, gains_h, qkv_h, out_h, gate_h, up_h, down_h,
        h_one_h, heads_h, mixed_h, rden_h, state_h, mid_h, h_two_h, gate_v_h, up_v_h, hid_h, part_h,
        *refs,
    ) = refs
    act_h, ig_h, *refs = refs
    outs, refs = refs[:6], refs[6:]
    parts, refs = [part_h] + refs[:5], refs[5:]
    landings, refs = refs[:18], refs[18:]
    (
        part, arena, d_mid, dm, gains, gain, gain_sum, gain_near, gain_far, gain_parts,
        t_own, t_pair, t_line, t_next, state, back, t_send, t_recv, gain_send, gain_recv, local,
        stage_g, stage_o, stage_q, stage_n,
        *sems,
    ) = refs
    rows, width = arena.shape
    hidden = gate_v_h.shape[1]
    values_wide = mixed_h.shape[1]
    heads_here = values_wide // 128
    q_wide = heads_here * FEAT
    at = Place(n)
    team = Team(at, rows)

    def take(count):
        nonlocal sems
        taken, sems = sems[:count], sems[count:]
        return taken

    sums = [take(6) for _ in range(2)]
    first_sems = take(4)
    dm_sems, act_sems, ig_sems = take(6), take(7), take(7)
    stages = (stage_g, stage_g, stage_g, stage_o, stage_q, stage_n)
    groups = []
    for g in range(6):
        mine, aside, *own_sems = take(9)
        groups.append(
            Scatter(
                at,
                parts[g],
                outs[g],
                landings[3 * g : 3 * g + 3],
                (mine, aside, stages[g]),
                own_sems,
                g < 3,
            )
        )
    s_down, s_gate, s_up, s_out, s_qkv, s_gains = groups
    at.greet((team.near, team.far))
    cell = iter(range(local.shape[0]))

    def load(src, dst):
        copy = fetch(src, dst, local.at[next(cell)])
        copy.start()
        return copy

    pump = Pump([])

    def begin(group):
        group.start()
        for d in range(at.m - 1, 0, -1):
            pump.events.append(functools.partial(group.step, d))
            if d == max(1, at.m - 2) and group.balanced:
                pump.events.append(group.extra)

    begin(s_down)
    get_gains = load(gains_h, gains)
    get_mid = load(mid_h, d_mid)
    part_sum = Sum(team, part, *sums[0][:2], sums[0][2:])
    feed_sum = Sum(team, part, *sums[1][:2], sums[1][2:])
    first_sum = Sum(team, part, *sums[0][:2], first_sems)
    spread = Spread(team, dm, dm_sems)
    ig_rows = team.quarter
    ig_spread = SpreadOut(team, arena.at[pl.ds(ig_rows, team.quarter)], ig_h, ig_sems)
    act_spread = SpreadOut(team, feed_sum.from_far, act_h, act_sems)
    piece = part_sum.wide

    def staged(sem, tile, parts_h, compute):
        count = width // 256

        def to_hbm(s, slot):
            here = pl.ds(pl.multiple_of(s * 256, 256), 256)
            return fetch(tile.at[slot], parts_h.at[here], sem.at[slot])

        @pl.loop(0, count)
        def _(s):
            slot = lax.rem(s, 2)
            pl.when(s > 1)(lambda: to_hbm(s - 2, slot).wait())
            columns = pl.ds(pl.multiple_of(s * 256, 256), 256)
            tile[slot] = compute(columns).astype(jnp.bfloat16)
            to_hbm(s, slot).start()

        for s in range(count - 2, count):
            to_hbm(s, s % 2).wait()

    def norm_back(x, grad, gain_ref, which):
        scale = lax.rsqrt(jnp.mean(x * x, axis=1, keepdims=True) + EPSILON)
        unit = x * scale
        total = jnp.sum((grad * unit).reshape(-1, 8, width), axis=0)
        gain_sum[8 * which : 8 * which + 8, :] += total
        scaled = grad * gain_ref[0:1, :]
        return scale * (scaled - unit * jnp.mean(scaled * unit, axis=1, keepdims=True))

    gain_sum[...] = jnp.zeros_like(gain_sum)

    def feed_forward(w_down, w_ff, ff, w_sem, tile_sem):
        get_cot = load(cot_h, arena)
        pieces = [(low, min(hidden, low + 512)) for low in range(0, hidden, 512)]
        get_pieces = [
            [
                load(src.at[:, low:high], dst.at[:, low:high])
                for src, dst in ((down_h, w_down), (gate_v_h, ff.at[0]), (up_v_h, ff.at[1]))
            ]
            for low, high in pieces
        ]
        tall = w_ff.shape[2]

        def weights(j, which):
            here = pl.ds(j * tall, tall)
            return fetch(
                (gate_h, up_h)[which].at[here], w_ff.at[j % 2, which], w_sem.at[j % 2, which]
            )

        for which in (0, 1):
            weights(0, which).start()
        get_cot.wait()
        block = 256
        for (low, high), gets in zip(pieces, get_pieces):
            for get in gets:
                get.wait()

            @pl.loop(0, rows // block)
            def _(r):
                here = pl.ds(pl.multiple_of(r * block, block), block)
                grad = dot(arena[here, :], w_down[:, low:high])
                gate = ff[0, here, low:high].astype(jnp.float32)
                sigma = jax.nn.sigmoid(gate)
                silu = gate * sigma
                up = ff[1, here, low:high].astype(jnp.float32)
                ff[0, here, low:high] = (grad * up * (sigma + silu * (1.0 - sigma))).astype(
                    jnp.bfloat16
                )
                ff[1, here, low:high] = (grad * silu).astype(jnp.bfloat16)

        pump(1)
        get_two = load(h_two_h, arena)
        count = width // tall
        for j in range(count):
            for which in (0, 1):
                if j + 1 < count:
                    weights(j + 1, which).start()
                weights(j, which).wait()

            @pl.loop(0, rows // 512)
            def _(r):
                here = pl.ds(pl.multiple_of(r * 512, 512), 512)
                grad = dot(ff[0, here, :], w_ff[j % 2, 0], COLS)
                grad += dot(ff[1, here, :], w_ff[j % 2, 1], COLS)
                part[here, j * tall : (j + 1) * tall] = grad.astype(jnp.bfloat16)

            if (j + 1) * tall % piece == 0:
                p = (j + 1) * tall // piece - 1
                part_sum.near(p).start()
                if p:
                    part_sum.fold(p - 1)
        part_sum.fold(Sum.pieces - 1)
        get_two.wait()
        pump(2)
        tile = w_ff.at[0]

        def grads(which):
            return lambda columns: dot(arena[:, columns], ff[which], BOTH)

        staged(tile_sem, tile, parts[1], grads(0))
        begin(s_gate)
        get_gains.wait()
        gain_row(gains, 0, gain.at[0])
        gain_row(gains, 1, gain.at[1])
        get_mid.wait()
        part_sum.arrive()
        quarter = pl.ds(pl.multiple_of(team.quarter_at, team.quarter), team.quarter)
        load(cot_h.at[quarter], dm.at[quarter]).wait()
        for j in range(Spread.pieces):

            @pl.loop(0, spread.tall // 32)
            def _(r):
                start = pl.multiple_of(j * spread.tall + r * 32, 32)
                here = pl.ds(pl.multiple_of(team.quarter_at + start, 32), 32)
                x = d_mid[pl.ds(start, 32), :]
                grad = norm_back(x, part_sum.rows(start, 32), gain.at[1], 1)
                grad = grad + dm[here, :].astype(jnp.float32)
                d_mid[pl.ds(start, 32), :] = grad
                dm[here, :] = grad.astype(jnp.bfloat16)

            spread.send(j)
        part_sum.drain()
        pump(1)
        staged(tile_sem, tile, parts[2], grads(1))
        get_hid = load(hid_h, ff.at[0])
        get_hid.wait()
        for j in range(Sum.pieces):
            columns = slice(j * piece, (j + 1) * piece)

            @pl.loop(0, rows // 512)
            def _(r):
                here = pl.ds(pl.multiple_of(r * 512, 512), 512)
                feed = dot(ff[0, here, :], w_down[columns, :], COLS)
                part[here, columns] = feed.astype(jnp.bfloat16)

            feed_sum.near(j).start()
            spread.pass_on(j)
            if j == Sum.pieces - 2:
                pump(1)


    pl.run_scoped(
        feed_forward,
        pltpu.VMEM(down_h.shape, jnp.bfloat16),
        pltpu.VMEM((2, 2, 256, hidden), jnp.bfloat16),
        pltpu.VMEM((2, rows, hidden), jnp.bfloat16),
        pltpu.SemaphoreType.DMA((2, 2)),
        pltpu.SemaphoreType.DMA((2,)),
    )

    def attention(
        heads, d_heads, mixed, w_out, w_qkv, delta, g, delta_row, d_query, d_key,
        dens, tile_o, tile_q, tile_sem, d_values, mid_part, mid_sem, qkv_sem,
    ):
        gets = [
            load(heads_h, heads),
            load(mixed_h, mixed),
            load(out_h, w_out),
            load(rden_h, delta),
            load(state_h, state),
        ]
        get_one = load(h_one_h, arena)

        def mid_rows(j):
            here = pl.ds(j * act_spread.tall, act_spread.tall)
            return fetch(mid_h.at[here], mid_part.at[j % 2], mid_sem.at[j % 2])

        def qkv_rows(j):
            here = pl.ds(j * piece, piece)
            return fetch(qkv_h.at[here], w_qkv.at[j % 2], qkv_sem.at[j % 2])

        for j in range(2):
            mid_rows(j).start()
            qkv_rows(j).start()
        for get in gets:
            get.wait()
        spread.arrive()

        @pl.loop(0, rows // 256)
        def _(r):
            here = pl.ds(pl.multiple_of(r * 256, 256), 256)
            d_values[here, :] = dot(dm[here, :], w_out[...])

        for j in range(Sum.pieces):
            feed_sum.fold(j)

        @pl.loop(0, heads_here)
        def _(h):
            across = pl.ds(pl.multiple_of(h * 128, 128), 128)
            grad = d_values[:, across] * column(delta[...], h)
            g[h] = grad.astype(jnp.bfloat16)
            sums_of = jnp.sum(grad * mixed[:, across].astype(jnp.float32), axis=1, keepdims=True)
            wide = jnp.broadcast_to(sums_of, (rows, 128))
            delta[...] = jnp.where(lanes((1, 128)) == h, wide, delta[...])
            delta_row[h] = wide.T[0:8]

        first = at.s * rows
        starts_col = row_start(lengths, first + lax.broadcasted_iota(jnp.int32, (rows, 1), 0))
        starts_row = row_start(lengths, first + lax.broadcasted_iota(jnp.int32, (1, rows), 1))
        last = row_start(lengths, first + rows - 1)
        tall = t_own.shape[1]
        wide = maps.shape[2]
        carried_row = jnp.where(starts_row < first, 1.0, 0.0)
        dens[1, 0:tall, 0:128] = jnp.zeros((tall, 128), jnp.float32)

        def values_of(h):
            return pl.ds(pl.multiple_of(2 * q_wide + h * 128, 128), 128)

        def head_at(h):
            return pl.ds(pl.multiple_of(h * 128, 128), 128)

        @pl.loop(0, heads_here)
        def _(h):
            query = of_head(heads[:, 0:q_wide], h)
            one = dot(maps_t[0], query, COLS) + plus_t[0][:, 0:1]
            two = dot(maps_t[1], query, COLS) + plus_t[1][:, 0:1]
            phi = one * two * plus_t[2][:, 0:1] * carried_row
            t_own[h] = dot(phi.astype(jnp.bfloat16), g[h]).astype(jnp.bfloat16)
            below = -jnp.sum(phi * delta_row[h][0:1, :], axis=1, keepdims=True)
            dens[1, 0:tall, 0:128] += jnp.where(lanes((tall, 128)) == h, below, 0.0)

        t_own[heads_here] = dens[1, 0:tall, 0:128].astype(jnp.bfloat16)
        to_pair = remote(t_own, t_pair, t_send.at[0], t_recv.at[0], at.pair)
        to_left = remote(t_next, t_line, t_send.at[1], t_recv.at[1], at.left)
        to_pair.start()
        begin(s_up)

        @pl.when(at.o == at.m - 1)
        def _():
            t_line[...] = jnp.zeros_like(t_line)

        def closed(s):
            return jnp.where(row_start(lengths, (s + 1) * rows - 1) >= s * rows, 0.0, 1.0)

        on_one, on_two = closed(at.o * 2), closed(at.o * 2 + 1)

        def relay():
            to_pair.wait_recv()
            pl.when(at.has_right)(lambda: to_left.wait_recv())

            @pl.loop(0, heads_here + 1)
            def _(h):
                mine, other = t_own[h].astype(jnp.float32), t_pair[h].astype(jnp.float32)
                t_one, t_two = jnp.where(at.i == 0, mine, other), jnp.where(at.i == 0, other, mine)
                come = t_line[h].astype(jnp.float32)
                middle = t_two + on_two * come
                t_next[h] = (t_one + on_one * middle).astype(jnp.bfloat16)
                back[h] = jnp.where(at.i == 0, middle, come).astype(jnp.bfloat16)

            pl.when(at.has_left)(lambda: to_left.start())

        turns = min(4, at.m)

        def turn(p):
            mine = at.o == at.m - 1 - p if p < turns - 1 else at.o <= at.m - turns
            pl.when(mine)(relay)

        d_query[...] = jnp.zeros_like(d_query)
        d_key[...] = jnp.zeros_like(d_key)
        tile = 128

        def intra(h):
            key, query = of_head(heads[:, q_wide : 2 * q_wide], h), of_head(heads[:, 0:q_wide], h)
            across = values_of(h)
            for j in range(rows // tile):
                here, upto = slice(j * tile, (j + 1) * tile), (j + 1) * tile
                mask = pair_mask(starts_col[here], starts_row[:, :upto], j * tile, 0)
                more, _ = scores(query[here], key[:upto], mask)
                d_weight = dot(g[h, here, :], heads[0:upto, across], COLS) - column(delta[here, :], h)
                d_score = jnp.where(mask, d_weight * more, 0.0).astype(jnp.bfloat16)
                d_query[here, :] += dot(d_score, key[:upto]) * 0.25
            for j in range(rows // tile):
                here, after = slice(j * tile, (j + 1) * tile), j * tile
                shape = (tile, rows - after)
                key_at = lax.broadcasted_iota(jnp.int32, shape, 0)
                query_at = lax.broadcasted_iota(jnp.int32, shape, 1)
                mask = (starts_col[here] == starts_row[:, after:]) & (key_at <= query_at)
                more, weight = scores(key[here], query[after:], mask)
                d_weight = dot(heads[here, across], g[h, after:, :], COLS)
                d_weight = d_weight - delta_row[h, 0:1, after:]
                d_score = jnp.where(mask, d_weight * more, 0.0).astype(jnp.bfloat16)
                d_values[here, head_at(h)] = dot(weight.astype(jnp.bfloat16), g[h, after:, :])
                grad = dot(d_score, query[after:]) * 0.25
                d_key[here, :] = jnp.where(h == 0, grad, d_key[here, :] + grad)

        for half in range(2):
            @pl.loop(half * heads_here // 2, (half + 1) * heads_here // 2)
            def _(h):
                intra(h)

            if half == 0:
                pump(1)
        turn(0)
        pump(1)

        def through(u, h, grad):
            one = dot(u, maps[0]) + plus[0, 0:1, :]
            two = dot(u, maps[1]) + plus[1, 0:1, :]
            grad = grad()
            left = dot((grad * two).astype(jnp.bfloat16), maps[0], COLS)
            left += dot((grad * one).astype(jnp.bfloat16), maps[1], COLS)
            return one * two, of_head(left, h)

        wider = 256

        def each_tile(body):
            @pl.loop(0, heads_here)
            def _(h):
                @pl.loop(0, rows // wider)
                def _(j):
                    here = pl.ds(pl.multiple_of(j * wider, wider), wider)
                    at_row = first + j * wider + lax.broadcasted_iota(jnp.int32, (wider, 1), 0)
                    body(h, here, row_start(lengths, at_row))

        filler = jnp.zeros((wide - tall, 128), jnp.bfloat16)
        dens[0] = jnp.zeros_like(dens[0])
        dens[0, 0:128, 0:tall] = state[heads_here].astype(jnp.float32).T

        def through_in(h, here, starts):
            carried = jnp.where(starts < first, 1.0, 0.0)

            def grad_phi():
                table = jnp.concatenate([state[h], filler], axis=0)
                grad = dot(g[h, here, :], table, COLS)
                grad = grad - column(delta[here, :], h) * dens[0, pl.ds(h, 1), :]
                return grad * plus[2, 0:1, :] * carried

            _, grad = through(of_head(heads[here, 0:q_wide], h), h, grad_phi)
            d_query[here, :] += grad

        each_tile(through_in)
        turn(1)
        pump(1)

        def grad_out(columns):
            return dot(dm[:, columns], mixed[...], BOTH)

        staged(tile_sem, tile_o, parts[3], grad_out)
        begin(s_out)
        turn(2)
        pump(1)
        feed_sum.arrive()
        for j in range(Spread.pieces):
            mid_rows(j).wait()

            @pl.loop(0, act_spread.tall // 32)
            def _(r):
                start = pl.multiple_of(j * act_spread.tall + r * 32, 32)
                x = mid_part[j % 2, pl.ds(pl.multiple_of(r * 32, 32), 32), :]
                x = x + feed_sum.rows(start, 32)
                feed_sum.from_far[pl.ds(start, 32), :] = x.astype(bf)

            if j + 2 < Spread.pieces:
                mid_rows(j + 2).start()
            act_spread.send(j)
        act_spread.keep().start()
        feed_sum.drain()
        for p in range(3, turns):
            turn(p)

        dens[1] = jnp.zeros_like(dens[1])
        dens[1, 0:128, 0:tall] = back[heads_here].astype(jnp.float32).T

        def through_out(h, here, starts):
            keep = jnp.where(starts == last, 1.0, 0.0)
            table = jnp.concatenate([back[h], filler], axis=0)

            def grad_phi():
                grad = dot(heads[here, values_of(h)], table, COLS)
                return (grad + dens[1, pl.ds(h, 1), :]) * keep

            phi, grad = through(of_head(heads[here, q_wide : 2 * q_wide], h), h, grad_phi)
            d_key[here, :] += grad
            far = dot((phi * keep).astype(jnp.bfloat16), table)
            d_heads[here, values_of(h)] = (d_values[here, head_at(h)] + far).astype(jnp.bfloat16)

        each_tile(through_out)
        d_heads[:, 0:q_wide] = d_query[...].astype(jnp.bfloat16)
        d_heads[:, q_wide : 2 * q_wide] = d_key[...].astype(jnp.bfloat16)
        pump(2)
        for j in range(Sum.pieces):
            columns = slice(j * piece, (j + 1) * piece)
            qkv_rows(j).wait()

            @pl.loop(0, rows // 256)
            def _(r):
                here = pl.ds(pl.multiple_of(r * 256, 256), 256)
                grad = dot(d_heads[here, :], w_qkv[j % 2], COLS)
                part[here, columns] = grad.astype(jnp.bfloat16)

            first_sum.near(j).start()
            if j + 2 < Sum.pieces:
                qkv_rows(j + 2).start()
            if j:
                first_sum.fold(j - 1)
        first_sum.fold(Sum.pieces - 1)

        pump(1)
        get_one.wait()

        def grad_qkv(columns):
            return dot(arena[:, columns], d_heads[...], BOTH)

        staged(tile_sem, tile_q, parts[4], grad_qkv)
        pump(1)
        begin(s_qkv)
        s_down.final()
        for j in range(Spread.pieces):
            act_spread.pass_on(j)
        to_pair.wait_send()
        pl.when(at.has_left)(lambda: to_left.wait_send())

    bf, f32 = jnp.bfloat16, jnp.float32
    pl.run_scoped(
        attention,
        pltpu.VMEM((rows, heads_h.shape[1]), bf),
        pltpu.VMEM((rows, heads_h.shape[1]), bf),
        pltpu.VMEM((rows, values_wide), bf),
        pltpu.VMEM(out_h.shape, bf),
        pltpu.VMEM((2, piece, qkv_h.shape[1]), bf),
        pltpu.VMEM((rows, 128), f32),
        pltpu.VMEM((heads_here, rows, 128), bf),
        pltpu.VMEM((heads_here, 8, rows), f32),
        pltpu.VMEM((rows, q_wide), f32),
        pltpu.VMEM((rows, q_wide), f32),
        pltpu.VMEM((2, maps.shape[2], maps.shape[2]), f32),
        pltpu.VMEM((2, 256, values_wide), bf),
        pltpu.VMEM((2, 256, heads_h.shape[1]), bf),
        pltpu.SemaphoreType.DMA((2,)),
        pltpu.VMEM((rows, values_wide), f32),
        pltpu.VMEM((2, act_spread.tall, width), f32),
        pltpu.SemaphoreType.DMA((2,)),
        pltpu.SemaphoreType.DMA((2,)),
    )

    quarter = pl.ds(pl.multiple_of(team.quarter_at, team.quarter), team.quarter)
    load(stream_h.at[quarter], arena.at[0 : team.quarter]).wait()
    first_sum.arrive()
    @pl.loop(0, team.quarter // 32)
    def _(r):
        start = pl.multiple_of(r * 32, 32)
        here = pl.ds(start, 32)
        x = arena[here, :].astype(f32)
        grad = norm_back(x, first_sum.rows(start, 32), gain.at[0], 0)
        arena[pl.ds(ig_rows + start, 32), :] = (d_mid[here, :] + grad).astype(bf)

    pump(1)
    gain_to_near = remote(gain_sum, gain_near, gain_send.at[0], gain_recv.at[0], team.near)
    gain_to_near.start()
    gain_to_near.wait()
    gain_sum[...] += gain_near[...]
    gain_to_far = remote(gain_sum, gain_far, gain_send.at[1], gain_recv.at[1], team.far)
    gain_to_far.start()
    for j in range(Spread.pieces):
        ig_spread.send(j)
    ig_spread.keep().start()
    pump(1)
    gain_to_far.wait()
    gain_near[...] = gain_sum[...] + gain_far[...]
    deep = width // n
    for s in range(n):
        gain_parts[s] = gain_near[:, s * deep : (s + 1) * deep]
    load(gain_parts, parts[5]).wait()
    begin(s_gains)
    pump(1)
    s_gate.final()
    pump(1)
    s_up.final()
    pump.rest()
    for group in groups[3:]:
        group.final()
    for j in range(Spread.pieces):
        ig_spread.pass_on(j)
    for spread_of in (ig_spread, act_spread):
        spread_of.arrive()
        spread_of.drain()
        spread_of.keep().wait()
    spread.drain()
    first_sum.drain()
    for group in groups:
        group.drain()


def backward(n, lengths, maps, stream, cot, wholes, kept):
    rows, width = stream.shape
    gains, qkv, out, gate, up, down = wholes
    heads_here = out.shape[1] // 128
    hidden = gate.shape[1]
    tall = maps[1].shape[1]
    bf, f32 = jnp.bfloat16, jnp.float32
    shape = jax.ShapeDtypeStruct
    deep = width // n
    kinds = [
        ((deep, hidden), bf),
        ((deep, hidden), bf),
        ((deep, hidden), bf),
        ((deep, out.shape[1]), bf),
        ((deep, qkv.shape[1]), bf),
        ((16, deep), f32),
    ]
    results = [shape((rows, width), bf)] * 2 + [shape(*kind) for kind in kinds]
    work = [shape((width, size[1]), kind) for size, kind in kinds[1:-1]]
    work += [shape((n,) + kinds[-1][0], f32)]
    work += sum((Scatter.landing(n, *kind) for kind in kinds), [])
    state = (heads_here + 1, tall, 128)
    scratch = [
        pltpu.VMEM((rows, width), bf),
        pltpu.VMEM((rows, width), bf),
        pltpu.VMEM((rows // 4, width), f32),
        pltpu.VMEM((rows, width), bf),
        pltpu.VMEM(gains.shape, f32),
        pltpu.VMEM((2, 8, width), f32),
        pltpu.VMEM((16, width), f32),
        pltpu.VMEM((16, width), f32),
        pltpu.VMEM((16, width), f32),
        pltpu.VMEM((n, 16, deep), f32),
    ]
    scratch += [pltpu.VMEM(state, bf)] * 6
    scratch += [pltpu.SemaphoreType.DMA((2,))] * 4
    scratch += [pltpu.SemaphoreType.DMA((24,))]
    scratch += [pltpu.VMEM((2,) + kinds[k][0], kinds[k][1]) for k in (0, 3, 4, 5)]
    scratch += Sum.scratch(rows, width) * 2 + Sum.scratch(rows, width)[2:] + Spread.scratch() + SpreadOut.scratch() * 2
    scratch += sum((Scatter.scratch(n, *kind) for kind in kinds), [])
    anywhere, inside = pl.BlockSpec(memory_space=pl.ANY), pl.BlockSpec(memory_space=pltpu.VMEM)
    given = [stream, cot, *wholes, *kept]
    result = pl.pallas_call(
        functools.partial(backward_kernel, n),
        out_shape=results + work,
        in_specs=[pl.BlockSpec(memory_space=pltpu.SMEM)] + [inside] * 4 + [anywhere] * len(given),
        out_specs=[anywhere] * (len(results) + len(work)),
        scratch_shapes=scratch,
        compiler_params=pltpu.CompilerParams(
            collective_id=1, has_side_effects=True, vmem_limit_bytes=63 * MIB
        ),
    )(lengths, *maps, *given)
    return result[: len(results)]


def finish_kernel(q_wide, *refs):
    act_h, ig_h, down_h, gate_h, up_h, out_h, qkv_h, *refs = refs
    act_o, ig_o, query_o, key_o, value_o, out_o, gate_o, up_o, down_o, *refs = refs
    act, ig, down, gate, up, out, qkv, *refs = refs
    ig_f, down_f, gate_f, up_f, out_f, query_f, key_f, value_f, get_sem, put_sem = refs
    parts = 8
    rows = ig.shape[0] // parts

    def get_rows(j):
        here = pl.ds(j * rows, rows)
        return fetch(ig_h.at[here], ig.at[here], get_sem.at[j])

    def put_rows(j):
        here = pl.ds(j * rows, rows)
        return fetch(ig_f.at[here], ig_o.at[here], put_sem.at[j])

    get_act, put_act = fetch(act_h, act, get_sem.at[parts]), fetch(act, act_o, get_sem.at[parts])
    gets = [
        fetch(src, dst, get_sem.at[parts + 1 + k])
        for k, (src, dst) in enumerate(
            ((down_h, down), (gate_h, gate), (up_h, up), (out_h, out), (qkv_h, qkv))
        )
    ]
    for j in range(parts):
        get_rows(j).start()
    for get in gets:
        get.start()
    get_act.start()
    for j in range(parts):
        get_rows(j).wait()

        @pl.loop(0, rows // 32)
        def _(r):
            here = pl.ds(pl.multiple_of(j * rows + r * 32, 32), 32)
            ig_f[here, :] = ig[here, :].astype(jnp.float32)

        put_rows(j).start()
    get_act.wait()
    put_act.start()
    puts = []

    def put(src, dst):
        puts.append(fetch(src, dst, put_sem.at[parts + len(puts)]))
        puts[-1].start()

    for get, src, mid, dst in zip(
        gets, (down, gate, up, out), (down_f, gate_f, up_f, out_f), (down_o, gate_o, up_o, out_o)
    ):
        get.wait()
        mid[...] = src[...].astype(jnp.float32).T
        put(mid, dst)
    gets[4].wait()
    query_f[...] = qkv[:, 0:q_wide].astype(jnp.float32).T
    key_f[...] = qkv[:, q_wide : 2 * q_wide].astype(jnp.float32).T
    value_f[...] = qkv[:, 2 * q_wide :].astype(jnp.float32)
    put(query_f, query_o)
    put(key_f, key_o)
    put(value_f, value_o)
    for j in range(parts):
        put_rows(j).wait()
    for copy in puts:
        copy.wait()
    put_act.wait()


def finish(q_wide, act, ig, down, gate, up, out, qkv):
    f32 = jnp.float32
    deep, hidden = gate.shape
    values = out.shape[1]
    shapes = [
        ig.shape,
        (q_wide, deep),
        (q_wide, deep),
        (deep, values),
        (values, deep),
        (hidden, deep),
        (hidden, deep),
        (hidden, deep),
    ]
    anywhere = pl.BlockSpec(memory_space=pl.ANY)
    given = (act, ig, down, gate, up, out, qkv)
    order = (0, 7, 5, 6, 4, 1, 2, 3)
    return pl.pallas_call(
        functools.partial(finish_kernel, q_wide),
        out_shape=[jax.ShapeDtypeStruct(act.shape, act.dtype)]
        + [jax.ShapeDtypeStruct(a, f32) for a in shapes],
        in_specs=[anywhere] * len(given),
        out_specs=[anywhere] * 9,
        scratch_shapes=[pltpu.VMEM(a.shape, a.dtype) for a in given]
        + [pltpu.VMEM(shapes[k], f32) for k in order]
        + [pltpu.SemaphoreType.DMA((16,)), pltpu.SemaphoreType.DMA((16,))],
        compiler_params=pltpu.CompilerParams(vmem_limit_bytes=56 * MIB),
    )(*given)


def on_device(
    stream_in,
    doc_lengths,
    first_gain,
    w_query,
    w_key,
    w_value,
    w_out,
    second_gain,
    w_gate,
    w_up,
    w_down,
    cotangent,
):
    n = lax.axis_size("seq")
    f32 = jnp.float32
    q_wide = w_query.shape[1]
    gains_own = jnp.concatenate([first_gain, second_gain]).astype(f32)
    gains_own = jnp.broadcast_to(gains_own[None], (16, gains_own.shape[0]))
    maps = feature_maps(q_wide)
    shards = (gains_own, w_query.T, w_key.T, w_value, w_out, w_gate.T, w_up.T, w_down)
    wholes, kept = forward(n, doc_lengths, stream_in, cotangent, maps, shards)
    *results, g_gains = backward(n, doc_lengths, maps, stream_in, cotangent, wholes, kept)
    activations, input_grad, query, key, value, out, gate, up, down = finish(q_wide, *results)
    return (
        activations,
        input_grad,
        jnp.sum(g_gains[:8], axis=0),
        query.T,
        key.T,
        value,
        out,
        jnp.sum(g_gains[8:], axis=0),
        gate.T,
        up.T,
        down,
    )


def solution(mesh):
    placed = (
        P("seq", None),
        P(),
        P("seq"),
        P("seq", "tp"),
        P("seq", "tp"),
        P("seq", "tp"),
        P("tp", "seq"),
        P("seq"),
        P("seq", "tp"),
        P("seq", "tp"),
        P("tp", "seq"),
        P("seq", None),
    )
    return jax.shard_map(
        on_device,
        mesh=mesh,
        in_specs=placed,
        out_specs=(
            P("seq", None),
            P("seq", None),
            P("seq"),
            P("seq", "tp"),
            P("seq", "tp"),
            P("seq", "tp"),
            P("tp", "seq"),
            P("seq"),
            P("seq", "tp"),
            P("seq", "tp"),
            P("tp", "seq"),
        ),
        check_vma=False,
    )
```
